32 devices in a mesh: real: 2 (over x), area: 16 (over z, y, core).
Axes of the slice: x: 2, y: 2, z: 4, core: 2. Of those that a mesh axis runs over, the one named last changes fastest.
Arguments:
- block_owner: int32 [128], replicated, may hold values from 0 to 127, as said below
- transfer_cells: int32 [16384], P('area'), may hold values from 0 to 131071, as said below
- transfer_nodes: int32 [16384], P('area'), may hold values from 0 to 32767, as said below
- transfer_weights: float32 [16384], P('area'), may hold values from 0.2 to 2
- row_counts: int32 [16], P('area'), may hold values from 204 to 1024, as said below
- matrix_start: float32 [16, 256, 1024], P('real', 'area'), parts along dimension 0, may hold values from -6 to 6
- matrix_source: float32 [16, 256, 1024], P('real', 'area'), parts along dimension 0, may hold values from -6 to 6
- matrix_storage: float32 [16, 256, 1024], P('real', 'area'), parts along dimension 0, may hold values from 0.5 to 8
- fracture_start: float32 [128, 512], P('area', 'real'), parts along dimension 1, may hold values from -6 to 6
- fracture_source: float32 [128, 512], P('area', 'real'), parts along dimension 1, may hold values from -6 to 6
- fracture_leak: float32 [128, 512], P('area', 'real'), parts along dimension 1, may hold values from 0.2 to 2
- fracture_links: int32 [4, 128, 256], P(None, 'area'), may hold values from 0 to 255
- link_weights: float32 [8, 128, 256], P('real', 'area'), parts along dimension 0, may hold values from 0.1 to 1
Outputs:
- matrix_pressure: float32 [16, 256, 1024], P('real', 'area'), parts along dimension 0
- fracture_pressure: float32 [128, 512], P('area', 'real'), parts along dimension 1
The draws below stay inside these ranges and needn't reach their ends.
There are 2 independent parts, one for each index of `real`. The reference program is written for one: setup_inputs(seed, part) draws one part's arguments, and reference() takes and returns one part's arrays. A program takes and returns all parts, laid end to end along the dimension named above; an argument that names none is the same for every part. Nothing has to cross between parts.
Inputs may be any that keep to these rules, and one draw needn't show every extreme that they name: `block_owner`: A permutation: the slot of each fracture block; slots 8 i to 8 (i + 1) - 1 lie on the i-th device of area. `transfer_cells`: rows that are not live hold values in the same range, to be ignored. `transfer_nodes`: of the live rows of one device, at most 96 name blocks whose slots lie on any one device; some device receives exactly 96 live rows from every device. The first row_counts[s] rows of device s are live; some device has all 1024 live.
All inputs are finite; a program needn't handle non-finite values.
Results may differ from the reference program's by a relative error of at most 0.0003.
Values sent between devices are 32-bit elements; how exact they have to be, the bound alone decides.
No kernel may reach another device: no remote copies, remote signals or barrier semaphores. Data moves between devices by JAX's collectives and lax.ppermute only.
A program may use at most 64 MiB of HBM per device.

```python
import math
import jax
import jax.numpy as jnp

DEPTH = 8
CX = 16
NY = 1024
NB_DEV = 8
ROWS_DEV = 1024
BLK = 256
K = 4
ITERS = 4
NX = 256
NB = 128
CAP = 96
CELLS_DEV = 131072
N_AREA = 16


def rows_layout(key):
    keys = jax.random.split(key, 9)
    owner_slot = jax.random.permutation(keys[0], NB).astype(jnp.int32)
    inverse = jnp.argsort(owner_slot).astype(jnp.int32)
    levels = jax.random.randint(keys[1], (N_AREA,), 1, 9)
    counts = jnp.maximum(ROWS_DEV // 5, ROWS_DEV * levels * levels // 64)
    full_device = jax.random.randint(keys[2], (), 0, N_AREA)
    counts = jnp.where(jnp.arange(N_AREA) == full_device, ROWS_DEV, counts).astype(jnp.int32)
    hot_owner = jax.random.randint(keys[3], (), 0, N_AREA)
    order_rows = jnp.arange(ROWS_DEV, dtype=jnp.int32)[None, :]
    live_rows = order_rows < counts[:, None]
    scores = jax.random.randint(keys[4], (N_AREA, ROWS_DEV), 0, 65536) * ROWS_DEV + order_rows
    scores = jnp.where(live_rows, scores, 2 ** 29 + order_rows)
    ranks = jnp.argsort(jnp.argsort(scores, axis=1), axis=1).astype(jnp.int32)
    offset = jax.random.randint(keys[5], (N_AREA, 1), 0, N_AREA - 1)
    others = (hot_owner + 1 + (ranks - CAP + offset) % (N_AREA - 1)) % N_AREA
    destination = jnp.where(ranks < CAP, hot_owner, others)
    local_slot = jax.random.randint(keys[6], (N_AREA, ROWS_DEV), 0, NB_DEV)
    node_within = jax.random.randint(keys[7], (N_AREA, ROWS_DEV), 0, BLK)
    blocks = inverse[destination * NB_DEV + local_slot]
    nodes = (blocks * BLK + node_within).astype(jnp.int32)
    cells = jax.random.randint(keys[8], (N_AREA, ROWS_DEV), 0, CELLS_DEV).astype(jnp.int32)
    return (owner_slot, cells.reshape(-1), nodes.reshape(-1), counts)


def draw_block_owner(key, part):
    shared = rows_layout(key)
    return shared[0]


def draw_transfer_cells(key, part):
    shared = rows_layout(key)
    return shared[1]


def draw_transfer_nodes(key, part):
    shared = rows_layout(key)
    return shared[2]


def draw_row_counts(key, part):
    shared = rows_layout(key)
    return shared[3]


def plant(array, own_key, low, largest):
    place = [jax.random.randint(jax.random.fold_in(own_key, axis), (), 0, length) for axis, length in enumerate(array.shape)]
    widest = array.shape.index(max(array.shape))
    beside = place[:widest] + [(place[widest] + 1) % array.shape[widest]] + place[widest + 1:]
    return array.at[tuple(place)].set(low).at[tuple(beside)].set(largest)


def block_scale(stream_key, extent, pieces, low, largest):
    loudness = 1.0
    for position, parts in pieces:
        draws = jax.random.uniform(jax.random.fold_in(jax.random.fold_in(stream_key, 6), position), (parts,), jnp.float32, low / len(pieces), largest / len(pieces))
        loudness = loudness * jnp.repeat(jnp.exp(draws), extent[position] // parts).reshape((-1,) + (1,) * (len(extent) - 1 - position))
    return loudness


def bell_draw(key, shape, deviation, most, pieces=(), kind=jnp.bfloat16):
    drawn = deviation * jax.random.normal(key, shape, jnp.float32)
    if pieces:
        drawn = drawn * block_scale(key, shape, pieces, -0.22, 0.18)
    return jnp.clip(drawn, -most, most).astype(kind)


def setup_inputs(seed: int = 0, part: int = 0) -> dict:
    splits = jax.random.split(jax.random.key(seed), 14)
    part_splits = jax.random.split(jax.random.fold_in(splits[13], part), 14)
    block_owner = draw_block_owner(jax.random.fold_in(splits[13], 71), part)
    transfer_cells = draw_transfer_cells(jax.random.fold_in(splits[13], 71), part)
    transfer_nodes = draw_transfer_nodes(jax.random.fold_in(splits[13], 71), part)
    transfer_weights = jnp.clip(jnp.exp(math.log(2.0) - 2.3025851 * jax.random.uniform(splits[3], (N_AREA * ROWS_DEV,), jnp.float32) ** block_scale(splits[3], (N_AREA * ROWS_DEV,), ((0, 16),), -0.2, 0.2)), 0.2, 2.0)
    row_counts = draw_row_counts(jax.random.fold_in(splits[13], 71), part)
    matrix_start = bell_draw(part_splits[5], (DEPTH, NX, NY), 1.0, 6.0, ((1, 16),), jnp.float32)
    matrix_source = bell_draw(part_splits[6], (DEPTH, NX, NY), 1.0, 6.0, ((1, 16),), jnp.float32)
    matrix_storage = jnp.clip(jnp.exp(math.log(8.0) - 2.7725887 * jax.random.uniform(part_splits[7], (DEPTH, NX, NY), jnp.float32) ** block_scale(part_splits[7], (DEPTH, NX, NY), ((1, 16),), -0.2, 0.2)), 0.5, 8.0)
    fracture_start = bell_draw(part_splits[8], (NB, BLK), 1.0, 6.0, ((0, 16),), jnp.float32)
    fracture_source = bell_draw(part_splits[9], (NB, BLK), 1.0, 6.0, ((0, 16),), jnp.float32)
    fracture_leak = jnp.clip(jnp.exp(math.log(2.0) - 2.3025851 * jax.random.uniform(part_splits[10], (NB, BLK), jnp.float32) ** block_scale(part_splits[10], (NB, BLK), ((0, 16),), -0.2, 0.2)), 0.2, 2.0)
    fracture_links = plant(jax.random.randint(splits[11], (K, NB, BLK), 0, BLK), jax.random.fold_in(splits[11], 1), 0, BLK - 1).astype(jnp.int32)
    link_weights = jnp.clip(jnp.exp(math.log(1.0) - 2.3025851 * jax.random.uniform(part_splits[12], (K, NB, BLK), jnp.float32) ** block_scale(part_splits[12], (K, NB, BLK), ((1, 16),), -0.2, 0.2)), 0.1, 1.0)
    return dict(block_owner=block_owner, transfer_cells=transfer_cells, transfer_nodes=transfer_nodes, transfer_weights=transfer_weights, row_counts=row_counts, matrix_start=matrix_start, matrix_source=matrix_source, matrix_storage=matrix_storage, fracture_start=fracture_start, fracture_source=fracture_source, fracture_leak=fracture_leak, fracture_links=fracture_links, link_weights=link_weights)


def relax_weights(steps_total):
    return [1.0 / (1.0 + 0.75 * math.cos(math.pi * (2 * index + 1) / (2 * steps_total))) for index in range(steps_total)]


def neighbours(values):
    padded = jnp.pad(values, 1)
    beside = padded[2:, 1:-1, 1:-1] + padded[:-2, 1:-1, 1:-1]
    beside = beside + padded[1:-1, 2:, 1:-1] + padded[1:-1, :-2, 1:-1]
    beside = beside + padded[1:-1, 1:-1, 2:] + padded[1:-1, 1:-1, :-2]
    return beside


def to_rows(values):
    return values.reshape(DEPTH, N_AREA, CX, NY).transpose(1, 0, 2, 3).reshape(-1)


def to_grid(values):
    return values.reshape(N_AREA, DEPTH, CX, NY).transpose(1, 0, 2, 3).reshape(DEPTH, NX, NY)


def reference(block_owner, transfer_cells, transfer_nodes, transfer_weights, row_counts, matrix_start, matrix_source, matrix_storage, fracture_start, fracture_source, fracture_leak, fracture_links, link_weights):
    row_index = jnp.arange(N_AREA * ROWS_DEV, dtype=jnp.int32)
    device = row_index // ROWS_DEV
    live_rows = (row_index % ROWS_DEV) < row_counts[device]
    weight = jnp.where(live_rows, transfer_weights, jnp.zeros_like(transfer_weights))
    cell_index = (device * CELLS_DEV + transfer_cells).astype(jnp.int32)
    node_index = (block_owner[transfer_nodes // BLK] * BLK + transfer_nodes % BLK).astype(jnp.int32)
    matrix_weight = to_grid(jnp.zeros((N_AREA * CELLS_DEV,), jnp.float32).at[cell_index].add(weight))
    fracture_weight = jnp.zeros((NB * BLK,), jnp.float32).at[node_index].add(weight).reshape(NB, BLK)
    matrix_diag = 6.0 + matrix_storage + matrix_weight
    fracture_diag = fracture_leak + jnp.sum(link_weights, axis=0) + fracture_weight
    matrix_now = matrix_start
    fracture_now = fracture_start
    for relaxation in relax_weights(ITERS):
        matrix_rows = to_rows(matrix_now)
        fracture_flat = fracture_now.reshape(-1)
        into_matrix = to_grid(jnp.zeros((N_AREA * CELLS_DEV,), jnp.float32).at[cell_index].add(weight * fracture_flat[node_index]))
        into_fracture = jnp.zeros((NB * BLK,), jnp.float32).at[node_index].add(weight * matrix_rows[cell_index]).reshape(NB, BLK)
        linked = jnp.take_along_axis(jnp.broadcast_to(fracture_now[None], link_weights.shape), fracture_links, axis=2)
        link_sum = jnp.sum(link_weights * linked, axis=0)
        matrix_next = matrix_now + relaxation * (matrix_source - matrix_diag * matrix_now + neighbours(matrix_now) + into_matrix) / matrix_diag
        fracture_next = fracture_now + relaxation * (fracture_source - fracture_diag * fracture_now + link_sum + into_fracture) / fracture_diag
        matrix_now = matrix_next
        fracture_now = fracture_next
    return matrix_now, fracture_now
```

```python
import functools
import math

import jax
import jax.numpy as jnp
from jax import lax
from jax.experimental import pallas as pl
from jax.experimental.pallas import tpu as pltpu
from jax.sharding import PartitionSpec as P

ITERS = 4
LANES = 128
F32 = jnp.float32
BF16 = jnp.bfloat16
VMEM_LIMIT = 32 * 1024 * 1024


def relax_weights(steps_total):
    return [
        1.0 / (1.0 + 0.75 * math.cos(math.pi * (2 * index + 1) / (2 * steps_total)))
        for index in range(steps_total)
    ]


def log2(value):
    assert value & (value - 1) == 0
    return value.bit_length() - 1


def iota(shape, dim):
    return lax.broadcasted_iota(jnp.int32, shape, dim)


def halves(x):
    high = x.astype(BF16)
    low = (x - high.astype(F32)).astype(BF16)
    return high, low


def matmul(a, b, contract):
    return lax.dot_general(a, b, ((contract[:1], contract[1:]), ((), ())), preferred_element_type=F32)


def to_dense(x, cap):
    return jnp.concatenate([x[i : i + 1, :cap] for i in range(x.shape[0])], axis=1)


def from_dense(x, devices, cap):
    rows = jnp.concatenate([x[:, i * cap : (i + 1) * cap] for i in range(devices)], axis=0)
    return jnp.concatenate([rows, jnp.zeros((devices, LANES - cap), x.dtype)], axis=1)


def lane_gather(table, index):
    return jnp.take_along_axis(table, index, axis=1, mode="promise_in_bounds")


def masked_parts(low, *values):
    mask = iota((LANES, low.shape[1]), 0) == low
    zero = jnp.zeros((), F32)
    parts = []
    for value in values:
        high = value.astype(BF16).astype(F32)
        parts.append(jnp.where(mask, high, zero).astype(BF16))
        parts.append(jnp.where(mask, value - high, zero).astype(BF16))
    return jnp.concatenate(parts, axis=0)


def fold(wide, index):
    start = 2 * index * LANES
    return wide[:, start : start + LANES] + wide[:, start + LANES : start + 2 * LANES]


def pick_low(tall, low):
    both = tall[:LANES] + tall[LANES:]
    return jnp.sum(
        jnp.where(iota(both.shape, 0) == low, both, 0.0), axis=0, keepdims=True
    )


def stack_lanes(x):
    return jnp.concatenate(
        [x[:, i * LANES : (i + 1) * LANES] for i in range(x.shape[1] // LANES)], axis=0
    )


def unstack_lanes(x, rows):
    return jnp.concatenate([x[i : i + rows] for i in range(0, x.shape[0], rows)], axis=1)


def put_columns(chunk, index, columns_ref):
    high, low = halves(chunk.T)
    columns_ref[:LANES, index * LANES : (index + 1) * LANES] = high
    columns_ref[LANES:, index * LANES : (index + 1) * LANES] = low


def setup_kernel(
    devices,
    cap,
    owned,
    blk,
    cols,
    counts_ref,
    owner_ref,
    cells_ref,
    nodes_ref,
    weights_ref,
    matrix_ref,
    fracture_ref,
    hot_ref,
    slot_index_ref,
    slot_weight_ref,
    slot_code_ref,
    message_ref,
    top_ref,
    bottom_ref,
    columns_ref,
):
    groups = cells_ref.shape[0]
    slots = devices * cap
    plane_rows = matrix_ref.shape[0] * matrix_ref.shape[1]
    col_groups = cols // LANES
    shape = (groups, LANES)
    nodes, cells = nodes_ref[...], cells_ref[...]
    live = iota(shape, 0) * LANES + iota(shape, 1) < counts_ref[0]
    weight = jnp.where(live, weights_ref[...], 0.0)
    block = nodes >> log2(blk)
    slot = jnp.zeros(shape, jnp.int32)
    for part in range(owner_ref.shape[0]):
        table = jnp.broadcast_to(owner_ref[part : part + 1, :], shape)
        found = lane_gather(table, block & (LANES - 1))
        slot = jnp.where(block >> log2(LANES) == part, found, slot)
    target = jnp.where(live, slot >> log2(owned), -1)
    node_high = ((nodes & (blk - 1)) >> log2(LANES)) * owned + (slot & (owned - 1))
    node_low = nodes & (LANES - 1)
    cell_plane = cells >> log2(cols)
    cell_group = (cells & (cols - 1)) >> log2(LANES)
    cell_low = cells & (LANES - 1)

    device_rows = iota((devices, LANES), 0)
    member = [(device_rows == target[q : q + 1]).astype(F32) for q in range(groups)]
    earlier = (iota((LANES, LANES), 0) < iota((LANES, LANES), 1)).astype(BF16)
    counted = matmul(jnp.concatenate(member, axis=0).astype(BF16), earlier, (1, 0))
    before = jnp.zeros((devices, 1), F32)
    placed = []
    for q in range(groups):
        rank = jnp.sum(
            member[q] * (counted[q * devices : (q + 1) * devices] + before), axis=0, keepdims=True
        ).astype(jnp.int32)
        before = before + jnp.sum(member[q], axis=1, keepdims=True)
        where = target[q : q + 1]
        placed.append(jnp.where(where >= 0, where * cap + rank, -1))
    placed = jnp.concatenate(placed, axis=1)

    high = weight.astype(BF16).astype(F32)
    middle = (weight - high).astype(BF16).astype(F32)
    low = weight - high - middle
    features = [
        jnp.where(live, 1.0, 0.0),
        node_high.astype(F32),
        node_low.astype(F32),
        cell_plane.astype(F32),
        cell_group.astype(F32),
        cell_low.astype(F32),
        high,
        middle,
        low,
    ]
    features = [jnp.concatenate([x[q : q + 1] for q in range(groups)], axis=1) for x in features]
    features = jnp.concatenate(
        features + [jnp.zeros((16 - len(features), groups * LANES), F32)], axis=0
    ).astype(BF16)
    placing = (iota((slots, groups * LANES), 0) == placed).astype(F32).astype(BF16)
    packed = matmul(features, placing, (1, 1))
    used = packed[0:1] > 0.5
    code = packed[1:2] * LANES + packed[2:3]
    code = jnp.where(used, code, -1.0)
    slot_high = jnp.where(used, packed[4:5] * plane_rows + packed[3:4], -1.0).astype(jnp.int32)
    slot_low = packed[5:6].astype(jnp.int32)
    slot_weight = packed[6:7] + packed[7:8] + packed[8:9]
    hot = (iota((col_groups * plane_rows, slots), 0) == slot_high).astype(F32).astype(BF16)
    hot_ref[...] = hot
    slot_index_ref[...] = slot_low
    slot_weight_ref[...] = slot_weight

    for c in range(col_groups):
        chunk = matrix_ref[:, :, c * LANES : (c + 1) * LANES].reshape(plane_rows, LANES)
        put_columns(chunk, c, columns_ref)
    picked = pick_low(matmul(columns_ref[...], hot, (1, 0)), slot_low)
    code = from_dense(code, devices, cap)
    slot_code_ref[...] = code.astype(jnp.int32)
    message_ref[:, 0, :] = jnp.where(iota((devices, LANES), 1) < cap, code, -1.0)
    message_ref[:, 1, :] = from_dense(slot_weight, devices, cap)
    message_ref[:, 2, :] = from_dense(slot_weight * picked, devices, cap)
    message_ref[:, 3, :] = jnp.zeros((devices, LANES), F32)
    table = stack_lanes(fracture_ref[...])
    message_ref[:, 4:, :] = jnp.broadcast_to(table[None], (devices,) + table.shape)
    top_ref[...] = matrix_ref[:, 0, :]
    bottom_ref[...] = matrix_ref[:, matrix_ref.shape[1] - 1, :]


def relaxed(now, source, inverse, low_side, high_side, relaxation):
    depth, rows, cols = now.shape
    zero_plane = jnp.zeros((1, rows, cols), F32)
    beside = jnp.concatenate([now[1:], zero_plane], axis=0)
    beside = beside + jnp.concatenate([zero_plane, now[:-1]], axis=0)
    beside = beside + jnp.concatenate([now[:, 1:], high_side[:, None]], axis=1)
    beside = beside + jnp.concatenate([low_side[:, None], now[:, :-1]], axis=1)
    flat = now.reshape(depth * rows, cols)
    place = iota(flat.shape, 1)
    left = jnp.where(place == 0, 0.0, pltpu.roll(flat, 1, 1))
    right = jnp.where(place == cols - 1, 0.0, pltpu.roll(flat, cols - 1, 1))
    beside = beside + (left + right).reshape(now.shape)
    return (1.0 - relaxation) * now + (relaxation * inverse) * (source + beside)


def linked(fracture, links_ref, link_weights_ref):
    total = jnp.zeros(fracture.shape, F32)
    width = fracture.shape[1]
    tables = [fracture[:, i : i + LANES] for i in range(0, width, LANES)]
    sums = []
    for start in range(0, width, LANES):
        total = jnp.zeros(tables[0].shape, F32)
        for j in range(links_ref.shape[0]):
            link = links_ref[j, :, start : start + LANES]
            found = jnp.zeros(tables[0].shape, F32)
            for i, table in enumerate(tables):
                found = jnp.where(
                    link >> log2(LANES) == i, lane_gather(table, link & (LANES - 1)), found
                )
            total = total + link_weights_ref[j, :, start : start + LANES] * found
        sums.append(total)
    return jnp.concatenate(sums, axis=1)


def first_window_kernel(
    relaxation,
    matrix_ref,
    low_side_ref,
    high_side_ref,
    source_ref,
    storage_ref,
    hot_ref,
    slot_index_ref,
    slot_weight_ref,
    fracture_ref,
    links_ref,
    link_weights_ref,
    partial_ref,
    inverse_ref,
    link_sum_ref,
):
    plane_rows = matrix_ref.shape[0] * matrix_ref.shape[1]
    parts = masked_parts(slot_index_ref[...], slot_weight_ref[...])
    added = fold(matmul(hot_ref[...], parts, (1, 1)), 0)
    for c in range(matrix_ref.shape[2] // LANES):
        lanes = slice(c * LANES, (c + 1) * LANES)
        extra = added[c * plane_rows : (c + 1) * plane_rows].reshape(matrix_ref.shape[:2] + (LANES,))
        inverse_ref[:, :, lanes] = 1.0 / (6.0 + storage_ref[:, :, lanes] + extra)
    partial_ref[...] = relaxed(
        matrix_ref[...],
        source_ref[...],
        inverse_ref[...],
        low_side_ref[...],
        high_side_ref[...],
        relaxation,
    )
    link_sum_ref[...] = linked(fracture_ref[...], links_ref, link_weights_ref)


def window_kernel(
    relaxation,
    matrix_ref,
    low_side_ref,
    high_side_ref,
    source_ref,
    inverse_ref,
    fracture_ref,
    links_ref,
    link_weights_ref,
    partial_ref,
    link_sum_ref,
):
    partial_ref[...] = relaxed(
        matrix_ref[...],
        source_ref[...],
        inverse_ref[...],
        low_side_ref[...],
        high_side_ref[...],
        relaxation,
    )
    link_sum_ref[...] = linked(fracture_ref[...], links_ref, link_weights_ref)


def couple(
    relaxation,
    cap,
    returned,
    partial_ref,
    inverse_ref,
    hot_ref,
    slot_index_ref,
    slot_weight_ref,
    matrix_ref,
    columns_ref,
):
    plane_rows = partial_ref.shape[0] * partial_ref.shape[1]
    low = slot_index_ref[...]
    weight = slot_weight_ref[...]
    parts = masked_parts(low, weight * to_dense(returned, cap))
    added = fold(matmul(hot_ref[...], parts, (1, 1)), 0)
    for c in range(partial_ref.shape[2] // LANES):
        lanes = slice(c * LANES, (c + 1) * LANES)
        extra = added[c * plane_rows : (c + 1) * plane_rows].reshape(
            partial_ref.shape[:2] + (LANES,)
        )
        chunk = partial_ref[:, :, lanes] + (relaxation * inverse_ref[:, :, lanes]) * extra
        matrix_ref[:, :, lanes] = chunk
        if columns_ref is not None:
            put_columns(chunk.reshape(plane_rows, LANES), c, columns_ref)
    if columns_ref is None:
        return None
    return weight * pick_low(matmul(columns_ref[...], hot_ref[...], (1, 0)), low)


def node_hot(code, rows):
    return (iota((rows, code.shape[1]), 0) == code >> log2(LANES)).astype(F32).astype(BF16)


def node_values(table, code):
    found = jnp.zeros(code.shape, F32)
    low = code & (LANES - 1)
    for row in range(table.shape[0]):
        values = jnp.broadcast_to(table[row : row + 1], code.shape)
        found = jnp.where(code >> log2(LANES) == row, lane_gather(values, low), found)
    return found


def first_step_kernel(
    relaxation,
    cap,
    arrived_ref,
    slot_code_ref,
    partial_ref,
    inverse_ref,
    hot_ref,
    slot_index_ref,
    slot_weight_ref,
    fracture_ref,
    link_sum_ref,
    fracture_source_ref,
    leak_ref,
    link_weights_ref,
    matrix_ref,
    fracture_next_ref,
    fracture_inverse_ref,
    node_code_ref,
    message_ref,
    top_ref,
    bottom_ref,
    columns_ref,
):
    devices = arrived_ref.shape[0]
    owned = fracture_ref.shape[0]
    slot_code = slot_code_ref[...]
    low = slot_code & (LANES - 1)
    returned = jnp.zeros(slot_code.shape, F32)
    table_rows = arrived_ref.shape[1] - 4
    for row in range(table_rows):
        found = lane_gather(arrived_ref[:, 4 + row, :], low)
        returned = jnp.where(slot_code >> log2(LANES) == row, found, returned)
    outgoing = couple(
        relaxation,
        cap,
        returned,
        partial_ref,
        inverse_ref,
        hot_ref,
        slot_index_ref,
        slot_weight_ref,
        matrix_ref,
        columns_ref,
    )
    code = arrived_ref[:, 0, :].astype(jnp.int32)
    node_code_ref[...] = code
    dense = to_dense(code, cap)
    parts = masked_parts(
        dense & (LANES - 1),
        to_dense(arrived_ref[:, 1, :], cap),
        to_dense(arrived_ref[:, 2, :], cap),
    )
    sums = matmul(node_hot(dense, table_rows), parts, (1, 1))
    diag = (
        leak_ref[...] + jnp.sum(link_weights_ref[...], axis=0) + unstack_lanes(fold(sums, 0), owned)
    )
    inverse = 1.0 / diag
    fracture_inverse_ref[...] = inverse
    fracture_next = (1.0 - relaxation) * fracture_ref[...] + (relaxation * inverse) * (
        fracture_source_ref[...] + link_sum_ref[...] + unstack_lanes(fold(sums, 1), owned)
    )
    fracture_next_ref[...] = fracture_next
    message_ref[:, 0, :] = from_dense(outgoing, devices, cap)
    message_ref[:, 1, :] = node_values(stack_lanes(fracture_next), code)
    top_ref[...] = matrix_ref[:, 0, :]
    bottom_ref[...] = matrix_ref[:, matrix_ref.shape[1] - 1, :]


def step_kernel(
    relaxation,
    cap,
    last,
    arrived_ref,
    node_code_ref,
    partial_ref,
    inverse_ref,
    hot_ref,
    slot_index_ref,
    slot_weight_ref,
    fracture_ref,
    link_sum_ref,
    fracture_source_ref,
    fracture_inverse_ref,
    matrix_ref,
    fracture_next_ref,
    message_ref=None,
    top_ref=None,
    bottom_ref=None,
    columns_ref=None,
):
    devices = arrived_ref.shape[0]
    owned, blk = fracture_ref.shape
    outgoing = couple(
        relaxation,
        cap,
        arrived_ref[:, 1, :],
        partial_ref,
        inverse_ref,
        hot_ref,
        slot_index_ref,
        slot_weight_ref,
        matrix_ref,
        columns_ref,
    )
    code = node_code_ref[...]
    dense = to_dense(code, cap)
    parts = masked_parts(dense & (LANES - 1), to_dense(arrived_ref[:, 0, :], cap))
    sums = matmul(node_hot(dense, owned * blk // LANES), parts, (1, 1))
    fracture_next = (1.0 - relaxation) * fracture_ref[...] + (
        relaxation * fracture_inverse_ref[...]
    ) * (fracture_source_ref[...] + link_sum_ref[...] + unstack_lanes(fold(sums, 0), owned))
    fracture_next_ref[...] = fracture_next
    if last:
        return
    message_ref[:, 0, :] = from_dense(outgoing, devices, cap)
    message_ref[:, 1, :] = node_values(stack_lanes(fracture_next), code)
    top_ref[...] = matrix_ref[:, 0, :]
    bottom_ref[...] = matrix_ref[:, matrix_ref.shape[1] - 1, :]


def call(kernel, outs, ins, name, micros, smem=(), scratch=()):
    bytes_accessed = int(micros * 3.0e6)
    return pl.pallas_call(
        kernel,
        out_shape=[jax.ShapeDtypeStruct(shape, dtype) for shape, dtype in outs],
        in_specs=[
            pl.BlockSpec(memory_space=pltpu.SMEM if i in smem else pltpu.VMEM)
            for i in range(len(ins))
        ],
        out_specs=[pl.BlockSpec(memory_space=pltpu.VMEM) for _ in outs],
        scratch_shapes=list(scratch),
        compiler_params=pltpu.CompilerParams(vmem_limit_bytes=VMEM_LIMIT),
        cost_estimate=pl.CostEstimate(flops=0, bytes_accessed=bytes_accessed, transcendentals=0),
        name=name,
    )(*ins)


def local(
    block_owner,
    transfer_cells,
    transfer_nodes,
    transfer_weights,
    row_counts,
    matrix_start,
    matrix_source,
    matrix_storage,
    fracture_start,
    fracture_source,
    fracture_leak,
    fracture_links,
    link_weights,
):
    devices = lax.axis_size("area")
    depth, area_rows, cols = matrix_start.shape
    owned, blk = fracture_start.shape
    total_rows = transfer_cells.shape[0]
    cap = 3 * total_rows // (2 * devices)
    slots = devices * cap
    cells = depth * area_rows * cols // LANES
    table_rows = owned * blk // LANES
    relax = relax_weights(ITERS)
    grid = (matrix_start.shape, F32)
    fracture = (fracture_start.shape, F32)
    side = ((depth, cols), F32)
    columns = pltpu.VMEM((2 * LANES, cells), BF16)
    padded = (devices, LANES)
    forward = [(i, i + 1) for i in range(devices - 1)]
    backward = [(target, source) for source, target in forward]

    def exchange(message):
        return lax.all_to_all(message, "area", split_axis=0, concat_axis=0, tiled=True)

    def sides(top, bottom):
        return lax.ppermute(bottom, "area", forward), lax.ppermute(top, "area", backward)

    hot, slot_index, slot_weight, slot_code, message, top, bottom = call(
        functools.partial(setup_kernel, devices, cap, owned, blk, cols),
        [
            ((cells, slots), BF16),
            ((1, slots), jnp.int32),
            ((1, slots), F32),
            (padded, jnp.int32),
            ((devices, 4 + table_rows, LANES), F32),
            side,
            side,
        ],
        [
            row_counts,
            block_owner.reshape(-1, LANES),
            transfer_cells.reshape(-1, LANES),
            transfer_nodes.reshape(-1, LANES),
            transfer_weights.reshape(-1, LANES),
            matrix_start,
            fracture_start,
        ],
        "place_rows",
        5.0,
        smem=(0,),
        scratch=[columns],
    )
    arrived = exchange(message)
    low_side, high_side = sides(top, bottom)
    partial, inverse, link_sum = call(
        functools.partial(first_window_kernel, relax[0]),
        [grid, grid, fracture],
        [
            matrix_start,
            low_side,
            high_side,
            matrix_source,
            matrix_storage,
            hot,
            slot_index,
            slot_weight,
            fracture_start,
            fracture_links,
            link_weights,
        ],
        "stencil_first",
        4.0,
    )
    matrix, fracture_now, fracture_inverse, node_code, message, top, bottom = call(
        functools.partial(first_step_kernel, relax[0], cap),
        [grid, fracture, fracture, (padded, jnp.int32), ((devices, 2, LANES), F32), side, side],
        [
            arrived,
            slot_code,
            partial,
            inverse,
            hot,
            slot_index,
            slot_weight,
            fracture_start,
            link_sum,
            fracture_source,
            fracture_leak,
            link_weights,
        ],
        "couple_first",
        4.0,
        scratch=[columns],
    )
    for index in range(1, ITERS):
        last = index == ITERS - 1
        arrived = exchange(message)
        low_side, high_side = sides(top, bottom)
        partial, link_sum = call(
            functools.partial(window_kernel, relax[index]),
            [grid, fracture],
            [
                matrix,
                low_side,
                high_side,
                matrix_source,
                inverse,
                fracture_now,
                fracture_links,
                link_weights,
            ],
            "stencil",
            3.0,
        )
        outs = call(
            functools.partial(step_kernel, relax[index], cap, last),
            [grid, fracture] + ([] if last else [((devices, 2, LANES), F32), side, side]),
            [
                arrived,
                node_code,
                partial,
                inverse,
                hot,
                slot_index,
                slot_weight,
                fracture_now,
                link_sum,
                fracture_source,
                fracture_inverse,
            ],
            "couple",
            3.0,
            scratch=[] if last else [columns],
        )
        matrix, fracture_now = outs[:2]
        if not last:
            message, top, bottom = outs[2:]
    return (matrix, fracture_now)


def solution(mesh):
    in_specs = (
        P(),
        P("area"),
        P("area"),
        P("area"),
        P("area"),
        P("real", "area", None),
        P("real", "area", None),
        P("real", "area", None),
        P("area", "real"),
        P("area", "real"),
        P("area", "real"),
        P(None, "area", None),
        P("real", "area", None),
    )
    out_specs = (P("real", "area", None), P("area", "real"))
    return jax.shard_map(local, mesh=mesh, in_specs=in_specs, out_specs=out_specs, check_vma=False)
```

```python
import functools
import math

import jax
import jax.numpy as jnp
from jax import lax
from jax.experimental import pallas as pl
from jax.experimental.pallas import tpu as pltpu
from jax.sharding import PartitionSpec as P

ITERS = 4
HALO = ITERS - 1
LANES = 128
F32 = jnp.float32
BF16 = jnp.bfloat16
VMEM_LIMIT = 32 * 1024 * 1024


def relax_weights(steps_total):
    return [
        1.0 / (1.0 + 0.75 * math.cos(math.pi * (2 * index + 1) / (2 * steps_total)))
        for index in range(steps_total)
    ]


def log2(value):
    assert value & (value - 1) == 0
    return value.bit_length() - 1


def iota(shape, dim):
    return lax.broadcasted_iota(jnp.int32, shape, dim)


def halves(x):
    high = x.astype(BF16)
    low = (x - high.astype(F32)).astype(BF16)
    return high, low


def matmul(a, b, contract):
    return lax.dot_general(a, b, ((contract[:1], contract[1:]), ((), ())), preferred_element_type=F32)


def to_dense(x, cap):
    return jnp.concatenate([x[i : i + 1, :cap] for i in range(x.shape[0])], axis=1)


def from_dense(x, devices, cap):
    rows = jnp.concatenate([x[:, i * cap : (i + 1) * cap] for i in range(devices)], axis=0)
    return jnp.concatenate([rows, jnp.zeros((devices, LANES - cap), x.dtype)], axis=1)


def lane_gather(table, index):
    return jnp.take_along_axis(table, index, axis=1, mode="promise_in_bounds")


def masked_parts(low, *values):
    mask = iota((LANES, low.shape[1]), 0) == low
    zero = jnp.zeros((), F32)
    parts = []
    for value in values:
        high = value.astype(BF16).astype(F32)
        parts.append(jnp.where(mask, high, zero).astype(BF16))
        parts.append(jnp.where(mask, value - high, zero).astype(BF16))
    return jnp.concatenate(parts, axis=0)


def fold(wide, index):
    start = 2 * index * LANES
    return wide[:, start : start + LANES] + wide[:, start + LANES : start + 2 * LANES]


def pick_low(tall, low):
    both = tall[:LANES] + tall[LANES:]
    return jnp.sum(
        jnp.where(iota(both.shape, 0) == low, both, 0.0), axis=0, keepdims=True
    )


def stack_lanes(x):
    return jnp.concatenate(
        [x[:, i * LANES : (i + 1) * LANES] for i in range(x.shape[1] // LANES)], axis=0
    )


def unstack_lanes(x, rows):
    return jnp.concatenate([x[i : i + rows] for i in range(0, x.shape[0], rows)], axis=1)


def put_columns(chunk, index, columns_ref):
    high, low = halves(chunk.T)
    columns_ref[:LANES, index * LANES : (index + 1) * LANES] = high
    columns_ref[LANES:, index * LANES : (index + 1) * LANES] = low


def fill_hot(hot_ref, slot_high):
    for start in range(0, hot_ref.shape[0], LANES):
        rows = iota((LANES, slot_high.shape[1]), 0) + start
        hot_ref[start : start + LANES, :] = (rows == slot_high).astype(F32).astype(BF16)


def setup_kernel(devices, cap, staged, *refs):
    sources, refs = refs[:staged], refs[staged:]
    slot_index_ref, slot_weight_ref, slot_code_ref, message_hbm, up_hbm, down_hbm = refs[:6]
    targets, refs = refs[6 : 6 + staged], refs[6 + staged :]
    message_ref, up_ref, down_ref, hot_ref, columns_ref, sems = refs
    copies = [
        pltpu.make_async_copy(sources[i], targets[i], sems.at[i]) for i in range(staged)
    ]
    for copy in copies:
        copy.start()
    for copy in copies[:5]:
        copy.wait()
    counts_ref, owner_ref, cells_ref, nodes_ref, weights_ref = targets[:5]
    matrix_ref, fracture_ref, source_ref, storage_ref = targets[5:]
    owned, blk = fracture_ref.shape
    depth, area_rows, cols = matrix_ref.shape
    groups = cells_ref.shape[0]
    slots = devices * cap
    plane_rows = matrix_ref.shape[0] * matrix_ref.shape[1]
    col_groups = cols // LANES
    shape = (groups, LANES)
    nodes, cells = nodes_ref[...], cells_ref[...]
    live = iota(shape, 0) * LANES + iota(shape, 1) < counts_ref[...]
    weight = jnp.where(live, weights_ref[...], 0.0)
    block = nodes >> log2(blk)
    slot = jnp.zeros(shape, jnp.int32)
    for part in range(owner_ref.shape[0]):
        table = jnp.broadcast_to(owner_ref[part : part + 1, :], shape)
        found = lane_gather(table, block & (LANES - 1))
        slot = jnp.where(block >> log2(LANES) == part, found, slot)
    target = jnp.where(live, slot >> log2(owned), -1)
    node_high = ((nodes & (blk - 1)) >> log2(LANES)) * owned + (slot & (owned - 1))
    node_low = nodes & (LANES - 1)
    cell_plane = cells >> log2(cols)
    cell_group = (cells & (cols - 1)) >> log2(LANES)
    cell_low = cells & (LANES - 1)

    device_rows = iota((devices, LANES), 0)
    member = [(device_rows == target[q : q + 1]).astype(F32) for q in range(groups)]
    earlier = (iota((LANES, LANES), 0) < iota((LANES, LANES), 1)).astype(BF16)
    counted = matmul(jnp.concatenate(member, axis=0).astype(BF16), earlier, (1, 0))
    before = jnp.zeros((devices, 1), F32)
    placed = []
    for q in range(groups):
        rank = jnp.sum(
            member[q] * (counted[q * devices : (q + 1) * devices] + before), axis=0, keepdims=True
        ).astype(jnp.int32)
        before = before + jnp.sum(member[q], axis=1, keepdims=True)
        where = target[q : q + 1]
        placed.append(jnp.where(where >= 0, where * cap + rank, -1))
    placed = jnp.concatenate(placed, axis=1)

    high = weight.astype(BF16).astype(F32)
    middle = (weight - high).astype(BF16).astype(F32)
    low = weight - high - middle
    features = [
        jnp.where(live, 1.0, 0.0),
        node_high.astype(F32),
        node_low.astype(F32),
        cell_plane.astype(F32),
        cell_group.astype(F32),
        cell_low.astype(F32),
        high,
        middle,
        low,
    ]
    features = [jnp.concatenate([x[q : q + 1] for q in range(groups)], axis=1) for x in features]
    features = jnp.concatenate(
        features + [jnp.zeros((16 - len(features), groups * LANES), F32)], axis=0
    ).astype(BF16)
    placing = (iota((slots, groups * LANES), 0) == placed).astype(F32).astype(BF16)
    packed = matmul(features, placing, (1, 1))
    used = packed[0:1] > 0.5
    code = packed[1:2] * LANES + packed[2:3]
    code = jnp.where(used, code, -1.0)
    slot_high = jnp.where(used, packed[4:5] * plane_rows + packed[3:4], -1.0).astype(jnp.int32)
    slot_low = packed[5:6].astype(jnp.int32)
    slot_weight = packed[6:7] + packed[7:8] + packed[8:9]
    fill_hot(hot_ref, slot_high)
    slot_index_ref[0:1] = slot_high
    slot_index_ref[1:2] = slot_low
    slot_weight_ref[...] = slot_weight
    padded_code = from_dense(code, devices, cap)
    slot_code_ref[...] = padded_code.astype(jnp.int32)
    message_ref[:, 0, :] = jnp.where(iota((devices, LANES), 1) < cap, padded_code, -1.0)
    message_ref[:, 1, :] = from_dense(slot_weight, devices, cap)
    message_ref[:, 3, :] = jnp.zeros((devices, LANES), F32)

    row = slot_high & (area_rows - 1)
    plane = (slot_high >> log2(area_rows)) & (depth - 1)
    group = slot_high >> log2(plane_rows)
    for far, side_ref in ((area_rows - 1 - row, up_ref), (row, down_ref)):
        place = (group * HALO + far) * depth + plane
        place = jnp.where(used & (far < HALO), place, -1).astype(F32)
        half = slots // 2
        for i, x in enumerate((place, packed[5:6], slot_weight, code)):
            side_ref[3 * HALO + 1, 2 * i : 2 * i + 1, :half] = x[:, :half]
            side_ref[3 * HALO + 1, 2 * i + 1 : 2 * i + 2, :half] = x[:, half:]

    for copy in copies[5:]:
        copy.wait()
    table = stack_lanes(fracture_ref[...])
    message_ref[:, 4:, :] = jnp.broadcast_to(table[None], (devices,) + table.shape)
    for c in range(col_groups):
        chunk = matrix_ref[:, :, c * LANES : (c + 1) * LANES].reshape(plane_rows, LANES)
        put_columns(chunk, c, columns_ref)
    for far in range(HALO + 1):
        up_ref[far] = matrix_ref[:, area_rows - 1 - far, :]
        down_ref[far] = matrix_ref[:, far, :]
    for start, ref in ((HALO + 1, source_ref), (2 * HALO + 1, storage_ref)):
        for far in range(HALO):
            up_ref[start + far] = ref[:, area_rows - 1 - far, :]
            down_ref[start + far] = ref[:, far, :]
    outs = [
        pltpu.make_async_copy(up_ref, up_hbm, sems.at[staged]),
        pltpu.make_async_copy(down_ref, down_hbm, sems.at[staged + 1]),
        pltpu.make_async_copy(message_ref, message_hbm, sems.at[staged + 2]),
    ]
    outs[0].start()
    outs[1].start()
    picked = pick_low(matmul(columns_ref[...], hot_ref[...], (1, 0)), slot_low)
    message_ref[:, 2, :] = from_dense(slot_weight * picked, devices, cap)
    outs[2].start()
    for out in outs:
        out.wait()


def relaxed(now, source, inverse, low_side, high_side, relaxation):
    depth, rows, cols = now.shape
    zero_plane = jnp.zeros((1, rows, cols), F32)
    beside = jnp.concatenate([now[1:], zero_plane], axis=0)
    beside = beside + jnp.concatenate([zero_plane, now[:-1]], axis=0)
    beside = beside + jnp.concatenate([now[:, 1:], high_side[:, None]], axis=1)
    beside = beside + jnp.concatenate([low_side[:, None], now[:, :-1]], axis=1)
    flat = now.reshape(depth * rows, cols)
    place = iota(flat.shape, 1)
    left = jnp.where(place == 0, 0.0, pltpu.roll(flat, 1, 1))
    right = jnp.where(place == cols - 1, 0.0, pltpu.roll(flat, cols - 1, 1))
    beside = beside + (left + right).reshape(now.shape)
    return (1.0 - relaxation) * now + relaxation * (source + inverse * beside)


def linked(fracture, links_ref, link_weights_ref):
    total = jnp.zeros(fracture.shape, F32)
    width = fracture.shape[1]
    tables = [fracture[:, i : i + LANES] for i in range(0, width, LANES)]
    sums = []
    for start in range(0, width, LANES):
        total = jnp.zeros(tables[0].shape, F32)
        for j in range(links_ref.shape[0]):
            link = links_ref[j, :, start : start + LANES]
            found = jnp.zeros(tables[0].shape, F32)
            for i, table in enumerate(tables):
                found = jnp.where(
                    link >> log2(LANES) == i, lane_gather(table, link & (LANES - 1)), found
                )
            total = total + link_weights_ref[j, :, start : start + LANES] * found
        sums.append(total)
    return jnp.concatenate(sums, axis=1)


def relaxed_side(now, beyond, edge, scaled, inverse, relaxation):
    depth, cols = edge.shape
    place = iota(edge.shape, 1)
    zero_plane = jnp.zeros((1, cols), F32)
    after = []
    for far in range(HALO):
        here = now[far]
        beside = jnp.concatenate([here[1:], zero_plane], axis=0)
        beside = beside + jnp.concatenate([zero_plane, here[:-1]], axis=0)
        beside = beside + jnp.where(place == 0, 0.0, pltpu.roll(here, 1, 1))
        beside = beside + jnp.where(place == cols - 1, 0.0, pltpu.roll(here, cols - 1, 1))
        beside = beside + (edge if far == 0 else now[far - 1])
        if far + 1 < HALO:
            beside = beside + now[far + 1]
        elif beyond is not None:
            beside = beside + beyond
        after.append(
            (1.0 - relaxation) * here + relaxation * (scaled[far] + inverse[far] * beside)
        )
    return after


def side_slots(side_ref, slots):
    half = slots // 2
    return [
        jnp.concatenate(
            [side_ref[3 * HALO + 1, i : i + 1, :half] for i in (2 * j, 2 * j + 1)], axis=1
        )
        for j in range(4)
    ]


def spread_side(place, low, values, depth, col_groups):
    rows = iota((col_groups * HALO * depth, place.shape[1]), 0)
    hot = (rows == place).astype(F32).astype(BF16)
    added = fold(matmul(hot, masked_parts(low, values), (1, 1)), 0)
    return [
        jnp.concatenate(
            [
                added[(group * HALO + far) * depth : (group * HALO + far + 1) * depth]
                for group in range(col_groups)
            ],
            axis=1,
        )
        for far in range(HALO)
    ]


def first_window_kernel(
    relaxation,
    matrix_ref,
    low_ref,
    high_ref,
    source_ref,
    storage_ref,
    slot_index_ref,
    slot_weight_ref,
    fracture_ref,
    links_ref,
    link_weights_ref,
    partial_ref,
    scaled_ref,
    inverse_ref,
    side_partial_ref,
    side_scaled_ref,
    side_inverse_ref,
    link_sum_ref,
    hot_ref,
):
    depth, area_rows, cols = matrix_ref.shape
    plane_rows = depth * area_rows
    slots = slot_index_ref.shape[1]
    fill_hot(hot_ref, slot_index_ref[0:1])
    parts = masked_parts(slot_index_ref[1:2], slot_weight_ref[...])
    added = fold(matmul(hot_ref[...], parts, (1, 1)), 0)
    for c in range(cols // LANES):
        lanes = slice(c * LANES, (c + 1) * LANES)
        extra = added[c * plane_rows : (c + 1) * plane_rows].reshape(depth, area_rows, LANES)
        inverse = 1.0 / (6.0 + storage_ref[:, :, lanes] + extra)
        scaled_ref[:, :, lanes] = source_ref[:, :, lanes] * inverse
        inverse_ref[:, :, lanes] = inverse
    partial_ref[...] = relaxed(
        matrix_ref[...],
        scaled_ref[...],
        inverse_ref[...],
        low_ref[0],
        high_ref[0],
        relaxation,
    )
    for side, (ref, edge) in enumerate(((low_ref, 0), (high_ref, area_rows - 1))):
        place, low, weight, _ = side_slots(ref, slots)
        added = spread_side(
            place.astype(jnp.int32), low.astype(jnp.int32), weight, depth, cols // LANES
        )
        for far in range(HALO):
            storage = ref[2 * HALO + 1 + far]
            inverse = jnp.where(storage > 0.0, 1.0 / (6.0 + storage + added[far]), 0.0)
            side_inverse_ref[side, far] = inverse
            side_scaled_ref[side, far] = ref[HALO + 1 + far] * inverse
        after = relaxed_side(
            [ref[far] for far in range(HALO)],
            ref[HALO],
            matrix_ref[:, edge, :],
            [side_scaled_ref[side, far] for far in range(HALO)],
            [side_inverse_ref[side, far] for far in range(HALO)],
            relaxation,
        )
        for far in range(HALO):
            side_partial_ref[side, far] = after[far]
    link_sum_ref[...] = linked(fracture_ref[...], links_ref, link_weights_ref)


def window_kernel(
    relaxation,
    before,
    cap,
    first,
    arrived_ref,
    low_ref,
    high_ref,
    matrix_ref,
    scaled_ref,
    inverse_ref,
    side_before_ref,
    side_scaled_ref,
    side_inverse_ref,
    fracture_ref,
    links_ref,
    link_weights_ref,
    partial_ref,
    side_partial_ref,
    link_sum_ref,
):
    depth, area_rows, cols = matrix_ref.shape
    devices = arrived_ref.shape[0]
    slots = devices * cap
    edges = []
    for side, (ref, edge) in enumerate(((low_ref, 0), (high_ref, area_rows - 1))):
        place, low, weight, code = side_slots(ref, slots)
        if first:
            code = from_dense(code, devices, cap).astype(jnp.int32)
            returned = device_values(arrived_ref, code)
        else:
            returned = arrived_ref[:, 2 + side, :]
        added = spread_side(
            place.astype(jnp.int32),
            low.astype(jnp.int32),
            weight * to_dense(returned, cap),
            depth,
            cols // LANES,
        )
        now = [
            side_before_ref[side, far] + before * side_inverse_ref[side, far] * added[far]
            for far in range(HALO)
        ]
        edges.append(now[0])
        after = relaxed_side(
            now,
            None,
            matrix_ref[:, edge, :],
            [side_scaled_ref[side, far] for far in range(HALO)],
            [side_inverse_ref[side, far] for far in range(HALO)],
            relaxation,
        )
        for far in range(HALO):
            side_partial_ref[side, far] = after[far]
    partial_ref[...] = relaxed(
        matrix_ref[...],
        scaled_ref[...],
        inverse_ref[...],
        edges[0],
        edges[1],
        relaxation,
    )
    link_sum_ref[...] = linked(fracture_ref[...], links_ref, link_weights_ref)


def couple(
    relaxation,
    cap,
    returned,
    partial_ref,
    inverse_ref,
    hot_ref,
    slot_index_ref,
    slot_weight_ref,
    matrix_ref,
    columns_ref,
):
    plane_rows = partial_ref.shape[0] * partial_ref.shape[1]
    fill_hot(hot_ref, slot_index_ref[0:1])
    low = slot_index_ref[1:2]
    weight = slot_weight_ref[...]
    parts = masked_parts(low, weight * to_dense(returned, cap))
    added = fold(matmul(hot_ref[...], parts, (1, 1)), 0)
    for c in range(partial_ref.shape[2] // LANES):
        lanes = slice(c * LANES, (c + 1) * LANES)
        extra = added[c * plane_rows : (c + 1) * plane_rows].reshape(
            partial_ref.shape[:2] + (LANES,)
        )
        chunk = partial_ref[:, :, lanes] + (relaxation * inverse_ref[:, :, lanes]) * extra
        matrix_ref[:, :, lanes] = chunk
        if columns_ref is not None:
            put_columns(chunk.reshape(plane_rows, LANES), c, columns_ref)
    if columns_ref is None:
        return None
    return weight * pick_low(matmul(columns_ref[...], hot_ref[...], (1, 0)), low)


def node_hot(code, rows):
    return (iota((rows, code.shape[1]), 0) == code >> log2(LANES)).astype(F32).astype(BF16)


def node_values(table, code):
    found = jnp.zeros(code.shape, F32)
    low = code & (LANES - 1)
    for row in range(table.shape[0]):
        values = jnp.broadcast_to(table[row : row + 1], code.shape)
        found = jnp.where(code >> log2(LANES) == row, lane_gather(values, low), found)
    return found


def device_values(arrived_ref, code):
    found = jnp.zeros(code.shape, F32)
    low = code & (LANES - 1)
    for row in range(arrived_ref.shape[1] - 4):
        values = lane_gather(arrived_ref[:, 4 + row, :], low)
        found = jnp.where(code >> log2(LANES) == row, values, found)
    return found


def put_requested(message_ref, values):
    zero = jnp.zeros((1, LANES), F32)
    message_ref[:, 1, :] = values
    message_ref[:, 2, :] = jnp.concatenate([zero, values[:-1]], axis=0)
    message_ref[:, 3, :] = jnp.concatenate([values[1:], zero], axis=0)


def first_step_kernel(
    relaxation,
    cap,
    arrived_ref,
    slot_code_ref,
    partial_ref,
    inverse_ref,
    slot_index_ref,
    slot_weight_ref,
    fracture_ref,
    link_sum_ref,
    fracture_source_ref,
    leak_ref,
    link_weights_ref,
    matrix_ref,
    fracture_next_ref,
    fracture_inverse_ref,
    node_code_ref,
    message_hbm,
    hot_ref,
    columns_ref,
    message_ref,
    sem,
):
    devices = arrived_ref.shape[0]
    owned = fracture_ref.shape[0]
    returned = device_values(arrived_ref, slot_code_ref[...])
    table_rows = arrived_ref.shape[1] - 4
    outgoing = couple(
        relaxation,
        cap,
        returned,
        partial_ref,
        inverse_ref,
        hot_ref,
        slot_index_ref,
        slot_weight_ref,
        matrix_ref,
        columns_ref,
    )
    code = arrived_ref[:, 0, :].astype(jnp.int32)
    node_code_ref[...] = code
    dense = to_dense(code, cap)
    parts = masked_parts(
        dense & (LANES - 1),
        to_dense(arrived_ref[:, 1, :], cap),
        to_dense(arrived_ref[:, 2, :], cap),
    )
    sums = matmul(node_hot(dense, table_rows), parts, (1, 1))
    diag = (
        leak_ref[...] + jnp.sum(link_weights_ref[...], axis=0) + unstack_lanes(fold(sums, 0), owned)
    )
    inverse = 1.0 / diag
    fracture_inverse_ref[...] = inverse
    fracture_next = (1.0 - relaxation) * fracture_ref[...] + (relaxation * inverse) * (
        fracture_source_ref[...] + link_sum_ref[...] + unstack_lanes(fold(sums, 1), owned)
    )
    fracture_next_ref[...] = fracture_next
    message_ref[:, 0, :] = from_dense(outgoing, devices, cap)
    put_requested(message_ref, node_values(stack_lanes(fracture_next), code))
    out = pltpu.make_async_copy(message_ref, message_hbm, sem)
    out.start()
    out.wait()


def step_kernel(
    relaxation,
    cap,
    last,
    arrived_ref,
    node_code_ref,
    partial_ref,
    inverse_ref,
    slot_index_ref,
    slot_weight_ref,
    fracture_ref,
    link_sum_ref,
    fracture_source_ref,
    fracture_inverse_ref,
    matrix_ref,
    fracture_next_ref,
    *refs,
):
    if last:
        (hot_ref,) = refs
        columns_ref = None
    else:
        message_hbm, hot_ref, columns_ref, message_ref, sem = refs
    devices = arrived_ref.shape[0]
    owned, blk = fracture_ref.shape
    outgoing = couple(
        relaxation,
        cap,
        arrived_ref[:, 1, :],
        partial_ref,
        inverse_ref,
        hot_ref,
        slot_index_ref,
        slot_weight_ref,
        matrix_ref,
        columns_ref,
    )
    code = node_code_ref[...]
    dense = to_dense(code, cap)
    parts = masked_parts(dense & (LANES - 1), to_dense(arrived_ref[:, 0, :], cap))
    sums = matmul(node_hot(dense, owned * blk // LANES), parts, (1, 1))
    fracture_next = (1.0 - relaxation) * fracture_ref[...] + (
        relaxation * fracture_inverse_ref[...]
    ) * (fracture_source_ref[...] + link_sum_ref[...] + unstack_lanes(fold(sums, 0), owned))
    fracture_next_ref[...] = fracture_next
    if last:
        return
    message_ref[:, 0, :] = from_dense(outgoing, devices, cap)
    put_requested(message_ref, node_values(stack_lanes(fracture_next), code))
    out = pltpu.make_async_copy(message_ref, message_hbm, sem)
    out.start()
    out.wait()


def call(kernel, outs, ins, name, micros, hbm_in=(), hbm_out=(), scratch=(), aliases=None, limit=VMEM_LIMIT):
    return pl.pallas_call(
        kernel,
        out_shape=[jax.ShapeDtypeStruct(shape, dtype) for shape, dtype in outs],
        in_specs=[
            pl.BlockSpec(memory_space=pltpu.HBM if i in hbm_in else pltpu.VMEM)
            for i in range(len(ins))
        ],
        out_specs=[
            pl.BlockSpec(memory_space=pltpu.HBM if i in hbm_out else pltpu.VMEM)
            for i in range(len(outs))
        ],
        scratch_shapes=list(scratch),
        input_output_aliases=aliases or {},
        compiler_params=pltpu.CompilerParams(vmem_limit_bytes=limit),
        cost_estimate=pl.CostEstimate(
            flops=0, bytes_accessed=int(micros * 3.0e6), transcendentals=0
        ),
        name=name,
    )(*ins)


def local(
    block_owner,
    transfer_cells,
    transfer_nodes,
    transfer_weights,
    row_counts,
    matrix_start,
    matrix_source,
    matrix_storage,
    fracture_start,
    fracture_source,
    fracture_leak,
    fracture_links,
    link_weights,
):
    devices = lax.axis_size("area")
    depth, area_rows, cols = matrix_start.shape
    owned, blk = fracture_start.shape
    total_rows = transfer_cells.shape[0]
    cap = 3 * total_rows // (2 * devices)
    slots = devices * cap
    cells = depth * area_rows * cols // LANES
    table_rows = owned * blk // LANES
    relax = relax_weights(ITERS)
    grid = (matrix_start.shape, F32)
    fracture = (fracture_start.shape, F32)
    side = ((3 * HALO + 2, depth, cols), F32)
    sides = ((2, HALO, depth, cols), F32)
    hot = pltpu.VMEM((cells, slots), BF16)
    columns = pltpu.VMEM((2 * LANES, cells), BF16)
    padded = (devices, LANES)
    first_message = ((devices, 4 + table_rows, LANES), F32)
    later_message = ((devices, 4, LANES), F32)
    forward = [(i, i + 1) for i in range(devices - 1)]
    backward = [(target, source) for source, target in forward]

    def exchange(message):
        return lax.all_to_all(message, "area", split_axis=0, concat_axis=0, tiled=True)

    staged = [
        row_counts.reshape(1, 1),
        block_owner.reshape(-1, LANES),
        transfer_cells.reshape(-1, LANES),
        transfer_nodes.reshape(-1, LANES),
        transfer_weights.reshape(-1, LANES),
        matrix_start,
        fracture_start,
        matrix_source,
        matrix_storage,
    ]
    slot_index, slot_weight, slot_code, message, up, down = call(
        functools.partial(setup_kernel, devices, cap, len(staged)),
        [
            ((2, slots), jnp.int32),
            ((1, slots), F32),
            (padded, jnp.int32),
            first_message,
            side,
            side,
        ],
        staged,
        "place_rows",
        5.0,
        hbm_in=range(len(staged)),
        hbm_out=(3, 4, 5),
        scratch=[pltpu.VMEM(x.shape, x.dtype) for x in staged]
        + [
            pltpu.VMEM(*first_message),
            pltpu.VMEM(*side),
            pltpu.VMEM(*side),
            hot,
            columns,
            pltpu.SemaphoreType.DMA((len(staged) + 3,)),
        ],
        limit=63 * 1024 * 1024,
    )
    arrived = exchange(message)
    low = lax.ppermute(up, "area", forward)
    high = lax.ppermute(down, "area", backward)
    partial, scaled, inverse, side_partial, side_scaled, side_inverse, link_sum = call(
        functools.partial(first_window_kernel, relax[0]),
        [grid, grid, grid, sides, sides, sides, fracture],
        [
            matrix_start,
            low,
            high,
            matrix_source,
            matrix_storage,
            slot_index,
            slot_weight,
            fracture_start,
            fracture_links,
            link_weights,
        ],
        "stencil_first",
        4.0,
        scratch=[hot],
    )
    fracture_now = fracture_start
    matrix, fracture_now, fracture_inverse, node_code, message = call(
        functools.partial(first_step_kernel, relax[0], cap),
        [grid, fracture, fracture, (padded, jnp.int32), later_message],
        [
            arrived,
            slot_code,
            partial,
            inverse,
            slot_index,
            slot_weight,
            fracture_now,
            link_sum,
            fracture_source,
            fracture_leak,
            link_weights,
        ],
        "couple_first",
        4.0,
        hbm_out=(4,),
        scratch=[hot, columns, pltpu.VMEM(*later_message), pltpu.SemaphoreType.DMA],
    )
    for index in range(1, ITERS):
        last = index == ITERS - 1
        old, arrived = arrived, exchange(message)
        partial, side_partial, link_sum = call(
            functools.partial(window_kernel, relax[index], relax[index - 1], cap, index == 1),
            [grid, sides, fracture],
            [
                old,
                low,
                high,
                matrix,
                scaled,
                inverse,
                side_partial,
                side_scaled,
                side_inverse,
                fracture_now,
                fracture_links,
                link_weights,
            ],
            "stencil",
            3.0,
            aliases={6: 1},
        )
        outs = call(
            functools.partial(step_kernel, relax[index], cap, last),
            [grid, fracture] + ([] if last else [later_message]),
            [
                arrived,
                node_code,
                partial,
                inverse,
                slot_index,
                slot_weight,
                fracture_now,
                link_sum,
                fracture_source,
                fracture_inverse,
            ],
            "couple",
            3.0,
            hbm_out=() if last else (2,),
            scratch=[hot]
            + ([] if last else [columns, pltpu.VMEM(*later_message), pltpu.SemaphoreType.DMA]),
        )
        matrix, fracture_now = outs[:2]
        if not last:
            message = outs[2]
    return (matrix, fracture_now)


def solution(mesh):
    in_specs = (
        P(),
        P("area"),
        P("area"),
        P("area"),
        P("area"),
        P("real", "area", None),
        P("real", "area", None),
        P("real", "area", None),
        P("area", "real"),
        P("area", "real"),
        P("area", "real"),
        P(None, "area", None),
        P("real", "area", None),
    )
    out_specs = (P("real", "area", None), P("area", "real"))
    return jax.shard_map(local, mesh=mesh, in_specs=in_specs, out_specs=out_specs, check_vma=False)
```

```python
import functools
import math

import jax
import jax.numpy as jnp
from jax import lax
from jax.experimental import pallas as pl
from jax.experimental.pallas import tpu as pltpu
from jax.sharding import PartitionSpec as P

ITERS = 4
HALO = ITERS - 1
LANES = 128
F32 = jnp.float32
BF16 = jnp.bfloat16
VMEM_LIMIT = 32 * 1024 * 1024


def relax_weights(steps_total):
    return [
        1.0 / (1.0 + 0.75 * math.cos(math.pi * (2 * index + 1) / (2 * steps_total)))
        for index in range(steps_total)
    ]


def log2(value):
    assert value & (value - 1) == 0
    return value.bit_length() - 1


def group_order(devices):
    part = devices // 4
    return [quarter * part + (i - 1) % part for quarter in (2, 0, 1, 3) for i in range(part)]


def iota(shape, dim):
    return lax.broadcasted_iota(jnp.int32, shape, dim)


def halves(x):
    high = x.astype(BF16)
    low = (x - high.astype(F32)).astype(BF16)
    return high, low


def matmul(a, b, contract):
    return lax.dot_general(a, b, ((contract[:1], contract[1:]), ((), ())), preferred_element_type=F32)


def to_dense(x, cap):
    return jnp.concatenate([x[i : i + 1, :cap] for i in range(x.shape[0])], axis=1)


def from_dense(x, devices, cap):
    rows = jnp.concatenate([x[:, i * cap : (i + 1) * cap] for i in range(devices)], axis=0)
    return jnp.concatenate([rows, jnp.zeros((devices, LANES - cap), x.dtype)], axis=1)


def lane_gather(table, index):
    return jnp.take_along_axis(table, index, axis=1, mode="promise_in_bounds")


def masked_parts(low, *values):
    mask = iota((LANES, low.shape[1]), 0) == low
    zero = jnp.zeros((), F32)
    parts = []
    for value in values:
        high = value.astype(BF16).astype(F32)
        parts.append(jnp.where(mask, high, zero).astype(BF16))
        parts.append(jnp.where(mask, value - high, zero).astype(BF16))
    return jnp.concatenate(parts, axis=0)


def fold(wide, index):
    start = 2 * index * LANES
    return wide[:, start : start + LANES] + wide[:, start + LANES : start + 2 * LANES]


def pick_low(tall, low):
    both = tall[:LANES] + tall[LANES:]
    return jnp.sum(
        jnp.where(iota(both.shape, 0) == low, both, 0.0), axis=0, keepdims=True
    )


def stack_lanes(x):
    return jnp.concatenate(
        [x[:, i * LANES : (i + 1) * LANES] for i in range(x.shape[1] // LANES)], axis=0
    )


def unstack_lanes(x, rows):
    return jnp.concatenate([x[i : i + rows] for i in range(0, x.shape[0], rows)], axis=1)


def put_columns(chunk, index, columns_ref):
    high, low = halves(chunk.T)
    columns_ref[:LANES, index * LANES : (index + 1) * LANES] = high
    columns_ref[LANES:, index * LANES : (index + 1) * LANES] = low


def fill_hot(hot_ref, slot_high):
    for start in range(0, hot_ref.shape[0], LANES):
        rows = iota((LANES, slot_high.shape[1]), 0) + start
        hot_ref[start : start + LANES, :] = (rows == slot_high).astype(F32).astype(BF16)


def setup_kernel(devices, cap, staged, *refs):
    sources, refs = refs[:staged], refs[staged:]
    slot_index_ref, slot_weight_ref, slot_code_ref, cell_rows_ref, cell_columns_ref = refs[:5]
    message_hbm, up_hbm, down_hbm = refs[5:8]
    targets, refs = refs[8 : 8 + staged], refs[8 + staged :]
    message_ref, up_ref, down_ref, hot_ref, columns_ref, sems = refs
    copies = [
        pltpu.make_async_copy(sources[i], targets[i], sems.at[i]) for i in range(staged)
    ]
    for copy in copies:
        copy.start()
    for copy in copies[:5]:
        copy.wait()
    counts_ref, owner_ref, cells_ref, nodes_ref, weights_ref = targets[:5]
    matrix_ref, fracture_ref, source_ref, storage_ref = targets[5:]
    owned, blk = fracture_ref.shape
    depth, area_rows, cols = matrix_ref.shape
    groups = cells_ref.shape[0]
    slots = devices * cap
    plane_rows = matrix_ref.shape[0] * matrix_ref.shape[1]
    col_groups = cols // LANES
    shape = (groups, LANES)
    nodes, cells = nodes_ref[...], cells_ref[...]
    live = iota(shape, 0) * LANES + iota(shape, 1) < counts_ref[...]
    weight = jnp.where(live, weights_ref[...], 0.0)
    block = nodes >> log2(blk)
    slot = jnp.zeros(shape, jnp.int32)
    for part in range(owner_ref.shape[0]):
        table = jnp.broadcast_to(owner_ref[part : part + 1, :], shape)
        found = lane_gather(table, block & (LANES - 1))
        slot = jnp.where(block >> log2(LANES) == part, found, slot)
    device = slot >> log2(owned)
    target = jnp.zeros(shape, jnp.int32)
    for position, member in enumerate(group_order(devices)):
        target = jnp.where(device == member, position, target)
    target = jnp.where(live, target, -1)
    node_high = ((nodes & (blk - 1)) >> log2(LANES)) * owned + (slot & (owned - 1))
    node_low = nodes & (LANES - 1)
    cell_plane = cells >> log2(cols)
    cell_group = (cells & (cols - 1)) >> log2(LANES)
    cell_low = cells & (LANES - 1)

    device_rows = iota((devices, LANES), 0)
    member = [(device_rows == target[q : q + 1]).astype(F32) for q in range(groups)]
    earlier = (iota((LANES, LANES), 0) < iota((LANES, LANES), 1)).astype(BF16)
    counted = matmul(jnp.concatenate(member, axis=0).astype(BF16), earlier, (1, 0))
    before = jnp.zeros((devices, 1), F32)
    placed = []
    for q in range(groups):
        rank = jnp.sum(
            member[q] * (counted[q * devices : (q + 1) * devices] + before), axis=0, keepdims=True
        ).astype(jnp.int32)
        before = before + jnp.sum(member[q], axis=1, keepdims=True)
        where = target[q : q + 1]
        placed.append(jnp.where(where >= 0, where * cap + rank, -1))
    placed = jnp.concatenate(placed, axis=1)

    high = weight.astype(BF16).astype(F32)
    middle = (weight - high).astype(BF16).astype(F32)
    low = weight - high - middle
    features = [
        jnp.where(live, 1.0, 0.0),
        node_high.astype(F32),
        node_low.astype(F32),
        cell_plane.astype(F32),
        cell_group.astype(F32),
        cell_low.astype(F32),
        high,
        middle,
        low,
    ]
    features = [jnp.concatenate([x[q : q + 1] for q in range(groups)], axis=1) for x in features]
    features = jnp.concatenate(
        features + [jnp.zeros((16 - len(features), groups * LANES), F32)], axis=0
    ).astype(BF16)
    placing = (iota((slots, groups * LANES), 0) == placed).astype(F32).astype(BF16)
    packed = matmul(features, placing, (1, 1))
    used = packed[0:1] > 0.5
    code = packed[1:2] * LANES + packed[2:3]
    code = jnp.where(used, code, -1.0)
    slot_high = jnp.where(used, packed[4:5] * plane_rows + packed[3:4], -1.0).astype(jnp.int32)
    slot_low = packed[5:6].astype(jnp.int32)
    slot_weight = packed[6:7] + packed[7:8] + packed[8:9]
    fill_hot(hot_ref, slot_high)
    slot_index_ref[0:1] = slot_high
    slot_index_ref[1:2] = slot_low
    slot_weight_ref[...] = slot_weight
    padded_code = from_dense(code, devices, cap)
    slot_code_ref[...] = padded_code.astype(jnp.int32)
    message_ref[:, 0, :] = jnp.where(iota((devices, LANES), 1) < cap, padded_code, -1.0)
    message_ref[:, 1, :] = from_dense(slot_weight, devices, cap)
    message_ref[:, 3, :] = jnp.zeros((devices, LANES), F32)

    cell = jnp.where(used, (slot_high * LANES + slot_low).astype(F32), -1.0)
    rows = stack_lanes(cell)
    cell_rows_ref[...] = rows
    cell_columns_ref[...] = turned(rows)

    row = slot_high & (area_rows - 1)
    plane = (slot_high >> log2(area_rows)) & (depth - 1)
    group = slot_high >> log2(plane_rows)
    half = slots // 2
    for far, side_ref in ((area_rows - 1 - row, up_ref), (row, down_ref)):
        place = (group * HALO + far) * depth + plane
        place = jnp.where(used & (far < HALO), place, -1).astype(F32)
        for i, x in enumerate((place, packed[5:6], slot_weight, code)):
            side_ref[3 * HALO + 1, 2 * i : 2 * i + 1, :half] = x[:, :half]
            side_ref[3 * HALO + 1, 2 * i + 1 : 2 * i + 2, :half] = x[:, half:]

    for copy in copies[5:]:
        copy.wait()
    nodes_table = stack_lanes(fracture_ref[...])
    message_ref[:, 4:, :] = jnp.broadcast_to(nodes_table[None], (devices,) + nodes_table.shape)
    for ref, start, count in (
        (matrix_ref, 0, HALO + 1),
        (source_ref, HALO + 1, HALO),
        (storage_ref, 2 * HALO + 1, HALO),
    ):
        for far in range(count):
            up_ref[start + far] = ref[:, area_rows - 1 - far, :]
            down_ref[start + far] = ref[:, far, :]
    outs = [
        pltpu.make_async_copy(up_ref, up_hbm, sems.at[staged]),
        pltpu.make_async_copy(down_ref, down_hbm, sems.at[staged + 1]),
        pltpu.make_async_copy(message_ref, message_hbm, sems.at[staged + 2]),
    ]
    outs[0].start()
    outs[1].start()
    for c in range(col_groups):
        chunk = matrix_ref[:, :, c * LANES : (c + 1) * LANES].reshape(plane_rows, LANES)
        put_columns(chunk, c, columns_ref)
    picked = pick_low(matmul(columns_ref[...], hot_ref[...], (1, 0)), slot_low)
    message_ref[:, 2, :] = from_dense(slot_weight * picked, devices, cap)
    outs[2].start()
    for out in outs:
        out.wait()


def turned(rows):
    count = rows.shape[0]
    extra = -count % 8
    if extra:
        rows = jnp.concatenate([rows, jnp.zeros((extra, LANES), rows.dtype)], axis=0)
    return rows.T


def same_cell_sum(values, cell_rows, cell_columns):
    value_columns = turned(stack_lanes(values))
    blocks = cell_rows.shape[0]
    sums = [jnp.zeros((8, LANES), F32) for _ in range(blocks)]
    for j in range(blocks):
        cell = jnp.broadcast_to(cell_columns[:, j : j + 1], (LANES, LANES))
        value = jnp.broadcast_to(value_columns[:, j : j + 1], (LANES, LANES))
        for i in range(blocks):
            hit = jnp.where(cell == cell_rows[i : i + 1], value, 0.0)
            sums[i] = sums[i] + jnp.sum(hit.reshape(LANES // 8, 8, LANES), axis=0)
    return jnp.concatenate([jnp.sum(x, axis=0, keepdims=True) for x in sums], axis=1)


def relaxed(now, source, inverse, low_side, high_side, relaxation):
    depth, rows, cols = now.shape
    zero_plane = jnp.zeros((1, rows, cols), F32)
    beside = jnp.concatenate([now[1:], zero_plane], axis=0)
    beside = beside + jnp.concatenate([zero_plane, now[:-1]], axis=0)
    beside = beside + jnp.concatenate([now[:, 1:], high_side[:, None]], axis=1)
    beside = beside + jnp.concatenate([low_side[:, None], now[:, :-1]], axis=1)
    flat = now.reshape(depth * rows, cols)
    place = iota(flat.shape, 1)
    left = jnp.where(place == 0, 0.0, pltpu.roll(flat, 1, 1))
    right = jnp.where(place == cols - 1, 0.0, pltpu.roll(flat, cols - 1, 1))
    beside = beside + (left + right).reshape(now.shape)
    return (1.0 - relaxation) * now + relaxation * (source + inverse * beside)


def linked(fracture, links_ref, link_weights_ref):
    total = jnp.zeros(fracture.shape, F32)
    width = fracture.shape[1]
    tables = [fracture[:, i : i + LANES] for i in range(0, width, LANES)]
    sums = []
    for start in range(0, width, LANES):
        total = jnp.zeros(tables[0].shape, F32)
        for j in range(links_ref.shape[0]):
            link = links_ref[j, :, start : start + LANES]
            found = jnp.zeros(tables[0].shape, F32)
            for i, table in enumerate(tables):
                found = jnp.where(
                    link >> log2(LANES) == i, lane_gather(table, link & (LANES - 1)), found
                )
            total = total + link_weights_ref[j, :, start : start + LANES] * found
        sums.append(total)
    return jnp.concatenate(sums, axis=1)


def relaxed_side(now, beyond, edge, scaled, inverse, relaxation):
    depth, cols = edge.shape
    place = iota(edge.shape, 1)
    zero_plane = jnp.zeros((1, cols), F32)
    after = []
    for far in range(HALO):
        here = now[far]
        beside = jnp.concatenate([here[1:], zero_plane], axis=0)
        beside = beside + jnp.concatenate([zero_plane, here[:-1]], axis=0)
        beside = beside + jnp.where(place == 0, 0.0, pltpu.roll(here, 1, 1))
        beside = beside + jnp.where(place == cols - 1, 0.0, pltpu.roll(here, cols - 1, 1))
        beside = beside + (edge if far == 0 else now[far - 1])
        if far + 1 < HALO:
            beside = beside + now[far + 1]
        elif beyond is not None:
            beside = beside + beyond
        after.append(
            (1.0 - relaxation) * here + relaxation * (scaled[far] + inverse[far] * beside)
        )
    return after


def side_slots(side_ref, slots):
    half = slots // 2
    return [
        jnp.concatenate(
            [side_ref[3 * HALO + 1, i : i + 1, :half] for i in (2 * j, 2 * j + 1)], axis=1
        )
        for j in range(4)
    ]


def spread_side(place, low, values, depth, col_groups):
    rows = iota((col_groups * HALO * depth, place.shape[1]), 0)
    hot = (rows == place).astype(F32).astype(BF16)
    added = fold(matmul(hot, masked_parts(low, values), (1, 1)), 0)
    return [
        jnp.concatenate(
            [
                added[(group * HALO + far) * depth : (group * HALO + far + 1) * depth]
                for group in range(col_groups)
            ],
            axis=1,
        )
        for far in range(HALO)
    ]


def pick_cells(table_ref, columns_ref, hot_ref, low):
    depth, area_rows, cols = table_ref.shape
    for c in range(cols // LANES):
        chunk = table_ref[:, :, c * LANES : (c + 1) * LANES]
        put_columns(chunk.reshape(depth * area_rows, LANES), c, columns_ref)
    return pick_low(matmul(columns_ref[...], hot_ref[...], (1, 0)), low)


def diagonal_kernel(
    source_ref,
    storage_ref,
    slot_index_ref,
    slot_weight_ref,
    scaled_ref,
    inverse_ref,
    row_inverse_ref,
    hot_ref,
    columns_ref,
):
    depth, area_rows, cols = source_ref.shape
    plane_rows = depth * area_rows
    low = slot_index_ref[1:2]
    weight = slot_weight_ref[...]
    fill_hot(hot_ref, slot_index_ref[0:1])
    added = fold(matmul(hot_ref[...], masked_parts(low, weight), (1, 1)), 0)
    for c in range(cols // LANES):
        lanes = slice(c * LANES, (c + 1) * LANES)
        extra = added[c * plane_rows : (c + 1) * plane_rows].reshape(depth, area_rows, LANES)
        inverse = 1.0 / (6.0 + storage_ref[:, :, lanes] + extra)
        scaled_ref[:, :, lanes] = source_ref[:, :, lanes] * inverse
        inverse_ref[:, :, lanes] = inverse
    row_inverse_ref[...] = weight * pick_cells(inverse_ref, columns_ref, hot_ref, low)


def first_window_kernel(
    relaxation,
    matrix_ref,
    low_ref,
    high_ref,
    scaled_ref,
    inverse_ref,
    slot_index_ref,
    slot_weight_ref,
    fracture_ref,
    links_ref,
    link_weights_ref,
    partial_ref,
    side_partial_ref,
    side_scaled_ref,
    side_inverse_ref,
    row_partial_ref,
    link_sum_ref,
    hot_ref,
    columns_ref,
):
    depth, area_rows, cols = matrix_ref.shape
    slots = slot_index_ref.shape[1]
    fill_hot(hot_ref, slot_index_ref[0:1])
    partial_ref[...] = relaxed(
        matrix_ref[...],
        scaled_ref[...],
        inverse_ref[...],
        low_ref[0],
        high_ref[0],
        relaxation,
    )
    row_partial_ref[...] = slot_weight_ref[...] * pick_cells(
        partial_ref, columns_ref, hot_ref, slot_index_ref[1:2]
    )
    for side, (ref, edge) in enumerate(((low_ref, 0), (high_ref, area_rows - 1))):
        place, low, weight, _ = side_slots(ref, slots)
        added = spread_side(
            place.astype(jnp.int32), low.astype(jnp.int32), weight, depth, cols // LANES
        )
        for far in range(HALO):
            storage = ref[2 * HALO + 1 + far]
            inverse = jnp.where(storage > 0.0, 1.0 / (6.0 + storage + added[far]), 0.0)
            side_inverse_ref[side, far] = inverse
            side_scaled_ref[side, far] = ref[HALO + 1 + far] * inverse
        after = relaxed_side(
            [ref[far] for far in range(HALO)],
            ref[HALO],
            matrix_ref[:, edge, :],
            [side_scaled_ref[side, far] for far in range(HALO)],
            [side_inverse_ref[side, far] for far in range(HALO)],
            relaxation,
        )
        for far in range(HALO):
            side_partial_ref[side, far] = after[far]
    link_sum_ref[...] = linked(fracture_ref[...], links_ref, link_weights_ref)


def add_rows(relaxation, values, partial_ref, inverse_ref, slot_index_ref, hot_ref, matrix_ref):
    depth, area_rows, cols = partial_ref.shape
    plane_rows = depth * area_rows
    fill_hot(hot_ref, slot_index_ref[0:1])
    added = fold(matmul(hot_ref[...], masked_parts(slot_index_ref[1:2], values), (1, 1)), 0)
    for c in range(cols // LANES):
        lanes = slice(c * LANES, (c + 1) * LANES)
        extra = added[c * plane_rows : (c + 1) * plane_rows].reshape(depth, area_rows, LANES)
        matrix_ref[:, :, lanes] = (
            partial_ref[:, :, lanes] + (relaxation * inverse_ref[:, :, lanes]) * extra
        )


def window_kernel(
    relaxation,
    before,
    cap,
    first,
    last,
    arrived_ref,
    low_ref,
    high_ref,
    partial_before_ref,
    scaled_ref,
    inverse_ref,
    side_before_ref,
    side_scaled_ref,
    side_inverse_ref,
    slot_index_ref,
    slot_weight_ref,
    slot_code_ref,
    fracture_ref,
    links_ref,
    link_weights_ref,
    partial_ref,
    side_partial_ref,
    link_sum_ref,
    *refs,
):
    if last:
        matrix_ref, hot_ref = refs
    else:
        row_partial_ref, matrix_ref, hot_ref, columns_ref = refs
    depth, area_rows, cols = scaled_ref.shape
    devices = arrived_ref.shape[0]
    slots = devices * cap
    returned = device_values(arrived_ref, slot_code_ref[...]) if first else arrived_ref[:, 1, :]
    values = slot_weight_ref[...] * to_dense(returned, cap)
    add_rows(before, values, partial_before_ref, inverse_ref, slot_index_ref, hot_ref, matrix_ref)
    edges = []
    for side, (ref, edge) in enumerate(((low_ref, 0), (high_ref, area_rows - 1))):
        place, low, weight, code = side_slots(ref, slots)
        if first:
            code = from_dense(code, devices, cap).astype(jnp.int32)
            returned = device_values(arrived_ref, code)
        else:
            returned = arrived_ref[:, 2 + side, :]
        added = spread_side(
            place.astype(jnp.int32),
            low.astype(jnp.int32),
            weight * to_dense(returned, cap),
            depth,
            cols // LANES,
        )
        now = [
            side_before_ref[side, far] + before * side_inverse_ref[side, far] * added[far]
            for far in range(HALO)
        ]
        edges.append(now[0])
        after = relaxed_side(
            now,
            None,
            matrix_ref[:, edge, :],
            [side_scaled_ref[side, far] for far in range(HALO)],
            [side_inverse_ref[side, far] for far in range(HALO)],
            relaxation,
        )
        for far in range(HALO):
            side_partial_ref[side, far] = after[far]
    partial_ref[...] = relaxed(
        matrix_ref[...],
        scaled_ref[...],
        inverse_ref[...],
        edges[0],
        edges[1],
        relaxation,
    )
    if not last:
        row_partial_ref[...] = slot_weight_ref[...] * pick_cells(
            partial_ref, columns_ref, hot_ref, slot_index_ref[1:2]
        )
    link_sum_ref[...] = linked(fracture_ref[...], links_ref, link_weights_ref)


def row_values(
    relaxation,
    cap,
    returned,
    slot_weight_ref,
    row_partial_ref,
    row_inverse_ref,
    cell_rows_ref,
    cell_columns_ref,
):
    values = slot_weight_ref[...] * to_dense(returned, cap)
    total = same_cell_sum(values, cell_rows_ref[...], cell_columns_ref[...])
    outgoing = row_partial_ref[...] + (relaxation * row_inverse_ref[...]) * total
    return from_dense(outgoing, returned.shape[0], cap)


def node_hot(code, rows):
    return (iota((rows, code.shape[1]), 0) == code >> log2(LANES)).astype(F32).astype(BF16)


def node_values(table, code):
    found = jnp.zeros(code.shape, F32)
    low = code & (LANES - 1)
    for row in range(table.shape[0]):
        values = jnp.broadcast_to(table[row : row + 1], code.shape)
        found = jnp.where(code >> log2(LANES) == row, lane_gather(values, low), found)
    return found


def device_values(arrived_ref, code):
    found = jnp.zeros(code.shape, F32)
    low = code & (LANES - 1)
    for row in range(arrived_ref.shape[1] - 4):
        values = lane_gather(arrived_ref[:, 4 + row, :], low)
        found = jnp.where(code >> log2(LANES) == row, values, found)
    return found


def put_requested(message_ref, values):
    zero = jnp.zeros((1, LANES), F32)
    order = group_order(values.shape[0])
    rows = {device: values[i : i + 1] for i, device in enumerate(order)}
    message_ref[:, 1, :] = values
    for place, step in ((2, -1), (3, 1)):
        message_ref[:, place, :] = jnp.concatenate(
            [rows.get(device + step, zero) for device in order], axis=0
        )


def first_step_kernel(
    relaxation,
    cap,
    arrived_ref,
    slot_code_ref,
    slot_weight_ref,
    row_partial_ref,
    row_inverse_ref,
    cell_rows_ref,
    cell_columns_ref,
    fracture_ref,
    link_sum_ref,
    fracture_source_ref,
    leak_ref,
    link_weights_ref,
    fracture_next_ref,
    fracture_inverse_ref,
    node_code_ref,
    message_hbm,
    message_ref,
    sem,
):
    owned = fracture_ref.shape[0]
    message_ref[:, 0, :] = row_values(
        relaxation,
        cap,
        device_values(arrived_ref, slot_code_ref[...]),
        slot_weight_ref,
        row_partial_ref,
        row_inverse_ref,
        cell_rows_ref,
        cell_columns_ref,
    )
    code = arrived_ref[:, 0, :].astype(jnp.int32)
    node_code_ref[...] = code
    dense = to_dense(code, cap)
    parts = masked_parts(
        dense & (LANES - 1),
        to_dense(arrived_ref[:, 1, :], cap),
        to_dense(arrived_ref[:, 2, :], cap),
    )
    sums = matmul(node_hot(dense, fracture_ref.shape[0] * fracture_ref.shape[1] // LANES), parts, (1, 1))
    diag = (
        leak_ref[...] + jnp.sum(link_weights_ref[...], axis=0) + unstack_lanes(fold(sums, 0), owned)
    )
    inverse = 1.0 / diag
    fracture_inverse_ref[...] = inverse
    fracture_next = (1.0 - relaxation) * fracture_ref[...] + (relaxation * inverse) * (
        fracture_source_ref[...] + link_sum_ref[...] + unstack_lanes(fold(sums, 1), owned)
    )
    fracture_next_ref[...] = fracture_next
    put_requested(message_ref, node_values(stack_lanes(fracture_next), code))
    out = pltpu.make_async_copy(message_ref, message_hbm, sem)
    out.start()
    out.wait()


def next_fracture(
    relaxation,
    cap,
    arrived_ref,
    code,
    fracture_ref,
    link_sum_ref,
    fracture_source_ref,
    fracture_inverse_ref,
):
    owned, blk = fracture_ref.shape
    dense = to_dense(code, cap)
    parts = masked_parts(dense & (LANES - 1), to_dense(arrived_ref[:, 0, :], cap))
    sums = matmul(node_hot(dense, owned * blk // LANES), parts, (1, 1))
    return (1.0 - relaxation) * fracture_ref[...] + (relaxation * fracture_inverse_ref[...]) * (
        fracture_source_ref[...] + link_sum_ref[...] + unstack_lanes(fold(sums, 0), owned)
    )


def step_kernel(
    relaxation,
    cap,
    arrived_ref,
    node_code_ref,
    slot_weight_ref,
    row_partial_ref,
    row_inverse_ref,
    cell_rows_ref,
    cell_columns_ref,
    fracture_ref,
    link_sum_ref,
    fracture_source_ref,
    fracture_inverse_ref,
    fracture_next_ref,
    message_hbm,
    message_ref,
    sem,
):
    message_ref[:, 0, :] = row_values(
        relaxation,
        cap,
        arrived_ref[:, 1, :],
        slot_weight_ref,
        row_partial_ref,
        row_inverse_ref,
        cell_rows_ref,
        cell_columns_ref,
    )
    code = node_code_ref[...]
    fracture_next = next_fracture(
        relaxation,
        cap,
        arrived_ref,
        code,
        fracture_ref,
        link_sum_ref,
        fracture_source_ref,
        fracture_inverse_ref,
    )
    fracture_next_ref[...] = fracture_next
    put_requested(message_ref, node_values(stack_lanes(fracture_next), code))
    out = pltpu.make_async_copy(message_ref, message_hbm, sem)
    out.start()
    out.wait()


def last_step_kernel(
    relaxation,
    cap,
    arrived_ref,
    node_code_ref,
    partial_ref,
    inverse_ref,
    slot_index_ref,
    slot_weight_ref,
    fracture_ref,
    link_sum_ref,
    fracture_source_ref,
    fracture_inverse_ref,
    matrix_ref,
    fracture_next_ref,
    hot_ref,
):
    values = slot_weight_ref[...] * to_dense(arrived_ref[:, 1, :], cap)
    add_rows(relaxation, values, partial_ref, inverse_ref, slot_index_ref, hot_ref, matrix_ref)
    fracture_next_ref[...] = next_fracture(
        relaxation,
        cap,
        arrived_ref,
        node_code_ref[...],
        fracture_ref,
        link_sum_ref,
        fracture_source_ref,
        fracture_inverse_ref,
    )


def call(kernel, outs, ins, name, micros, hbm_in=(), hbm_out=(), scratch=(), aliases=None, limit=VMEM_LIMIT):
    return pl.pallas_call(
        kernel,
        out_shape=[jax.ShapeDtypeStruct(shape, dtype) for shape, dtype in outs],
        in_specs=[
            pl.BlockSpec(memory_space=pltpu.HBM if i in hbm_in else pltpu.VMEM)
            for i in range(len(ins))
        ],
        out_specs=[
            pl.BlockSpec(memory_space=pltpu.HBM if i in hbm_out else pltpu.VMEM)
            for i in range(len(outs))
        ],
        scratch_shapes=list(scratch),
        input_output_aliases=aliases or {},
        compiler_params=pltpu.CompilerParams(vmem_limit_bytes=limit),
        cost_estimate=pl.CostEstimate(
            flops=0, bytes_accessed=int(micros * 3.0e6), transcendentals=0
        ),
        name=name,
    )(*ins)


def local(
    block_owner,
    transfer_cells,
    transfer_nodes,
    transfer_weights,
    row_counts,
    matrix_start,
    matrix_source,
    matrix_storage,
    fracture_start,
    fracture_source,
    fracture_leak,
    fracture_links,
    link_weights,
):
    devices = lax.axis_size("area")
    depth, area_rows, cols = matrix_start.shape
    owned, blk = fracture_start.shape
    total_rows = transfer_cells.shape[0]
    cap = 3 * total_rows // (2 * devices)
    slots = devices * cap
    cells = depth * area_rows * cols // LANES
    relax = relax_weights(ITERS)
    grid = (matrix_start.shape, F32)
    fracture = (fracture_start.shape, F32)
    side = ((3 * HALO + 2, depth, cols), F32)
    sides = ((2, HALO, depth, cols), F32)
    hot = pltpu.VMEM((cells, slots), BF16)
    columns = pltpu.VMEM((2 * LANES, cells), BF16)
    padded = (devices, LANES)
    first_message = ((devices, 4 + owned * blk // LANES, LANES), F32)
    message_type = ((devices, 4, LANES), F32)
    forward = [(i, i + 1) for i in range(devices - 1)]
    backward = [(target, source) for source, target in forward]

    def exchange(message):
        return lax.all_to_all(
            message,
            "area",
            split_axis=0,
            concat_axis=0,
            tiled=True,
            axis_index_groups=[group_order(devices)],
        )

    staged = [
        row_counts.reshape(1, 1),
        block_owner.reshape(-1, LANES),
        transfer_cells.reshape(-1, LANES),
        transfer_nodes.reshape(-1, LANES),
        transfer_weights.reshape(-1, LANES),
        matrix_start,
        fracture_start,
        matrix_source,
        matrix_storage,
    ]
    slot_rows = ((slots // LANES, LANES), F32)
    slot_columns = ((LANES, slots // LANES + -(slots // LANES) % 8), F32)
    dense = ((1, slots), F32)
    slot_index, slot_weight, slot_code, cell_rows, cell_columns, message, up, down = call(
        functools.partial(setup_kernel, devices, cap, len(staged)),
        [
            ((2, slots), jnp.int32),
            dense,
            (padded, jnp.int32),
            slot_rows,
            slot_columns,
            first_message,
            side,
            side,
        ],
        staged,
        "place_rows",
        5.0,
        hbm_in=range(len(staged)),
        hbm_out=(5, 6, 7),
        scratch=[pltpu.VMEM(x.shape, x.dtype) for x in staged]
        + [
            pltpu.VMEM(*first_message),
            pltpu.VMEM(*side),
            pltpu.VMEM(*side),
            hot,
            columns,
            pltpu.SemaphoreType.DMA((len(staged) + 3,)),
        ],
        limit=63 * 1024 * 1024,
    )
    arrived = exchange(message)
    low = lax.ppermute(up, "area", forward)
    high = lax.ppermute(down, "area", backward)
    scaled, inverse, row_inverse = call(
        diagonal_kernel,
        [grid, grid, dense],
        [matrix_source, matrix_storage, slot_index, slot_weight],
        "diagonal",
        2.0,
        scratch=[hot, columns],
    )
    partial, side_partial, side_scaled, side_inverse, row_partial, link_sum = call(
        functools.partial(first_window_kernel, relax[0]),
        [grid, sides, sides, sides, dense, fracture],
        [
            matrix_start,
            low,
            high,
            scaled,
            inverse,
            slot_index,
            slot_weight,
            fracture_start,
            fracture_links,
            link_weights,
        ],
        "stencil_first",
        2.0,
        scratch=[hot, columns],
    )
    message_scratch = [pltpu.VMEM(*message_type), pltpu.SemaphoreType.DMA]
    fracture_now, fracture_inverse, node_code, message = call(
        functools.partial(first_step_kernel, relax[0], cap),
        [fracture, fracture, (padded, jnp.int32), message_type],
        [
            arrived,
            slot_code,
            slot_weight,
            row_partial,
            row_inverse,
            cell_rows,
            cell_columns,
            fracture_start,
            link_sum,
            fracture_source,
            fracture_leak,
            link_weights,
        ],
        "couple_first",
        2.0,
        hbm_out=(3,),
        scratch=message_scratch,
    )
    for index in range(1, ITERS):
        last = index == ITERS - 1
        old, arrived = arrived, exchange(message)
        outs = call(
            functools.partial(window_kernel, relax[index], relax[index - 1], cap, index == 1, last),
            [grid, sides, fracture] + ([] if last else [dense]),
            [
                old,
                low,
                high,
                partial,
                scaled,
                inverse,
                side_partial,
                side_scaled,
                side_inverse,
                slot_index,
                slot_weight,
                slot_code,
                fracture_now,
                fracture_links,
                link_weights,
            ],
            "stencil",
            3.0,
            aliases={3: 0, 6: 1},
            scratch=[pltpu.VMEM(*grid), hot] + ([] if last else [columns]),
        )
        partial, side_partial, link_sum = outs[:3]
        fractures = [fracture_now, link_sum, fracture_source, fracture_inverse]
        if last:
            return call(
                functools.partial(last_step_kernel, relax[index], cap),
                [grid, fracture],
                [arrived, node_code, partial, inverse, slot_index, slot_weight] + fractures,
                "couple_last",
                2.0,
                scratch=[hot],
            )
        row_partial = outs[3]
        fracture_now, message = call(
            functools.partial(step_kernel, relax[index], cap),
            [fracture, message_type],
            [arrived, node_code, slot_weight, row_partial, row_inverse, cell_rows, cell_columns]
            + fractures,
            "couple",
            2.0,
            hbm_out=(1,),
            scratch=message_scratch,
        )


def solution(mesh):
    in_specs = (
        P(),
        P("area"),
        P("area"),
        P("area"),
        P("area"),
        P("real", "area", None),
        P("real", "area", None),
        P("real", "area", None),
        P("area", "real"),
        P("area", "real"),
        P("area", "real"),
        P(None, "area", None),
        P("real", "area", None),
    )
    out_specs = (P("real", "area", None), P("area", "real"))
    return jax.shard_map(local, mesh=mesh, in_specs=in_specs, out_specs=out_specs, check_vma=False)
```

```python
import functools
import math

import jax
import jax.numpy as jnp
from jax import lax
from jax.experimental import pallas as pl
from jax.experimental.pallas import tpu as pltpu
from jax.sharding import PartitionSpec as P

ITERS = 4
HALO = ITERS - 1
GRID_SLOTS = 72
LANES = 128
F32 = jnp.float32
BF16 = jnp.bfloat16
VMEM_LIMIT = 32 * 1024 * 1024


def relax_weights(steps_total):
    return [
        1.0 / (1.0 + 0.75 * math.cos(math.pi * (2 * index + 1) / (2 * steps_total)))
        for index in range(steps_total)
    ]


def log2(value):
    assert value & (value - 1) == 0
    return value.bit_length() - 1


def group_order(devices):
    part = devices // 4
    return [quarter * part + (i - 1) % part for quarter in (2, 0, 1, 3) for i in range(part)]


def iota(shape, dim):
    return lax.broadcasted_iota(jnp.int32, shape, dim)


def halves(x):
    high = x.astype(BF16)
    low = (x - high.astype(F32)).astype(BF16)
    return high, low


def matmul(a, b, contract):
    return lax.dot_general(a, b, ((contract[:1], contract[1:]), ((), ())), preferred_element_type=F32)


def to_dense(x, cap):
    return jnp.concatenate([x[i : i + 1, :cap] for i in range(x.shape[0])], axis=1)


def from_dense(x, devices, cap):
    rows = jnp.concatenate([x[:, i * cap : (i + 1) * cap] for i in range(devices)], axis=0)
    return jnp.concatenate([rows, jnp.zeros((devices, LANES - cap), x.dtype)], axis=1)


def lane_gather(table, index):
    return jnp.take_along_axis(table, index, axis=1, mode="promise_in_bounds")


def masked_parts(low, *values):
    mask = iota((LANES, low.shape[1]), 0) == low
    zero = jnp.zeros((), F32)
    parts = []
    for value in values:
        high = value.astype(BF16).astype(F32)
        parts.append(jnp.where(mask, high, zero).astype(BF16))
        parts.append(jnp.where(mask, value - high, zero).astype(BF16))
    return jnp.concatenate(parts, axis=0)


def fold(wide, index):
    start = 2 * index * LANES
    return wide[:, start : start + LANES] + wide[:, start + LANES : start + 2 * LANES]


def pick_low(tall, low):
    both = tall[:LANES] + tall[LANES:]
    return jnp.sum(
        jnp.where(iota(both.shape, 0) == low, both, 0.0), axis=0, keepdims=True
    )


def stack_lanes(x):
    return jnp.concatenate(
        [x[:, i * LANES : (i + 1) * LANES] for i in range(x.shape[1] // LANES)], axis=0
    )


def unstack_lanes(x, rows):
    return jnp.concatenate([x[i : i + rows] for i in range(0, x.shape[0], rows)], axis=1)


def put_columns(chunk, index, columns_ref):
    high, low = halves(chunk.T)
    columns_ref[:LANES, index * LANES : (index + 1) * LANES] = high
    columns_ref[LANES:, index * LANES : (index + 1) * LANES] = low


def fill_hot(hot_ref, high):
    for start in range(0, hot_ref.shape[0], LANES):
        rows = iota((LANES, high.shape[1]), 0) + start
        hot_ref[start : start + LANES, :] = (rows == high).astype(F32).astype(BF16)


def pick_entries(table, row, lane):
    found = jnp.zeros(row.shape, table.dtype)
    for i in range(table.shape[0]):
        values = jnp.broadcast_to(table[i : i + 1], row.shape)
        found = jnp.where(row == i, lane_gather(values, lane), found)
    return found


def setup_kernel(devices, cap, staged, *refs):
    sources, refs = refs[:staged], refs[staged:]
    rows_ref, slots_ref, message_hbm, pair_hbm, cross_hbm, grids_hbm = refs[:6]
    targets, refs = refs[6 : 6 + staged], refs[6 + staged :]
    message_ref, pair_ref, cross_ref, hot_ref, columns_ref, sems = refs
    copies = [
        pltpu.make_async_copy(sources[i], targets[i], sems.at[i]) for i in range(staged)
    ]
    kept = [
        pltpu.make_async_copy(targets[i], grids_hbm.at[j], sems.at[staged + 3 + j])
        for j, i in enumerate((5, 7, 8))
    ]
    for copy in copies:
        copy.start()
    for copy in copies[:5]:
        copy.wait()
    counts_ref, owner_ref, cells_ref, nodes_ref, weights_ref = targets[:5]
    matrix_ref, fracture_ref, source_ref, storage_ref = targets[5:]
    owned, blk = fracture_ref.shape
    depth, area_rows, cols = matrix_ref.shape
    groups = cells_ref.shape[0]
    plane_rows = depth * area_rows
    shape = (groups, LANES)
    nodes, cells = nodes_ref[...], cells_ref[...]
    live = iota(shape, 0) * LANES + iota(shape, 1) < counts_ref[...]
    weight = jnp.where(live, weights_ref[...], 0.0)
    block = nodes >> log2(blk)
    slot = jnp.zeros(shape, jnp.int32)
    for part in range(owner_ref.shape[0]):
        table = jnp.broadcast_to(owner_ref[part : part + 1, :], shape)
        found = lane_gather(table, block & (LANES - 1))
        slot = jnp.where(block >> log2(LANES) == part, found, slot)
    device = slot >> log2(owned)
    target = jnp.zeros(shape, jnp.int32)
    for position, place in enumerate(group_order(devices)):
        target = jnp.where(device == place, position, target)
    target = jnp.where(live, target, -1)
    node_high = ((nodes & (blk - 1)) >> log2(LANES)) * owned + (slot & (owned - 1))
    node_low = nodes & (LANES - 1)
    plane_row = cells >> log2(cols)
    cell_group = (cells & (cols - 1)) >> log2(LANES)
    cell_high = cell_group * plane_rows + plane_row
    cell_low = cells & (LANES - 1)
    high, low = unstack_lanes(cell_high, 1), unstack_lanes(cell_low, 1)
    row_weight = unstack_lanes(weight, 1)
    fill_hot(hot_ref, high)

    device_rows = iota((devices, LANES), 0)
    member = [(device_rows == target[q : q + 1]).astype(F32) for q in range(groups)]
    earlier = (iota((LANES, LANES), 0) < iota((LANES, LANES), 1)).astype(F32).astype(BF16)
    counted = matmul(jnp.concatenate(member, axis=0).astype(BF16), earlier, (1, 0))
    before = jnp.zeros((devices, 1), F32)
    rank = []
    for q in range(groups):
        inside = counted[q * devices : (q + 1) * devices] + before
        rank.append(jnp.sum(member[q] * inside, axis=0, keepdims=True).astype(jnp.int32))
        before = before + jnp.sum(member[q], axis=1, keepdims=True)
    rank_row = jnp.concatenate(rank, axis=1)
    rank = jnp.concatenate(rank, axis=0)
    member = jnp.concatenate(member, axis=1)

    first = weight.astype(BF16).astype(F32)
    second = (weight - first).astype(BF16).astype(F32)
    features = [
        jnp.ones(shape, F32),
        node_high.astype(F32),
        node_low.astype(F32),
        first,
        second,
        weight - first - second,
        iota(shape, 0).astype(F32),
        iota(shape, 1).astype(F32),
    ]
    features = [member * unstack_lanes(x, 1) for x in features]
    ranked = (iota((LANES, groups * LANES), 0) == rank_row).astype(F32).astype(BF16)
    packed = matmul(jnp.concatenate(features, axis=0).astype(BF16), ranked, (1, 1))
    packed = [packed[i * devices : (i + 1) * devices] for i in range(len(features))]
    code = jnp.where(packed[0] > 0.5, packed[1] * LANES + packed[2], -1.0)
    slot_row, slot_lane = packed[6].astype(jnp.int32), packed[7].astype(jnp.int32)
    slots_ref[0], slots_ref[1], slots_ref[2] = packed[6], packed[7], code
    for i, x in enumerate((weight, target, rank, cells, cell_high, cell_low)):
        rows_ref[i] = x.astype(F32)
    message_ref[:, 0, :] = code
    message_ref[:, 1, :] = packed[3] + packed[4] + packed[5]
    message_ref[:, 3, :] = jnp.zeros((devices, LANES), F32)

    odd = (lax.axis_index("area") & 1) == 1
    plane = plane_row >> log2(area_rows)
    row = plane_row & (area_rows - 1)
    places = []
    for far in (area_rows - 1 - row, row):
        place = (cell_group * HALO + far) * depth + plane
        places.append(jnp.where(live & (far < HALO), place, -1).astype(F32))
    info = [low, row_weight, unstack_lanes(target, 1), unstack_lanes(rank, 1)]
    info = [x.astype(F32) for x in info]
    dense = to_dense(code, cap)
    half = dense.shape[1] // 2
    for ref, place in (
        (pair_ref, jnp.where(odd, places[1], places[0])),
        (cross_ref, jnp.where(odd, places[0], places[1])),
    ):
        tile = ref.at[3 * HALO + 1]
        for i, x in enumerate([unstack_lanes(place, 1)] + info):
            tile[i : i + 1, :] = x
        tile[5:6, :half] = dense[:, :half]
        tile[6:7, :half] = dense[:, half:]

    for copy in copies[5:]:
        copy.wait()
    for copy in kept:
        copy.start()
    node_table = stack_lanes(fracture_ref[...])
    message_ref[:, 4:, :] = jnp.broadcast_to(node_table[None], (devices,) + node_table.shape)
    for ref, start, count in (
        (matrix_ref, 0, HALO + 1),
        (source_ref, HALO + 1, HALO),
        (storage_ref, 2 * HALO + 1, HALO),
    ):
        for far in range(count):
            up = ref[:, area_rows - 1 - far, :]
            down = ref[:, far, :]
            pair_ref[start + far] = jnp.where(odd, down, up)
            cross_ref[start + far] = jnp.where(odd, up, down)
    outs = [
        pltpu.make_async_copy(pair_ref, pair_hbm, sems.at[staged]),
        pltpu.make_async_copy(cross_ref, cross_hbm, sems.at[staged + 1]),
        pltpu.make_async_copy(message_ref, message_hbm, sems.at[staged + 2]),
    ]
    outs[0].start()
    outs[1].start()
    picked = stack_lanes(pick_cells(matrix_ref, columns_ref, hot_ref, low))
    message_ref[:, 2, :] = pick_entries(weight * picked, slot_row, slot_lane)
    outs[2].start()
    for out in outs + kept:
        out.wait()


def turned(rows):
    count = rows.shape[0]
    extra = -count % 8
    if extra:
        rows = jnp.concatenate([rows, jnp.zeros((extra, LANES), rows.dtype)], axis=0)
    return rows.T


def same_cell_sum(values, cell_rows, cell_columns):
    value_columns = turned(values)
    blocks = cell_rows.shape[0]
    sums = [jnp.zeros((8, LANES), F32) for _ in range(blocks)]
    for j in range(blocks):
        cell = jnp.broadcast_to(cell_columns[:, j : j + 1], (LANES, LANES))
        value = jnp.broadcast_to(value_columns[:, j : j + 1], (LANES, LANES))
        for i in range(blocks):
            hit = jnp.where(cell == cell_rows[i : i + 1], value, 0.0)
            sums[i] = sums[i] + jnp.sum(hit.reshape(LANES // 8, 8, LANES), axis=0)
    return jnp.concatenate([jnp.sum(x, axis=0, keepdims=True) for x in sums], axis=0)


def relaxed(now, source, inverse, low_side, high_side, relaxation):
    depth, rows, cols = now.shape
    zero_plane = jnp.zeros((1, rows, cols), F32)
    beside = jnp.concatenate([now[1:], zero_plane], axis=0)
    beside = beside + jnp.concatenate([zero_plane, now[:-1]], axis=0)
    beside = beside + jnp.concatenate([now[:, 1:], high_side[:, None]], axis=1)
    beside = beside + jnp.concatenate([low_side[:, None], now[:, :-1]], axis=1)
    flat = now.reshape(depth * rows, cols)
    place = iota(flat.shape, 1)
    left = jnp.where(place == 0, 0.0, pltpu.roll(flat, 1, 1))
    right = jnp.where(place == cols - 1, 0.0, pltpu.roll(flat, cols - 1, 1))
    beside = beside + (left + right).reshape(now.shape)
    return (1.0 - relaxation) * now + relaxation * (source + inverse * beside)


def linked(fracture, links_ref, link_weights_ref):
    total = jnp.zeros(fracture.shape, F32)
    width = fracture.shape[1]
    tables = [fracture[:, i : i + LANES] for i in range(0, width, LANES)]
    sums = []
    for start in range(0, width, LANES):
        total = jnp.zeros(tables[0].shape, F32)
        for j in range(links_ref.shape[0]):
            link = links_ref[j, :, start : start + LANES]
            found = jnp.zeros(tables[0].shape, F32)
            for i, table in enumerate(tables):
                found = jnp.where(
                    link >> log2(LANES) == i, lane_gather(table, link & (LANES - 1)), found
                )
            total = total + link_weights_ref[j, :, start : start + LANES] * found
        sums.append(total)
    return jnp.concatenate(sums, axis=1)


def relaxed_side(now, beyond, edge, scaled, inverse, relaxation):
    depth, cols = edge.shape
    place = iota(edge.shape, 1)
    zero_plane = jnp.zeros((1, cols), F32)
    after = []
    for far in range(HALO):
        here = now[far]
        beside = jnp.concatenate([here[1:], zero_plane], axis=0)
        beside = beside + jnp.concatenate([zero_plane, here[:-1]], axis=0)
        beside = beside + jnp.where(place == 0, 0.0, pltpu.roll(here, 1, 1))
        beside = beside + jnp.where(place == cols - 1, 0.0, pltpu.roll(here, cols - 1, 1))
        beside = beside + (edge if far == 0 else now[far - 1])
        if far + 1 < HALO:
            beside = beside + now[far + 1]
        elif beyond is not None:
            beside = beside + beyond
        after.append(
            (1.0 - relaxation) * here + relaxation * (scaled[far] + inverse[far] * beside)
        )
    return after


def spread_side(place, low, values, depth, col_groups):
    rows = iota((col_groups * HALO * depth, place.shape[1]), 0)
    hot = (rows == place).astype(F32).astype(BF16)
    added = fold(matmul(hot, masked_parts(low, values), (1, 1)), 0)
    return [
        jnp.concatenate(
            [
                added[(group * HALO + far) * depth : (group * HALO + far + 1) * depth]
                for group in range(col_groups)
            ],
            axis=1,
        )
        for far in range(HALO)
    ]


def pick_cells(table_ref, columns_ref, hot_ref, low):
    depth, area_rows, cols = table_ref.shape
    for c in range(cols // LANES):
        chunk = table_ref[:, :, c * LANES : (c + 1) * LANES]
        put_columns(chunk.reshape(depth * area_rows, LANES), c, columns_ref)
    return pick_low(matmul(columns_ref[...], hot_ref[...], (1, 0)), low)


def side_kernel_inputs(info_ref, side):
    rows = [info_ref[side, i : i + 1, :] for i in range(5)]
    whole = [x.astype(jnp.int32) for x in rows]
    return whole[0], whole[1], rows[2], whole[3], whole[4]


def row_integer(rows_ref, index):
    return rows_ref[index].astype(jnp.int32)


def row_cells(rows_ref):
    return [unstack_lanes(row_integer(rows_ref, index), 1) for index in (4, 5)]


def diagonal_kernel(
    grids_hbm,
    rows_ref,
    matrix_ref,
    scaled_ref,
    inverse_ref,
    row_inverse_ref,
    source_ref,
    storage_ref,
    hot_ref,
    columns_ref,
    sems,
):
    copies = [
        pltpu.make_async_copy(grids_hbm.at[1], source_ref, sems.at[0]),
        pltpu.make_async_copy(grids_hbm.at[2], storage_ref, sems.at[1]),
    ]
    matrix_copy = pltpu.make_async_copy(grids_hbm.at[0], matrix_ref, sems.at[2])
    for copy in copies + [matrix_copy]:
        copy.start()
    depth, area_rows, cols = source_ref.shape
    plane_rows = depth * area_rows
    high, low = row_cells(rows_ref)
    weight = rows_ref[0]
    fill_hot(hot_ref, high)
    added = fold(matmul(hot_ref[...], masked_parts(low, unstack_lanes(weight, 1)), (1, 1)), 0)
    for copy in copies:
        copy.wait()
    for c in range(cols // LANES):
        lanes = slice(c * LANES, (c + 1) * LANES)
        extra = added[c * plane_rows : (c + 1) * plane_rows].reshape(depth, area_rows, LANES)
        inverse = 1.0 / (6.0 + storage_ref[:, :, lanes] + extra)
        scaled_ref[:, :, lanes] = source_ref[:, :, lanes] * inverse
        inverse_ref[:, :, lanes] = inverse
    row_inverse_ref[...] = weight * stack_lanes(
        pick_cells(inverse_ref, columns_ref, hot_ref, low)
    )
    matrix_copy.wait()


def first_window_kernel(
    relaxation,
    matrix_ref,
    scaled_ref,
    inverse_ref,
    pair_ref,
    cross_ref,
    rows_ref,
    fracture_ref,
    links_ref,
    link_weights_ref,
    partial_ref,
    side_partial_ref,
    side_scaled_ref,
    side_inverse_ref,
    side_info_ref,
    row_partial_ref,
    link_sum_ref,
    hot_ref,
    columns_ref,
):
    depth, area_rows, cols = matrix_ref.shape
    high, low = row_cells(rows_ref)
    fill_hot(hot_ref, high)
    odd = (lax.axis_index("area") & 1) == 1
    tiles = pair_ref.shape[0]
    lower = [jnp.where(odd, pair_ref[i], cross_ref[i]) for i in range(tiles)]
    upper = [jnp.where(odd, cross_ref[i], pair_ref[i]) for i in range(tiles)]
    whole = matrix_ref[...]
    partial_ref[...] = relaxed(
        whole,
        scaled_ref[...],
        inverse_ref[...],
        lower[0],
        upper[0],
        relaxation,
    )
    row_partial_ref[...] = rows_ref[0] * stack_lanes(
        pick_cells(partial_ref, columns_ref, hot_ref, low)
    )
    for side, (tiles, edge) in enumerate(((lower, 0), (upper, area_rows - 1))):
        side_info_ref[side] = tiles[3 * HALO + 1]
        place, side_low, side_weight, _, _ = side_kernel_inputs(side_info_ref, side)
        added = spread_side(place, side_low, side_weight, depth, cols // LANES)
        for far in range(HALO):
            storage = tiles[2 * HALO + 1 + far]
            inverse = jnp.where(storage > 0.0, 1.0 / (6.0 + storage + added[far]), 0.0)
            side_inverse_ref[side, far] = inverse
            side_scaled_ref[side, far] = tiles[HALO + 1 + far] * inverse
        after = relaxed_side(
            tiles[:HALO],
            tiles[HALO],
            whole[:, edge, :],
            [side_scaled_ref[side, far] for far in range(HALO)],
            [side_inverse_ref[side, far] for far in range(HALO)],
            relaxation,
        )
        for far in range(HALO):
            side_partial_ref[side, far] = after[far]
    link_sum_ref[...] = linked(fracture_ref[...], links_ref, link_weights_ref)


def add_rows(relaxation, values, partial_ref, inverse_ref, rows_ref, hot_ref, matrix_ref):
    depth, area_rows, cols = partial_ref.shape
    plane_rows = depth * area_rows
    high, low = row_cells(rows_ref)
    fill_hot(hot_ref, high)
    parts = masked_parts(low, unstack_lanes(values, 1))
    added = fold(matmul(hot_ref[...], parts, (1, 1)), 0)
    for c in range(cols // LANES):
        lanes = slice(c * LANES, (c + 1) * LANES)
        extra = added[c * plane_rows : (c + 1) * plane_rows].reshape(depth, area_rows, LANES)
        matrix_ref[:, :, lanes] = (
            partial_ref[:, :, lanes] + (relaxation * inverse_ref[:, :, lanes]) * extra
        )


def returned_values(returned, rows_ref):
    target, rank = row_integer(rows_ref, 1), row_integer(rows_ref, 2)
    return rows_ref[0] * pick_entries(returned, target, rank)


def window_kernel(
    relaxation,
    before,
    cap,
    first,
    last,
    arrived_ref,
    partial_before_ref,
    scaled_ref,
    inverse_ref,
    side_before_ref,
    side_scaled_ref,
    side_inverse_ref,
    side_info_ref,
    rows_ref,
    slots_ref,
    fracture_ref,
    links_ref,
    link_weights_ref,
    partial_ref,
    side_partial_ref,
    link_sum_ref,
    *refs,
):
    if last:
        matrix_ref, hot_ref = refs
    else:
        row_partial_ref, matrix_ref, hot_ref, columns_ref = refs
    depth, area_rows, cols = scaled_ref.shape
    devices = arrived_ref.shape[0]
    half = devices * cap // 2
    returned = device_values(arrived_ref, row_integer(slots_ref, 2)) if first else arrived_ref[:, 1, :]
    values = returned_values(returned, rows_ref)
    add_rows(before, values, partial_before_ref, inverse_ref, rows_ref, hot_ref, matrix_ref)
    edges = []
    for side, edge in enumerate((0, area_rows - 1)):
        place, low, weight, target, rank = side_kernel_inputs(side_info_ref, side)
        if first:
            code = jnp.concatenate(
                [side_info_ref[side, i : i + 1, :half] for i in (5, 6)], axis=1
            )
            code = from_dense(code, devices, cap).astype(jnp.int32)
            returned = device_values(arrived_ref, code)
        else:
            returned = arrived_ref[:, 2 + side, :]
        values = pick_entries(returned, stack_lanes(target), stack_lanes(rank))
        values = weight * unstack_lanes(values, 1)
        added = spread_side(place, low, values, depth, cols // LANES)
        now = [
            side_before_ref[side, far] + before * side_inverse_ref[side, far] * added[far]
            for far in range(HALO)
        ]
        edges.append(now[0])
        after = relaxed_side(
            now,
            None,
            matrix_ref[:, edge, :],
            [side_scaled_ref[side, far] for far in range(HALO)],
            [side_inverse_ref[side, far] for far in range(HALO)],
            relaxation,
        )
        for far in range(HALO):
            side_partial_ref[side, far] = after[far]
    partial_ref[...] = relaxed(
        matrix_ref[...],
        scaled_ref[...],
        inverse_ref[...],
        edges[0],
        edges[1],
        relaxation,
    )
    if not last:
        row_partial_ref[...] = rows_ref[0] * stack_lanes(
            pick_cells(partial_ref, columns_ref, hot_ref, row_cells(rows_ref)[1])
        )
    link_sum_ref[...] = linked(fracture_ref[...], links_ref, link_weights_ref)


def row_values(relaxation, returned, slots_ref, rows_ref, row_partial_ref, row_inverse_ref):
    cells = rows_ref[3]
    total = same_cell_sum(returned_values(returned, rows_ref), cells, turned(cells))
    outgoing = row_partial_ref[...] + (relaxation * row_inverse_ref[...]) * total
    return pick_entries(outgoing, row_integer(slots_ref, 0), row_integer(slots_ref, 1))


def node_hot(code, rows):
    return (iota((rows, code.shape[1]), 0) == code >> log2(LANES)).astype(F32).astype(BF16)


def node_values(table, code):
    found = jnp.zeros(code.shape, F32)
    low = code & (LANES - 1)
    for row in range(table.shape[0]):
        values = jnp.broadcast_to(table[row : row + 1], code.shape)
        found = jnp.where(code >> log2(LANES) == row, lane_gather(values, low), found)
    return found


def device_values(arrived_ref, code):
    found = jnp.zeros(code.shape, F32)
    low = code & (LANES - 1)
    for row in range(arrived_ref.shape[1] - 4):
        values = lane_gather(arrived_ref[:, 4 + row, :], low)
        found = jnp.where(code >> log2(LANES) == row, values, found)
    return found


def put_requested(message_ref, values):
    zero = jnp.zeros((1, LANES), F32)
    order = group_order(values.shape[0])
    rows = {device: values[i : i + 1] for i, device in enumerate(order)}
    message_ref[:, 1, :] = values
    for place, step in ((2, -1), (3, 1)):
        message_ref[:, place, :] = jnp.concatenate(
            [rows.get(device + step, zero) for device in order], axis=0
        )


def first_step_kernel(
    relaxation,
    cap,
    arrived_ref,
    slots_ref,
    rows_ref,
    row_partial_ref,
    row_inverse_ref,
    fracture_ref,
    link_sum_ref,
    fracture_source_ref,
    leak_ref,
    link_weights_ref,
    fracture_next_ref,
    fracture_inverse_ref,
    node_code_ref,
    message_hbm,
    message_ref,
    sem,
):
    owned = fracture_ref.shape[0]
    message_ref[:, 0, :] = row_values(
        relaxation,
        device_values(arrived_ref, row_integer(slots_ref, 2)),
        slots_ref,
        rows_ref,
        row_partial_ref,
        row_inverse_ref,
    )
    code = arrived_ref[:, 0, :].astype(jnp.int32)
    node_code_ref[...] = code
    dense = to_dense(code, cap)
    parts = masked_parts(
        dense & (LANES - 1),
        to_dense(arrived_ref[:, 1, :], cap),
        to_dense(arrived_ref[:, 2, :], cap),
    )
    sums = matmul(node_hot(dense, fracture_ref.shape[0] * fracture_ref.shape[1] // LANES), parts, (1, 1))
    diag = (
        leak_ref[...] + jnp.sum(link_weights_ref[...], axis=0) + unstack_lanes(fold(sums, 0), owned)
    )
    inverse = 1.0 / diag
    fracture_inverse_ref[...] = inverse
    fracture_next = (1.0 - relaxation) * fracture_ref[...] + (relaxation * inverse) * (
        fracture_source_ref[...] + link_sum_ref[...] + unstack_lanes(fold(sums, 1), owned)
    )
    fracture_next_ref[...] = fracture_next
    put_requested(message_ref, node_values(stack_lanes(fracture_next), code))
    out = pltpu.make_async_copy(message_ref, message_hbm, sem)
    out.start()
    out.wait()


def next_fracture(
    relaxation,
    cap,
    arrived_ref,
    code,
    fracture_ref,
    link_sum_ref,
    fracture_source_ref,
    fracture_inverse_ref,
):
    owned, blk = fracture_ref.shape
    dense = to_dense(code, cap)
    parts = masked_parts(dense & (LANES - 1), to_dense(arrived_ref[:, 0, :], cap))
    sums = matmul(node_hot(dense, owned * blk // LANES), parts, (1, 1))
    return (1.0 - relaxation) * fracture_ref[...] + (relaxation * fracture_inverse_ref[...]) * (
        fracture_source_ref[...] + link_sum_ref[...] + unstack_lanes(fold(sums, 0), owned)
    )


def step_kernel(
    relaxation,
    cap,
    arrived_ref,
    node_code_ref,
    slots_ref,
    rows_ref,
    row_partial_ref,
    row_inverse_ref,
    fracture_ref,
    link_sum_ref,
    fracture_source_ref,
    fracture_inverse_ref,
    fracture_next_ref,
    message_hbm,
    message_ref,
    sem,
):
    message_ref[:, 0, :] = row_values(
        relaxation,
        arrived_ref[:, 1, :],
        slots_ref,
        rows_ref,
        row_partial_ref,
        row_inverse_ref,
    )
    code = node_code_ref[...]
    fracture_next = next_fracture(
        relaxation,
        cap,
        arrived_ref,
        code,
        fracture_ref,
        link_sum_ref,
        fracture_source_ref,
        fracture_inverse_ref,
    )
    fracture_next_ref[...] = fracture_next
    put_requested(message_ref, node_values(stack_lanes(fracture_next), code))
    out = pltpu.make_async_copy(message_ref, message_hbm, sem)
    out.start()
    out.wait()


def last_step_kernel(
    relaxation,
    cap,
    arrived_ref,
    node_code_ref,
    partial_ref,
    inverse_ref,
    rows_ref,
    fracture_ref,
    link_sum_ref,
    fracture_source_ref,
    fracture_inverse_ref,
    matrix_ref,
    fracture_next_ref,
    hot_ref,
):
    values = returned_values(arrived_ref[:, 1, :], rows_ref)
    add_rows(relaxation, values, partial_ref, inverse_ref, rows_ref, hot_ref, matrix_ref)
    fracture_next_ref[...] = next_fracture(
        relaxation,
        cap,
        arrived_ref,
        node_code_ref[...],
        fracture_ref,
        link_sum_ref,
        fracture_source_ref,
        fracture_inverse_ref,
    )


def call(kernel, outs, ins, name, micros, hbm_in=(), hbm_out=(), scratch=(), aliases=None, limit=VMEM_LIMIT):
    return pl.pallas_call(
        kernel,
        out_shape=[jax.ShapeDtypeStruct(shape, dtype) for shape, dtype in outs],
        in_specs=[
            pl.BlockSpec(memory_space=pltpu.HBM if i in hbm_in else pltpu.VMEM)
            for i in range(len(ins))
        ],
        out_specs=[
            pl.BlockSpec(memory_space=pltpu.HBM if i in hbm_out else pltpu.VMEM)
            for i in range(len(outs))
        ],
        scratch_shapes=list(scratch),
        input_output_aliases=aliases or {},
        compiler_params=pltpu.CompilerParams(vmem_limit_bytes=limit),
        cost_estimate=pl.CostEstimate(
            flops=0, bytes_accessed=int(micros * 3.0e6), transcendentals=0
        ),
        name=name,
    )(*ins)


def local(
    block_owner,
    transfer_cells,
    transfer_nodes,
    transfer_weights,
    row_counts,
    matrix_start,
    matrix_source,
    matrix_storage,
    fracture_start,
    fracture_source,
    fracture_leak,
    fracture_links,
    link_weights,
):
    devices = lax.axis_size("area")
    depth, area_rows, cols = matrix_start.shape
    owned, blk = fracture_start.shape
    total_rows = transfer_cells.shape[0]
    cap = 3 * total_rows // (2 * devices)
    cells = depth * area_rows * cols // LANES
    relax = relax_weights(ITERS)
    grid = (matrix_start.shape, F32)
    grids = ((GRID_SLOTS,) + matrix_start.shape, F32)
    fracture = (fracture_start.shape, F32)
    side = ((3 * HALO + 2, depth, cols), F32)
    sides = ((2, HALO, depth, cols), F32)
    hot = pltpu.VMEM((cells, total_rows), BF16)
    columns = pltpu.VMEM((2 * LANES, cells), BF16)
    padded = (devices, LANES)
    first_message = ((devices, 4 + owned * blk // LANES, LANES), F32)
    message_type = ((devices, 4, LANES), F32)
    pairs, crossings = [
        [(i + a, i + b) for i in range(start, devices - 1, 2) for a, b in ((0, 1), (1, 0))]
        for start in (0, 1)
    ]

    def exchange(message):
        return lax.all_to_all(
            message,
            "area",
            split_axis=0,
            concat_axis=0,
            tiled=True,
            axis_index_groups=[group_order(devices)],
        )

    staged = [
        row_counts.reshape(1, 1),
        block_owner.reshape(-1, LANES),
        transfer_cells.reshape(-1, LANES),
        transfer_nodes.reshape(-1, LANES),
        transfer_weights.reshape(-1, LANES),
        matrix_start,
        fracture_start,
        matrix_source,
        matrix_storage,
    ]
    row_shape = (total_rows // LANES, LANES)
    rows = (row_shape, F32)
    row_info, slot_info, message, pair, cross, grids_start = call(
        functools.partial(setup_kernel, devices, cap, len(staged)),
        [((6,) + row_shape, F32), ((3,) + padded, F32), first_message, side, side, grids],
        staged,
        "place_rows",
        5.0,
        hbm_in=range(len(staged)),
        hbm_out=(2, 3, 4, 5),
        scratch=[pltpu.VMEM(x.shape, x.dtype) for x in staged]
        + [
            pltpu.VMEM(*first_message),
            pltpu.VMEM(*side),
            pltpu.VMEM(*side),
            hot,
            columns,
            pltpu.SemaphoreType.DMA((len(staged) + 6,)),
        ],
        limit=63 * 1024 * 1024,
    )
    arrived = exchange(message)
    pair = lax.ppermute(pair, "area", pairs)
    cross = lax.ppermute(cross, "area", crossings)
    matrix, scaled, inverse, row_inverse = call(
        diagonal_kernel,
        [grid, grid, grid, rows],
        [grids_start, row_info],
        "diagonal",
        2.0,
        hbm_in=(0,),
        scratch=[pltpu.VMEM(*grid)] * 2 + [hot, columns, pltpu.SemaphoreType.DMA((3,))],
    )
    partial, side_partial, side_scaled, side_inverse, side_info, row_partial, link_sum = call(
        functools.partial(first_window_kernel, relax[0]),
        [grid, sides, sides, sides, ((2, depth, cols), F32), rows, fracture],
        [
            matrix,
            scaled,
            inverse,
            pair,
            cross,
            row_info,
            fracture_start,
            fracture_links,
            link_weights,
        ],
        "stencil_first",
        2.0,
        scratch=[hot, columns],
    )
    fracture_now = fracture_start
    message_scratch = [pltpu.VMEM(*message_type), pltpu.SemaphoreType.DMA]
    fracture_now, fracture_inverse, node_code, message = call(
        functools.partial(first_step_kernel, relax[0], cap),
        [fracture, fracture, (padded, jnp.int32), message_type],
        [
            arrived,
            slot_info,
            row_info,
            row_partial,
            row_inverse,
            fracture_now,
            link_sum,
            fracture_source,
            fracture_leak,
            link_weights,
        ],
        "couple_first",
        2.0,
        hbm_out=(3,),
        scratch=message_scratch,
    )
    for index in range(1, ITERS):
        last = index == ITERS - 1
        old, arrived = arrived, exchange(message)
        outs = call(
            functools.partial(window_kernel, relax[index], relax[index - 1], cap, index == 1, last),
            [grid, sides, fracture] + ([] if last else [rows]),
            [
                old,
                partial,
                scaled,
                inverse,
                side_partial,
                side_scaled,
                side_inverse,
                side_info,
                row_info,
                slot_info,
                fracture_now,
                fracture_links,
                link_weights,
            ],
            "stencil",
            3.0,
            aliases={1: 0, 4: 1},
            scratch=[pltpu.VMEM(*grid), hot] + ([] if last else [columns]),
        )
        partial, side_partial, link_sum = outs[:3]
        fractures = [fracture_now, link_sum, fracture_source, fracture_inverse]
        if last:
            return call(
                functools.partial(last_step_kernel, relax[index], cap),
                [grid, fracture],
                [arrived, node_code, partial, inverse, row_info] + fractures,
                "couple_last",
                2.0,
                scratch=[hot],
            )
        row_partial = outs[3]
        fracture_now, message = call(
            functools.partial(step_kernel, relax[index], cap),
            [fracture, message_type],
            [arrived, node_code, slot_info, row_info, row_partial, row_inverse] + fractures,
            "couple",
            2.0,
            hbm_out=(1,),
            scratch=message_scratch,
        )


def solution(mesh):
    in_specs = (
        P(),
        P("area"),
        P("area"),
        P("area"),
        P("area"),
        P("real", "area", None),
        P("real", "area", None),
        P("real", "area", None),
        P("area", "real"),
        P("area", "real"),
        P("area", "real"),
        P(None, "area", None),
        P("real", "area", None),
    )
    out_specs = (P("real", "area", None), P("area", "real"))
    return jax.shard_map(local, mesh=mesh, in_specs=in_specs, out_specs=out_specs, check_vma=False)
```

```python
import functools
import math

import jax
import jax.numpy as jnp
from jax import lax
from jax.experimental import pallas as pl
from jax.experimental.pallas import tpu as pltpu
from jax.sharding import PartitionSpec as P

ITERS = 4
HALO = ITERS - 1
GRID_SLOTS = 72
LANES = 128
F32 = jnp.float32
BF16 = jnp.bfloat16
VMEM_LIMIT = 32 * 1024 * 1024


def relax_weights(steps_total):
    return [
        1.0 / (1.0 + 0.75 * math.cos(math.pi * (2 * index + 1) / (2 * steps_total)))
        for index in range(steps_total)
    ]


def log2(value):
    assert value & (value - 1) == 0
    return value.bit_length() - 1


def group_order(devices):
    part = devices // 4
    return [quarter * part + (i - 1) % part for quarter in (2, 0, 1, 3) for i in range(part)]


def iota(shape, dim):
    return lax.broadcasted_iota(jnp.int32, shape, dim)


def halves(x):
    high = x.astype(BF16)
    low = (x - high.astype(F32)).astype(BF16)
    return high, low


def matmul(a, b, contract):
    return lax.dot_general(a, b, ((contract[:1], contract[1:]), ((), ())), preferred_element_type=F32)


def to_dense(x, cap):
    return jnp.concatenate([x[i : i + 1, :cap] for i in range(x.shape[0])], axis=1)


def from_dense(x, devices, cap):
    rows = jnp.concatenate([x[:, i * cap : (i + 1) * cap] for i in range(devices)], axis=0)
    return jnp.concatenate([rows, jnp.zeros((devices, LANES - cap), x.dtype)], axis=1)


def lane_gather(table, index):
    return jnp.take_along_axis(table, index, axis=1, mode="promise_in_bounds")


def masked_parts(low, *values):
    mask = iota((LANES, low.shape[1]), 0) == low
    zero = jnp.zeros((), F32)
    parts = []
    for value in values:
        high = value.astype(BF16).astype(F32)
        parts.append(jnp.where(mask, high, zero).astype(BF16))
        parts.append(jnp.where(mask, value - high, zero).astype(BF16))
    return jnp.concatenate(parts, axis=0)


def fold(wide, index):
    start = 2 * index * LANES
    return wide[:, start : start + LANES] + wide[:, start + LANES : start + 2 * LANES]


def pick_low(tall, low):
    both = tall[:LANES] + tall[LANES:]
    return jnp.sum(
        jnp.where(iota(both.shape, 0) == low, both, 0.0), axis=0, keepdims=True
    )


def stack_lanes(x):
    return jnp.concatenate(
        [x[:, i * LANES : (i + 1) * LANES] for i in range(x.shape[1] // LANES)], axis=0
    )


def unstack_lanes(x, rows):
    return jnp.concatenate([x[i : i + rows] for i in range(0, x.shape[0], rows)], axis=1)


def put_columns(chunk, index, columns_ref):
    high, low = halves(chunk.T)
    columns_ref[:LANES, index * LANES : (index + 1) * LANES] = high
    columns_ref[LANES:, index * LANES : (index + 1) * LANES] = low


def fill_hot(hot_ref, high):
    for start in range(0, hot_ref.shape[0], LANES):
        rows = iota((LANES, high.shape[1]), 0) + start
        hot_ref[start : start + LANES, :] = (rows == high).astype(F32).astype(BF16)


def pick_entries(table, row, lane):
    found = jnp.zeros(row.shape, table.dtype)
    for i in range(table.shape[0]):
        values = jnp.broadcast_to(table[i : i + 1], row.shape)
        found = jnp.where(row == i, lane_gather(values, lane), found)
    return found


def row_slice(grids_hbm, rows_ref):
    count, groups, lanes = rows_ref.shape
    return grids_hbm.at[3, :count, :groups, :lanes]


def setup_kernel(devices, cap, staged, *refs):
    sources, refs = refs[:staged], refs[staged:]
    slots_ref, message_hbm, pair_hbm, cross_hbm, grids_hbm, link_sum_ref = refs[:6]
    targets, refs = refs[6 : 6 + staged], refs[6 + staged :]
    rows_ref, message_ref, pair_ref, cross_ref, hot_ref, columns_ref, sems = refs
    copies = [
        pltpu.make_async_copy(sources[i], targets[i], sems.at[i]) for i in range(staged)
    ]
    kept = [
        pltpu.make_async_copy(targets[i], grids_hbm.at[j], sems.at[staged + 3 + j])
        for j, i in enumerate((5, 7, 8))
    ]
    kept.append(pltpu.make_async_copy(rows_ref, row_slice(grids_hbm, rows_ref), sems.at[staged + 6]))
    for copy in copies:
        copy.start()
    for copy in copies[:5]:
        copy.wait()
    counts_ref, owner_ref, cells_ref, nodes_ref, weights_ref = targets[:5]
    matrix_ref, fracture_ref, source_ref, storage_ref, links_ref, link_weights_ref = targets[5:]
    owned, blk = fracture_ref.shape
    depth, area_rows, cols = matrix_ref.shape
    groups = cells_ref.shape[0]
    plane_rows = depth * area_rows
    shape = (groups, LANES)
    nodes, cells = nodes_ref[...], cells_ref[...]
    live = iota(shape, 0) * LANES + iota(shape, 1) < counts_ref[...]
    weight = jnp.where(live, weights_ref[...], 0.0)
    block = nodes >> log2(blk)
    slot = jnp.zeros(shape, jnp.int32)
    for part in range(owner_ref.shape[0]):
        table = jnp.broadcast_to(owner_ref[part : part + 1, :], shape)
        found = lane_gather(table, block & (LANES - 1))
        slot = jnp.where(block >> log2(LANES) == part, found, slot)
    device = slot >> log2(owned)
    target = jnp.zeros(shape, jnp.int32)
    for position, place in enumerate(group_order(devices)):
        target = jnp.where(device == place, position, target)
    target = jnp.where(live, target, -1)
    node_high = ((nodes & (blk - 1)) >> log2(LANES)) * owned + (slot & (owned - 1))
    node_low = nodes & (LANES - 1)
    plane_row = cells >> log2(cols)
    cell_group = (cells & (cols - 1)) >> log2(LANES)
    cell_high = cell_group * plane_rows + plane_row
    cell_low = cells & (LANES - 1)
    high, low = unstack_lanes(cell_high, 1), unstack_lanes(cell_low, 1)
    row_weight = unstack_lanes(weight, 1)
    fill_hot(hot_ref, high)

    device_rows = iota((devices, LANES), 0)
    member = [(device_rows == target[q : q + 1]).astype(F32) for q in range(groups)]
    earlier = (iota((LANES, LANES), 0) < iota((LANES, LANES), 1)).astype(F32).astype(BF16)
    counted = matmul(jnp.concatenate(member, axis=0).astype(BF16), earlier, (1, 0))
    before = jnp.zeros((devices, 1), F32)
    rank = []
    for q in range(groups):
        inside = counted[q * devices : (q + 1) * devices] + before
        rank.append(jnp.sum(member[q] * inside, axis=0, keepdims=True).astype(jnp.int32))
        before = before + jnp.sum(member[q], axis=1, keepdims=True)
    rank_row = jnp.concatenate(rank, axis=1)
    rank = jnp.concatenate(rank, axis=0)
    member = jnp.concatenate(member, axis=1)

    first = weight.astype(BF16).astype(F32)
    second = (weight - first).astype(BF16).astype(F32)
    features = [
        jnp.ones(shape, F32),
        node_high.astype(F32),
        node_low.astype(F32),
        first,
        second,
        weight - first - second,
        iota(shape, 0).astype(F32),
        iota(shape, 1).astype(F32),
    ]
    features = [member * unstack_lanes(x, 1) for x in features]
    ranked = (iota((LANES, groups * LANES), 0) == rank_row).astype(F32).astype(BF16)
    packed = matmul(jnp.concatenate(features, axis=0).astype(BF16), ranked, (1, 1))
    packed = [packed[i * devices : (i + 1) * devices] for i in range(len(features))]
    code = jnp.where(packed[0] > 0.5, packed[1] * LANES + packed[2], -1.0)
    slot_row, slot_lane = packed[6].astype(jnp.int32), packed[7].astype(jnp.int32)
    slots_ref[0], slots_ref[1], slots_ref[2] = packed[6], packed[7], code
    for i, x in enumerate((weight, target, rank, cells, cell_high, cell_low)):
        rows_ref[i] = x.astype(F32)
    kept[3].start()
    message_ref[:, 0, 0, :] = code
    message_ref[:, 0, 1, :] = packed[3] + packed[4] + packed[5]
    message_ref[:, 0, 3, :] = jnp.zeros((devices, LANES), F32)

    odd = (lax.axis_index("area") & 1) == 1
    plane = plane_row >> log2(area_rows)
    row = plane_row & (area_rows - 1)
    places = []
    for far in (area_rows - 1 - row, row):
        place = (cell_group * HALO + far) * depth + plane
        places.append(jnp.where(live & (far < HALO), place, -1).astype(F32))
    info = [low, row_weight, unstack_lanes(target, 1), unstack_lanes(rank, 1)]
    info = [x.astype(F32) for x in info]
    dense = to_dense(code, cap)
    half = dense.shape[1] // 2
    for ref, place in (
        (pair_ref, jnp.where(odd, places[1], places[0])),
        (cross_ref, jnp.where(odd, places[0], places[1])),
    ):
        tile = ref.at[3 * HALO + 1]
        for i, x in enumerate([unstack_lanes(place, 1)] + info):
            tile[i : i + 1, :] = x
        tile[5:6, :half] = dense[:, :half]
        tile[6:7, :half] = dense[:, half:]

    for copy in copies[5:]:
        copy.wait()
    for copy in kept[:3]:
        copy.start()
    link_sum_ref[...] = linked(fracture_ref[...], links_ref, link_weights_ref)
    node_table = stack_lanes(fracture_ref[...])
    for i in range(node_table.shape[0]):
        message_ref[:, 1 + i // 4, i % 4, :] = jnp.broadcast_to(
            node_table[i : i + 1], (devices, LANES)
        )
    for ref, start, count in (
        (matrix_ref, 0, HALO + 1),
        (source_ref, HALO + 1, HALO),
        (storage_ref, 2 * HALO + 1, HALO),
    ):
        for far in range(count):
            up = ref[:, area_rows - 1 - far, :]
            down = ref[:, far, :]
            pair_ref[start + far] = jnp.where(odd, down, up)
            cross_ref[start + far] = jnp.where(odd, up, down)
    outs = [
        pltpu.make_async_copy(pair_ref, pair_hbm, sems.at[staged]),
        pltpu.make_async_copy(cross_ref, cross_hbm, sems.at[staged + 1]),
        pltpu.make_async_copy(message_ref, message_hbm, sems.at[staged + 2]),
    ]
    outs[0].start()
    outs[1].start()
    picked = stack_lanes(pick_cells(matrix_ref, columns_ref, hot_ref, low))
    message_ref[:, 0, 2, :] = pick_entries(weight * picked, slot_row, slot_lane)
    outs[2].start()
    for out in outs + kept:
        out.wait()


def turned(rows):
    count = rows.shape[0]
    extra = -count % 8
    if extra:
        rows = jnp.concatenate([rows, jnp.zeros((extra, LANES), rows.dtype)], axis=0)
    return rows.T


def same_cell_sum(values, cell_rows, cell_columns):
    value_columns = turned(values)
    blocks = cell_rows.shape[0]
    sums = [jnp.zeros((8, LANES), F32) for _ in range(blocks)]
    for j in range(blocks):
        cell = jnp.broadcast_to(cell_columns[:, j : j + 1], (LANES, LANES))
        value = jnp.broadcast_to(value_columns[:, j : j + 1], (LANES, LANES))
        for i in range(blocks):
            hit = jnp.where(cell == cell_rows[i : i + 1], value, 0.0)
            sums[i] = sums[i] + jnp.sum(hit.reshape(LANES // 8, 8, LANES), axis=0)
    return jnp.concatenate([jnp.sum(x, axis=0, keepdims=True) for x in sums], axis=0)


def relaxed(now, source, inverse, low_side, high_side, relaxation):
    depth, rows, cols = now.shape
    zero_plane = jnp.zeros((1, rows, cols), F32)
    beside = jnp.concatenate([now[1:], zero_plane], axis=0)
    beside = beside + jnp.concatenate([zero_plane, now[:-1]], axis=0)
    zero_row = jnp.zeros((depth, 1, cols), F32)
    above = zero_row if high_side is None else high_side[:, None]
    below = zero_row if low_side is None else low_side[:, None]
    beside = beside + jnp.concatenate([now[:, 1:], above], axis=1)
    beside = beside + jnp.concatenate([below, now[:, :-1]], axis=1)
    flat = now.reshape(depth * rows, cols)
    place = iota(flat.shape, 1)
    left = jnp.where(place == 0, 0.0, pltpu.roll(flat, 1, 1))
    right = jnp.where(place == cols - 1, 0.0, pltpu.roll(flat, cols - 1, 1))
    beside = beside + (left + right).reshape(now.shape)
    return (1.0 - relaxation) * now + relaxation * (source + inverse * beside)


def linked(fracture, links_ref, link_weights_ref):
    total = jnp.zeros(fracture.shape, F32)
    width = fracture.shape[1]
    tables = [fracture[:, i : i + LANES] for i in range(0, width, LANES)]
    sums = []
    for start in range(0, width, LANES):
        total = jnp.zeros(tables[0].shape, F32)
        for j in range(links_ref.shape[0]):
            link = links_ref[j, :, start : start + LANES]
            found = jnp.zeros(tables[0].shape, F32)
            for i, table in enumerate(tables):
                found = jnp.where(
                    link >> log2(LANES) == i, lane_gather(table, link & (LANES - 1)), found
                )
            total = total + link_weights_ref[j, :, start : start + LANES] * found
        sums.append(total)
    return jnp.concatenate(sums, axis=1)


def relaxed_side(now, beyond, edge, scaled, inverse, relaxation):
    depth, cols = edge.shape
    place = iota(edge.shape, 1)
    zero_plane = jnp.zeros((1, cols), F32)
    after = []
    for far in range(HALO):
        here = now[far]
        beside = jnp.concatenate([here[1:], zero_plane], axis=0)
        beside = beside + jnp.concatenate([zero_plane, here[:-1]], axis=0)
        beside = beside + jnp.where(place == 0, 0.0, pltpu.roll(here, 1, 1))
        beside = beside + jnp.where(place == cols - 1, 0.0, pltpu.roll(here, cols - 1, 1))
        beside = beside + (edge if far == 0 else now[far - 1])
        if far + 1 < HALO:
            beside = beside + now[far + 1]
        elif beyond is not None:
            beside = beside + beyond
        after.append(
            (1.0 - relaxation) * here + relaxation * (scaled[far] + inverse[far] * beside)
        )
    return after


def spread_side(place, low, values, depth, col_groups):
    rows = iota((col_groups * HALO * depth, place.shape[1]), 0)
    hot = (rows == place).astype(F32).astype(BF16)
    added = fold(matmul(hot, masked_parts(low, values), (1, 1)), 0)
    return [
        jnp.concatenate(
            [
                added[(group * HALO + far) * depth : (group * HALO + far + 1) * depth]
                for group in range(col_groups)
            ],
            axis=1,
        )
        for far in range(HALO)
    ]


def pick_cells(table_ref, columns_ref, hot_ref, low):
    depth, area_rows, cols = table_ref.shape
    for c in range(cols // LANES):
        chunk = table_ref[:, :, c * LANES : (c + 1) * LANES]
        put_columns(chunk.reshape(depth * area_rows, LANES), c, columns_ref)
    return pick_low(matmul(columns_ref[...], hot_ref[...], (1, 0)), low)


def side_kernel_inputs(info_ref, side):
    rows = [info_ref[side, i : i + 1, :] for i in range(5)]
    whole = [x.astype(jnp.int32) for x in rows]
    return whole[0], whole[1], rows[2], whole[3], whole[4]


def row_integer(rows_ref, index):
    return rows_ref[index].astype(jnp.int32)


def row_cells(rows_ref):
    return [unstack_lanes(row_integer(rows_ref, index), 1) for index in (4, 5)]


def first_window_kernel(
    relaxation,
    grids_hbm,
    rows_ref,
    partial_ref,
    scaled_ref,
    inverse_ref,
    edges_ref,
    row_partial_ref,
    row_inverse_ref,
    matrix_ref,
    source_ref,
    storage_ref,
    hot_ref,
    columns_ref,
    sems,
):
    copies = [
        pltpu.make_async_copy(row_slice(grids_hbm, rows_ref), rows_ref, sems.at[3]),
        pltpu.make_async_copy(grids_hbm.at[2], storage_ref, sems.at[2]),
        pltpu.make_async_copy(grids_hbm.at[1], source_ref, sems.at[1]),
        pltpu.make_async_copy(grids_hbm.at[0], matrix_ref, sems.at[0]),
    ]
    for copy in copies:
        copy.start()
    for copy in copies:
        copy.wait()
    depth, area_rows, cols = matrix_ref.shape
    plane_rows = depth * area_rows
    high, low = row_cells(rows_ref)
    weight = rows_ref[0]
    fill_hot(hot_ref, high)
    added = fold(matmul(hot_ref[...], masked_parts(low, unstack_lanes(weight, 1)), (1, 1)), 0)
    for c in range(cols // LANES):
        lanes = slice(c * LANES, (c + 1) * LANES)
        extra = added[c * plane_rows : (c + 1) * plane_rows].reshape(depth, area_rows, LANES)
        inverse = 1.0 / (6.0 + storage_ref[:, :, lanes] + extra)
        scaled_ref[:, :, lanes] = source_ref[:, :, lanes] * inverse
        inverse_ref[:, :, lanes] = inverse
    row_inverse_ref[...] = weight * stack_lanes(
        pick_cells(inverse_ref, columns_ref, hot_ref, low)
    )
    partial_ref[...] = relaxed(
        matrix_ref[...], scaled_ref[...], inverse_ref[...], None, None, relaxation
    )
    row_partial_ref[...] = weight * stack_lanes(pick_cells(partial_ref, columns_ref, hot_ref, low))
    edges_ref[0] = matrix_ref[:, 0, :]
    edges_ref[1] = matrix_ref[:, area_rows - 1, :]


def row_integer(rows_ref, index):
    return rows_ref[index].astype(jnp.int32)


def row_cells(rows_ref):
    return [unstack_lanes(row_integer(rows_ref, index), 1) for index in (4, 5)]


def both_sides(pair_ref, cross_ref, tiles):
    odd = (lax.axis_index("area") & 1) == 1
    lower = [jnp.where(odd, pair_ref[i], cross_ref[i]) for i in tiles]
    upper = [jnp.where(odd, cross_ref[i], pair_ref[i]) for i in tiles]
    return lower, upper


def beside_rows(pair_ref, cross_ref, rows_ref, area_rows):
    (lower,), (upper,) = both_sides(pair_ref, cross_ref, (0,))
    depth = lower.shape[0]
    high, low = row_cells(rows_ref)
    row = high & (area_rows - 1)
    plane = (high >> log2(area_rows)) & (depth - 1)
    place = (high >> log2(depth * area_rows)) * depth + plane
    table = jnp.concatenate([stack_lanes(lower), stack_lanes(upper)], axis=0)
    place = jnp.where(row == 0, place, place + table.shape[0] // 2)
    place = jnp.where((row == 0) | (row == area_rows - 1), place, -1)
    hot = (iota((table.shape[0], place.shape[1]), 0) == place).astype(F32).astype(BF16)
    columns = jnp.concatenate(halves(table.T), axis=0)
    return stack_lanes(pick_low(matmul(columns, hot, (1, 0)), low))


def add_rows(relaxation, values, partial_ref, inverse_ref, rows_ref, hot_ref, matrix_ref):
    depth, area_rows, cols = partial_ref.shape
    plane_rows = depth * area_rows
    high, low = row_cells(rows_ref)
    fill_hot(hot_ref, high)
    parts = masked_parts(low, unstack_lanes(values, 1))
    added = fold(matmul(hot_ref[...], parts, (1, 1)), 0)
    for c in range(cols // LANES):
        lanes = slice(c * LANES, (c + 1) * LANES)
        extra = added[c * plane_rows : (c + 1) * plane_rows].reshape(depth, area_rows, LANES)
        matrix_ref[:, :, lanes] = (
            partial_ref[:, :, lanes] + (relaxation * inverse_ref[:, :, lanes]) * extra
        )


def returned_values(returned, rows_ref):
    target, rank = row_integer(rows_ref, 1), row_integer(rows_ref, 2)
    return rows_ref[0] * pick_entries(returned, target, rank)


def first_sides(relaxation, pair_ref, cross_ref, edges_ref, scaled_ref, inverse_ref, info_ref):
    depth, cols = edges_ref.shape[1:]
    partial = []
    for side, tiles in enumerate(both_sides(pair_ref, cross_ref, range(3 * HALO + 2))):
        info_ref[side] = tiles[3 * HALO + 1]
        place, low, weight, _, _ = side_kernel_inputs(info_ref, side)
        added = spread_side(place, low, weight, depth, cols // LANES)
        scaled, inverse = [], []
        for far in range(HALO):
            storage = tiles[2 * HALO + 1 + far]
            inverse.append(jnp.where(storage > 0.0, 1.0 / (6.0 + storage + added[far]), 0.0))
            scaled.append(tiles[HALO + 1 + far] * inverse[far])
            scaled_ref[side, far] = scaled[far]
            inverse_ref[side, far] = inverse[far]
        partial.append(
            relaxed_side(
                tiles[:HALO], tiles[HALO], edges_ref[side], scaled, inverse, relaxation
            )
        )
    return partial


def window_kernel(
    relaxation,
    before,
    cap,
    first,
    last,
    arrived_ref,
    partial_before_ref,
    scaled_ref,
    inverse_ref,
    rows_ref,
    slots_ref,
    fracture_ref,
    links_ref,
    link_weights_ref,
    *refs,
):
    depth, area_rows, cols = scaled_ref.shape
    devices = arrived_ref.shape[0]
    half = devices * cap // 2
    if first:
        pair_ref, cross_ref, edges_ref, *refs = refs
        partial_ref, side_partial_ref, link_sum_ref, *refs = refs
        side_scaled_ref, side_inverse_ref, side_info_ref, *refs = refs
    else:
        side_before_ref, side_scaled_ref, side_inverse_ref, side_info_ref, *refs = refs
        partial_ref, side_partial_ref, link_sum_ref, *refs = refs
    if last:
        matrix_ref, hot_ref = refs
    else:
        row_partial_ref, matrix_ref, hot_ref, columns_ref = refs
    returned = device_values(arrived_ref, row_integer(slots_ref, 2)) if first else arrived_ref[:, 1, :]
    values = returned_values(returned, rows_ref)
    add_rows(before, values, partial_before_ref, inverse_ref, rows_ref, hot_ref, matrix_ref)
    if first:
        lower, upper = both_sides(pair_ref, cross_ref, (0,))
        for edge, tile in ((0, lower[0]), (area_rows - 1, upper[0])):
            matrix_ref[:, edge, :] = (
                matrix_ref[:, edge, :] + (before * inverse_ref[:, edge, :]) * tile
            )
        side_before = first_sides(
            before, pair_ref, cross_ref, edges_ref, side_scaled_ref, side_inverse_ref, side_info_ref
        )
    else:
        side_before = [[side_before_ref[side, far] for far in range(HALO)] for side in range(2)]
    edges = []
    for side, edge in enumerate((0, area_rows - 1)):
        place, low, weight, target, rank = side_kernel_inputs(side_info_ref, side)
        if first:
            code = jnp.concatenate(
                [side_info_ref[side, i : i + 1, :half] for i in (5, 6)], axis=1
            )
            code = from_dense(code, devices, cap).astype(jnp.int32)
            returned = device_values(arrived_ref, code)
        else:
            returned = arrived_ref[:, 2 + side, :]
        values = pick_entries(returned, stack_lanes(target), stack_lanes(rank))
        values = weight * unstack_lanes(values, 1)
        added = spread_side(place, low, values, depth, cols // LANES)
        now = [
            side_before[side][far] + before * side_inverse_ref[side, far] * added[far]
            for far in range(HALO)
        ]
        edges.append(now[0])
        after = relaxed_side(
            now,
            None,
            matrix_ref[:, edge, :],
            [side_scaled_ref[side, far] for far in range(HALO)],
            [side_inverse_ref[side, far] for far in range(HALO)],
            relaxation,
        )
        for far in range(HALO):
            side_partial_ref[side, far] = after[far]
    partial_ref[...] = relaxed(
        matrix_ref[...],
        scaled_ref[...],
        inverse_ref[...],
        edges[0],
        edges[1],
        relaxation,
    )
    if not last:
        row_partial_ref[...] = rows_ref[0] * stack_lanes(
            pick_cells(partial_ref, columns_ref, hot_ref, row_cells(rows_ref)[1])
        )
    link_sum_ref[...] = linked(fracture_ref[...], links_ref, link_weights_ref)


def returned_values(returned, rows_ref):
    target, rank = row_integer(rows_ref, 1), row_integer(rows_ref, 2)
    return rows_ref[0] * pick_entries(returned, target, rank)


def row_values(
    relaxation, returned, slots_ref, rows_ref, row_partial_ref, row_inverse_ref, beside=None
):
    cells = rows_ref[3]
    total = same_cell_sum(returned_values(returned, rows_ref), cells, turned(cells))
    if beside is not None:
        total = total + beside
    outgoing = row_partial_ref[...] + (relaxation * row_inverse_ref[...]) * total
    return pick_entries(outgoing, row_integer(slots_ref, 0), row_integer(slots_ref, 1))


def node_sums(code, shape, *values):
    owned, blk = shape
    rows = owned * blk // LANES
    member = iota((rows, code.shape[1]), 0) == code >> log2(LANES)
    low = (iota((LANES, code.shape[1]), 0) == code & (LANES - 1)).astype(F32).astype(BF16)
    parts = []
    for value in values:
        high = value.astype(BF16).astype(F32)
        parts += [jnp.where(member, high, 0.0), jnp.where(member, value - high, 0.0)]
    sums = matmul(jnp.concatenate(parts, axis=0).astype(BF16), low, (1, 1))
    sums = [sums[i : i + rows] for i in range(0, sums.shape[0], rows)]
    return [
        unstack_lanes(sums[2 * i] + sums[2 * i + 1], owned) for i in range(len(values))
    ]


def node_values(table, code):
    found = jnp.zeros(code.shape, F32)
    low = code & (LANES - 1)
    for row in range(table.shape[0]):
        values = jnp.broadcast_to(table[row : row + 1], code.shape)
        found = jnp.where(code >> log2(LANES) == row, lane_gather(values, low), found)
    return found


def device_values(arrived_ref, code):
    found = jnp.zeros(code.shape, F32)
    low = code & (LANES - 1)
    for row in range(4 * (arrived_ref.shape[1] - 1)):
        values = lane_gather(arrived_ref[:, 1 + row // 4, row % 4, :], low)
        found = jnp.where(code >> log2(LANES) == row, values, found)
    return found


def put_requested(message_ref, values):
    zero = jnp.zeros((1, LANES), F32)
    order = group_order(values.shape[0])
    rows = {device: values[i : i + 1] for i, device in enumerate(order)}
    message_ref[:, 1, :] = values
    for place, step in ((2, -1), (3, 1)):
        message_ref[:, place, :] = jnp.concatenate(
            [rows.get(device + step, zero) for device in order], axis=0
        )


def first_step_kernel(
    relaxation,
    cap,
    area_rows,
    arrived_ref,
    pair_ref,
    cross_ref,
    slots_ref,
    rows_ref,
    row_partial_ref,
    row_inverse_ref,
    fracture_ref,
    link_sum_ref,
    fracture_source_ref,
    leak_ref,
    link_weights_ref,
    fracture_next_ref,
    fracture_inverse_ref,
    node_code_ref,
    message_hbm,
    message_ref,
    sem,
):
    message_ref[:, 0, :] = row_values(
        relaxation,
        device_values(arrived_ref, row_integer(slots_ref, 2)),
        slots_ref,
        rows_ref,
        row_partial_ref,
        row_inverse_ref,
        beside_rows(pair_ref, cross_ref, rows_ref, area_rows),
    )
    code = arrived_ref[:, 0, 0, :].astype(jnp.int32)
    node_code_ref[...] = code
    dense = to_dense(code, cap)
    weight_sum, value_sum = node_sums(
        dense,
        fracture_ref.shape,
        to_dense(arrived_ref[:, 0, 1, :], cap),
        to_dense(arrived_ref[:, 0, 2, :], cap),
    )
    diag = leak_ref[...] + jnp.sum(link_weights_ref[...], axis=0) + weight_sum
    inverse = 1.0 / diag
    fracture_inverse_ref[...] = inverse
    fracture_next = (1.0 - relaxation) * fracture_ref[...] + (relaxation * inverse) * (
        fracture_source_ref[...] + link_sum_ref[...] + value_sum
    )
    fracture_next_ref[...] = fracture_next
    put_requested(message_ref, node_values(stack_lanes(fracture_next), code))
    out = pltpu.make_async_copy(message_ref, message_hbm, sem)
    out.start()
    out.wait()


def next_fracture(
    relaxation,
    cap,
    arrived_ref,
    code,
    fracture_ref,
    link_sum_ref,
    fracture_source_ref,
    fracture_inverse_ref,
):
    (value_sum,) = node_sums(
        to_dense(code, cap), fracture_ref.shape, to_dense(arrived_ref[:, 0, :], cap)
    )
    return (1.0 - relaxation) * fracture_ref[...] + (relaxation * fracture_inverse_ref[...]) * (
        fracture_source_ref[...] + link_sum_ref[...] + value_sum
    )


def step_kernel(
    relaxation,
    cap,
    arrived_ref,
    node_code_ref,
    slots_ref,
    rows_ref,
    row_partial_ref,
    row_inverse_ref,
    fracture_ref,
    link_sum_ref,
    fracture_source_ref,
    fracture_inverse_ref,
    fracture_next_ref,
    message_hbm,
    message_ref,
    sem,
):
    message_ref[:, 0, :] = row_values(
        relaxation,
        arrived_ref[:, 1, :],
        slots_ref,
        rows_ref,
        row_partial_ref,
        row_inverse_ref,
    )
    code = node_code_ref[...]
    fracture_next = next_fracture(
        relaxation,
        cap,
        arrived_ref,
        code,
        fracture_ref,
        link_sum_ref,
        fracture_source_ref,
        fracture_inverse_ref,
    )
    fracture_next_ref[...] = fracture_next
    put_requested(message_ref, node_values(stack_lanes(fracture_next), code))
    out = pltpu.make_async_copy(message_ref, message_hbm, sem)
    out.start()
    out.wait()


def last_step_kernel(
    relaxation,
    cap,
    arrived_ref,
    node_code_ref,
    partial_ref,
    inverse_ref,
    rows_ref,
    fracture_ref,
    link_sum_ref,
    fracture_source_ref,
    fracture_inverse_ref,
    matrix_ref,
    fracture_next_ref,
    hot_ref,
):
    values = returned_values(arrived_ref[:, 1, :], rows_ref)
    add_rows(relaxation, values, partial_ref, inverse_ref, rows_ref, hot_ref, matrix_ref)
    fracture_next_ref[...] = next_fracture(
        relaxation,
        cap,
        arrived_ref,
        node_code_ref[...],
        fracture_ref,
        link_sum_ref,
        fracture_source_ref,
        fracture_inverse_ref,
    )


def call(kernel, outs, ins, name, micros, hbm_in=(), hbm_out=(), scratch=(), aliases=None, limit=VMEM_LIMIT):
    return pl.pallas_call(
        kernel,
        out_shape=[jax.ShapeDtypeStruct(shape, dtype) for shape, dtype in outs],
        in_specs=[
            pl.BlockSpec(memory_space=pltpu.HBM if i in hbm_in else pltpu.VMEM)
            for i in range(len(ins))
        ],
        out_specs=[
            pl.BlockSpec(memory_space=pltpu.HBM if i in hbm_out else pltpu.VMEM)
            for i in range(len(outs))
        ],
        scratch_shapes=list(scratch),
        input_output_aliases=aliases or {},
        compiler_params=pltpu.CompilerParams(vmem_limit_bytes=limit),
        cost_estimate=pl.CostEstimate(
            flops=0, bytes_accessed=int(micros * 3.0e6), transcendentals=0
        ),
        name=name,
    )(*ins)


def local(
    block_owner,
    transfer_cells,
    transfer_nodes,
    transfer_weights,
    row_counts,
    matrix_start,
    matrix_source,
    matrix_storage,
    fracture_start,
    fracture_source,
    fracture_leak,
    fracture_links,
    link_weights,
):
    devices = lax.axis_size("area")
    depth, area_rows, cols = matrix_start.shape
    owned, blk = fracture_start.shape
    total_rows = transfer_cells.shape[0]
    cap = 3 * total_rows // (2 * devices)
    cells = depth * area_rows * cols // LANES
    relax = relax_weights(ITERS)
    grid = (matrix_start.shape, F32)
    grids = ((GRID_SLOTS,) + matrix_start.shape, F32)
    fracture = (fracture_start.shape, F32)
    side = ((3 * HALO + 2, depth, cols), F32)
    sides = ((2, HALO, depth, cols), F32)
    hot = pltpu.VMEM((cells, total_rows), BF16)
    columns = pltpu.VMEM((2 * LANES, cells), BF16)
    padded = (devices, LANES)
    first_message = ((devices, 1 + owned * blk // LANES // 4, 4, LANES), F32)
    message_type = ((devices, 4, LANES), F32)
    pairs, crossings = [
        [(i + a, i + b) for i in range(start, devices - 1, 2) for a, b in ((0, 1), (1, 0))]
        for start in (0, 1)
    ]

    def exchange(message):
        return lax.all_to_all(
            message,
            "area",
            split_axis=0,
            concat_axis=0,
            tiled=True,
            axis_index_groups=[group_order(devices)],
        )

    staged = [
        row_counts.reshape(1, 1),
        block_owner.reshape(-1, LANES),
        transfer_cells.reshape(-1, LANES),
        transfer_nodes.reshape(-1, LANES),
        transfer_weights.reshape(-1, LANES),
        matrix_start,
        fracture_start,
        matrix_source,
        matrix_storage,
        fracture_links,
        link_weights,
    ]
    row_shape = (total_rows // LANES, LANES)
    rows = (row_shape, F32)
    info = ((6,) + row_shape, F32)
    edges = ((2, depth, cols), F32)
    slot_info, message, pair, cross, grids_start, link_sum = call(
        functools.partial(setup_kernel, devices, cap, len(staged)),
        [((3,) + padded, F32), first_message, side, side, grids, fracture],
        staged,
        "place_rows",
        5.0,
        hbm_in=range(len(staged)),
        hbm_out=(1, 2, 3, 4),
        scratch=[pltpu.VMEM(x.shape, x.dtype) for x in staged]
        + [
            pltpu.VMEM(*info),
            pltpu.VMEM(*first_message),
            pltpu.VMEM(*side),
            pltpu.VMEM(*side),
            hot,
            columns,
            pltpu.SemaphoreType.DMA((len(staged) + 7,)),
        ],
        limit=63 * 1024 * 1024,
    )
    arrived = exchange(message)
    pair = lax.ppermute(pair, "area", pairs)
    cross = lax.ppermute(cross, "area", crossings)
    row_info, partial, scaled, inverse, edge_rows, row_partial, row_inverse = call(
        functools.partial(first_window_kernel, relax[0]),
        [info, grid, grid, grid, edges, rows, rows],
        [grids_start],
        "stencil_first",
        4.0,
        hbm_in=(0,),
        scratch=[pltpu.VMEM(*grid)] * 3 + [hot, columns, pltpu.SemaphoreType.DMA((4,))],
    )
    fracture_now = fracture_start
    message_scratch = [pltpu.VMEM(*message_type), pltpu.SemaphoreType.DMA]
    fracture_now, fracture_inverse, node_code, message = call(
        functools.partial(first_step_kernel, relax[0], cap, area_rows),
        [fracture, fracture, (padded, jnp.int32), message_type],
        [
            arrived,
            pair,
            cross,
            slot_info,
            row_info,
            row_partial,
            row_inverse,
            fracture_now,
            link_sum,
            fracture_source,
            fracture_leak,
            link_weights,
        ],
        "couple_first",
        2.0,
        hbm_out=(3,),
        scratch=message_scratch,
    )
    for index in range(1, ITERS):
        last = index == ITERS - 1
        old, arrived = arrived, exchange(message)
        first = index == 1
        inputs = [old, partial, scaled, inverse, row_info, slot_info, fracture_now]
        inputs += [fracture_links, link_weights]
        if first:
            inputs += [pair, cross, edge_rows]
        else:
            inputs += [side_partial, side_scaled, side_inverse, side_info]
        outs = call(
            functools.partial(window_kernel, relax[index], relax[index - 1], cap, first, last),
            [grid, sides, fracture]
            + ([sides, sides, edges] if first else [])
            + ([] if last else [rows]),
            inputs,
            "stencil",
            3.0,
            aliases={1: 0} if first else {1: 0, 9: 1},
            scratch=[pltpu.VMEM(*grid), hot] + ([] if last else [columns]),
        )
        partial, side_partial, link_sum = outs[:3]
        if first:
            side_scaled, side_inverse, side_info = outs[3:6]
        fractures = [fracture_now, link_sum, fracture_source, fracture_inverse]
        if last:
            return call(
                functools.partial(last_step_kernel, relax[index], cap),
                [grid, fracture],
                [arrived, node_code, partial, inverse, row_info] + fractures,
                "couple_last",
                2.0,
                scratch=[hot],
            )
        row_partial = outs[-1]
        fracture_now, message = call(
            functools.partial(step_kernel, relax[index], cap),
            [fracture, message_type],
            [arrived, node_code, slot_info, row_info, row_partial, row_inverse] + fractures,
            "couple",
            2.0,
            hbm_out=(1,),
            scratch=message_scratch,
        )


def solution(mesh):
    in_specs = (
        P(),
        P("area"),
        P("area"),
        P("area"),
        P("area"),
        P("real", "area", None),
        P("real", "area", None),
        P("real", "area", None),
        P("area", "real"),
        P("area", "real"),
        P("area", "real"),
        P(None, "area", None),
        P("real", "area", None),
    )
    out_specs = (P("real", "area", None), P("area", "real"))
    return jax.shard_map(local, mesh=mesh, in_specs=in_specs, out_specs=out_specs, check_vma=False)
```

```python
import functools
import math

import jax
import jax.numpy as jnp
from jax import lax
from jax.experimental import pallas as pl
from jax.experimental.pallas import tpu as pltpu
from jax.sharding import PartitionSpec as P

ITERS = 4
HALO = ITERS - 1
GRID_SLOTS = 72
LANES = 128
F32 = jnp.float32
BF16 = jnp.bfloat16
VMEM_LIMIT = 32 * 1024 * 1024


def relax_weights(steps_total):
    return [
        1.0 / (1.0 + 0.75 * math.cos(math.pi * (2 * index + 1) / (2 * steps_total)))
        for index in range(steps_total)
    ]


def log2(value):
    assert value & (value - 1) == 0
    return value.bit_length() - 1


def group_order(devices):
    part = devices // 4
    return [quarter * part + (i - 1) % part for quarter in (2, 0, 1, 3) for i in range(part)]


def iota(shape, dim):
    return lax.broadcasted_iota(jnp.int32, shape, dim)


def halves(x):
    high = x.astype(BF16)
    low = (x - high.astype(F32)).astype(BF16)
    return high, low


def matmul(a, b, contract):
    return lax.dot_general(a, b, ((contract[:1], contract[1:]), ((), ())), preferred_element_type=F32)


def to_dense(x, cap):
    return jnp.concatenate([x[i : i + 1, :cap] for i in range(x.shape[0])], axis=1)


def from_dense(x, devices, cap):
    rows = jnp.concatenate([x[:, i * cap : (i + 1) * cap] for i in range(devices)], axis=0)
    return jnp.concatenate([rows, jnp.zeros((devices, LANES - cap), x.dtype)], axis=1)


def lane_gather(table, index):
    return jnp.take_along_axis(table, index, axis=1, mode="promise_in_bounds")


def masked_parts(low, *values):
    mask = iota((LANES, low.shape[1]), 0) == low
    zero = jnp.zeros((), F32)
    parts = []
    for value in values:
        high = value.astype(BF16).astype(F32)
        parts.append(jnp.where(mask, high, zero).astype(BF16))
        parts.append(jnp.where(mask, value - high, zero).astype(BF16))
    return jnp.concatenate(parts, axis=0)


def fold(wide, index):
    start = 2 * index * LANES
    return wide[:, start : start + LANES] + wide[:, start + LANES : start + 2 * LANES]


def pick_low(tall, low):
    both = tall[:LANES] + tall[LANES:]
    return jnp.sum(
        jnp.where(iota(both.shape, 0) == low, both, 0.0), axis=0, keepdims=True
    )


def stack_lanes(x):
    return jnp.concatenate(
        [x[:, i * LANES : (i + 1) * LANES] for i in range(x.shape[1] // LANES)], axis=0
    )


def unstack_lanes(x, rows):
    return jnp.concatenate([x[i : i + rows] for i in range(0, x.shape[0], rows)], axis=1)


def put_columns(chunk, index, columns_ref):
    high, low = halves(chunk.T)
    columns_ref[:LANES, index * LANES : (index + 1) * LANES] = high
    columns_ref[LANES:, index * LANES : (index + 1) * LANES] = low


def fill_hot(hot_ref, high):
    for start in range(0, hot_ref.shape[0], LANES):
        rows = iota((LANES, high.shape[1]), 0) + start
        hot_ref[start : start + LANES, :] = (rows == high).astype(F32).astype(BF16)


def pick_entries(table, row, lane):
    found = jnp.zeros(row.shape, table.dtype)
    for i in range(table.shape[0]):
        values = jnp.broadcast_to(table[i : i + 1], row.shape)
        found = jnp.where(row == i, lane_gather(values, lane), found)
    return found


def row_slice(grids_hbm, rows_ref):
    count, groups, lanes = rows_ref.shape
    return grids_hbm.at[3, :count, :groups, :lanes]


def setup_kernel(devices, cap, staged, *refs):
    sources, refs = refs[:staged], refs[staged:]
    slots_ref, message_hbm, pair_hbm, cross_hbm, grids_hbm, link_sum_ref = refs[:6]
    targets, refs = refs[6 : 6 + staged], refs[6 + staged :]
    rows_ref, message_ref, pair_ref, cross_ref, hot_ref, columns_ref, sems = refs
    copies = [
        pltpu.make_async_copy(sources[i], targets[i], sems.at[i]) for i in range(staged)
    ]
    kept = [
        pltpu.make_async_copy(targets[i], grids_hbm.at[j], sems.at[staged + 3 + j])
        for j, i in enumerate((5, 7, 8))
    ]
    kept.append(pltpu.make_async_copy(rows_ref, row_slice(grids_hbm, rows_ref), sems.at[staged + 6]))
    for copy in copies:
        copy.start()
    for copy in copies[:5]:
        copy.wait()
    counts_ref, owner_ref, cells_ref, nodes_ref, weights_ref = targets[:5]
    matrix_ref, fracture_ref, source_ref, storage_ref, links_ref, link_weights_ref = targets[5:]
    owned, blk = fracture_ref.shape
    depth, area_rows, cols = matrix_ref.shape
    groups = cells_ref.shape[0]
    plane_rows = depth * area_rows
    shape = (groups, LANES)
    nodes, cells = nodes_ref[...], cells_ref[...]
    live = iota(shape, 0) * LANES + iota(shape, 1) < counts_ref[...]
    weight = jnp.where(live, weights_ref[...], 0.0)
    block = nodes >> log2(blk)
    slot = jnp.zeros(shape, jnp.int32)
    for part in range(owner_ref.shape[0]):
        table = jnp.broadcast_to(owner_ref[part : part + 1, :], shape)
        found = lane_gather(table, block & (LANES - 1))
        slot = jnp.where(block >> log2(LANES) == part, found, slot)
    device = slot >> log2(owned)
    target = jnp.zeros(shape, jnp.int32)
    for position, place in enumerate(group_order(devices)):
        target = jnp.where(device == place, position, target)
    target = jnp.where(live, target, -1)
    node_high = ((nodes & (blk - 1)) >> log2(LANES)) * owned + (slot & (owned - 1))
    node_low = nodes & (LANES - 1)
    plane_row = cells >> log2(cols)
    cell_group = (cells & (cols - 1)) >> log2(LANES)
    cell_high = cell_group * plane_rows + plane_row
    cell_low = cells & (LANES - 1)
    high, low = unstack_lanes(cell_high, 1), unstack_lanes(cell_low, 1)
    row_weight = unstack_lanes(weight, 1)
    fill_hot(hot_ref, high)

    device_rows = iota((devices, LANES), 0)
    member = [(device_rows == target[q : q + 1]).astype(F32) for q in range(groups)]
    earlier = (iota((LANES, LANES), 0) < iota((LANES, LANES), 1)).astype(F32).astype(BF16)
    counted = matmul(jnp.concatenate(member, axis=0).astype(BF16), earlier, (1, 0))
    before = jnp.zeros((devices, 1), F32)
    rank = []
    for q in range(groups):
        inside = counted[q * devices : (q + 1) * devices] + before
        rank.append(jnp.sum(member[q] * inside, axis=0, keepdims=True).astype(jnp.int32))
        before = before + jnp.sum(member[q], axis=1, keepdims=True)
    rank_row = jnp.concatenate(rank, axis=1)
    rank = jnp.concatenate(rank, axis=0)
    member = jnp.concatenate(member, axis=1)

    first = weight.astype(BF16).astype(F32)
    second = (weight - first).astype(BF16).astype(F32)
    features = [
        jnp.ones(shape, F32),
        node_high.astype(F32),
        node_low.astype(F32),
        first,
        second,
        weight - first - second,
        iota(shape, 0).astype(F32),
        iota(shape, 1).astype(F32),
    ]
    features = [member * unstack_lanes(x, 1) for x in features]
    ranked = (iota((LANES, groups * LANES), 0) == rank_row).astype(F32).astype(BF16)
    packed = matmul(jnp.concatenate(features, axis=0).astype(BF16), ranked, (1, 1))
    packed = [packed[i * devices : (i + 1) * devices] for i in range(len(features))]
    code = jnp.where(packed[0] > 0.5, packed[1] * LANES + packed[2], -1.0)
    slot_row, slot_lane = packed[6].astype(jnp.int32), packed[7].astype(jnp.int32)
    slots_ref[0], slots_ref[1], slots_ref[2] = packed[6], packed[7], code
    alone = -1 - iota(shape, 0) * LANES - iota(shape, 1)
    cell = jnp.where(live, cells, alone)
    for i, x in enumerate((weight, target, rank, cell, cell_high, cell_low)):
        rows_ref[i] = x.astype(F32)
    kept[3].start()
    message_ref[:, 0, 0, :] = code
    message_ref[:, 0, 1, :] = packed[3] + packed[4] + packed[5]
    message_ref[:, 0, 3, :] = jnp.zeros((devices, LANES), F32)

    odd = (lax.axis_index("area") & 1) == 1
    plane = plane_row >> log2(area_rows)
    row = plane_row & (area_rows - 1)
    places = []
    for far in (area_rows - 1 - row, row):
        place = (cell_group * HALO + far) * depth + plane
        places.append(jnp.where(live & (far < HALO), place, -1).astype(F32))
    info = [low, row_weight, unstack_lanes(target, 1), unstack_lanes(rank, 1)]
    info = [x.astype(F32) for x in info]
    dense = to_dense(code, cap)
    half = dense.shape[1] // 2
    for ref, place in (
        (pair_ref, jnp.where(odd, places[1], places[0])),
        (cross_ref, jnp.where(odd, places[0], places[1])),
    ):
        tile = ref.at[3 * HALO + 1]
        for i, x in enumerate([unstack_lanes(place, 1)] + info):
            tile[i : i + 1, :] = x
        tile[5:6, :half] = dense[:, :half]
        tile[6:7, :half] = dense[:, half:]

    for copy in copies[5:]:
        copy.wait()
    for copy in kept[:3]:
        copy.start()
    link_sum_ref[...] = linked(fracture_ref[...], links_ref, link_weights_ref)
    node_table = stack_lanes(fracture_ref[...])
    for i in range(node_table.shape[0]):
        message_ref[:, 1 + i // 4, i % 4, :] = jnp.broadcast_to(
            node_table[i : i + 1], (devices, LANES)
        )
    for ref, start, count in (
        (matrix_ref, 0, HALO + 1),
        (source_ref, HALO + 1, HALO),
        (storage_ref, 2 * HALO + 1, HALO),
    ):
        for far in range(count):
            up = ref[:, area_rows - 1 - far, :]
            down = ref[:, far, :]
            pair_ref[start + far] = jnp.where(odd, down, up)
            cross_ref[start + far] = jnp.where(odd, up, down)
    outs = [
        pltpu.make_async_copy(pair_ref, pair_hbm, sems.at[staged]),
        pltpu.make_async_copy(cross_ref, cross_hbm, sems.at[staged + 1]),
        pltpu.make_async_copy(message_ref, message_hbm, sems.at[staged + 2]),
    ]
    outs[0].start()
    outs[1].start()
    picked = stack_lanes(pick_cells(matrix_ref, columns_ref, hot_ref, low))
    message_ref[:, 0, 2, :] = pick_entries(weight * picked, slot_row, slot_lane)
    outs[2].start()
    for out in outs + kept:
        out.wait()


def turned(rows):
    count = rows.shape[0]
    extra = -count % 8
    if extra:
        rows = jnp.concatenate([rows, jnp.zeros((extra, LANES), rows.dtype)], axis=0)
    return rows.T


def find_chains(cells):
    blocks = cells.shape[0]
    columns = turned(cells)
    none = float(blocks * LANES)
    sublane, lane = iota((LANES, LANES), 0), iota((LANES, LANES), 1)
    after = [jnp.full((8, LANES), none, F32) for _ in range(blocks)]
    before = [jnp.full((8, LANES), -1.0, F32) for _ in range(blocks)]
    count = [jnp.zeros((8, LANES), F32) for _ in range(blocks)]
    for j in range(blocks):
        cell = jnp.broadcast_to(columns[:, j : j + 1], (LANES, LANES))
        place = (sublane + j * LANES).astype(F32)
        for i in range(blocks):
            same = cell == cells[i : i + 1]
            parts = (LANES // 8, 8, LANES)
            ones = jnp.where(same, 1.0, 0.0).reshape(parts)
            count[i] = count[i] + jnp.sum(ones, axis=0)
            if j >= i:
                later = same & (sublane > lane) if j == i else same
                found = jnp.where(later, place, none).reshape(parts)
                after[i] = jnp.minimum(after[i], jnp.min(found, axis=0))
            if j <= i:
                sooner = same & (sublane < lane) if j == i else same
                found = jnp.where(sooner, place, -1.0).reshape(parts)
                before[i] = jnp.maximum(before[i], jnp.max(found, axis=0))
    after = jnp.concatenate([jnp.min(x, axis=0, keepdims=True) for x in after], axis=0)
    before = jnp.concatenate([jnp.max(x, axis=0, keepdims=True) for x in before], axis=0)
    count = jnp.concatenate([jnp.sum(x, axis=0, keepdims=True) for x in count], axis=0)
    return jnp.where(after < none, after, -1.0), before, count


def same_cell_sum(values, chains_ref):
    most = jnp.max(chains_ref[2]).astype(jnp.int32)
    rounds = log2(values.size)
    steps = sum((most > (1 << i)).astype(jnp.int32) for i in range(rounds))

    def step(_, state):
        after = []
        for total, link in (state[:2], state[2:]):
            row, lane = (link - 1) >> log2(LANES), (link - 1) & (LANES - 1)
            after += [total + pick_entries(total, row, lane), pick_entries(link, row, lane)]
        return tuple(after)

    ahead, behind = [row_integer(chains_ref, i) + 1 for i in range(2)]
    ahead, _, behind, _ = lax.fori_loop(0, steps, step, (values, ahead, values, behind))
    return ahead + behind - values


def relaxed(now, source, inverse, low_side, high_side, relaxation):
    depth, rows, cols = now.shape
    zero_plane = jnp.zeros((1, rows, cols), F32)
    beside = jnp.concatenate([now[1:], zero_plane], axis=0)
    beside = beside + jnp.concatenate([zero_plane, now[:-1]], axis=0)
    zero_row = jnp.zeros((depth, 1, cols), F32)
    above = zero_row if high_side is None else high_side[:, None]
    below = zero_row if low_side is None else low_side[:, None]
    beside = beside + jnp.concatenate([now[:, 1:], above], axis=1)
    beside = beside + jnp.concatenate([below, now[:, :-1]], axis=1)
    flat = now.reshape(depth * rows, cols)
    place = iota(flat.shape, 1)
    left = jnp.where(place == 0, 0.0, pltpu.roll(flat, 1, 1))
    right = jnp.where(place == cols - 1, 0.0, pltpu.roll(flat, cols - 1, 1))
    beside = beside + (left + right).reshape(now.shape)
    return (1.0 - relaxation) * now + relaxation * (source + inverse * beside)


def linked(fracture, links_ref, link_weights_ref):
    total = jnp.zeros(fracture.shape, F32)
    width = fracture.shape[1]
    tables = [fracture[:, i : i + LANES] for i in range(0, width, LANES)]
    sums = []
    for start in range(0, width, LANES):
        total = jnp.zeros(tables[0].shape, F32)
        for j in range(links_ref.shape[0]):
            link = links_ref[j, :, start : start + LANES]
            found = jnp.zeros(tables[0].shape, F32)
            for i, table in enumerate(tables):
                found = jnp.where(
                    link >> log2(LANES) == i, lane_gather(table, link & (LANES - 1)), found
                )
            total = total + link_weights_ref[j, :, start : start + LANES] * found
        sums.append(total)
    return jnp.concatenate(sums, axis=1)


def relaxed_side(now, beyond, edge, scaled, inverse, relaxation):
    depth, cols = edge.shape
    place = iota(edge.shape, 1)
    zero_plane = jnp.zeros((1, cols), F32)
    after = []
    for far in range(HALO):
        here = now[far]
        beside = jnp.concatenate([here[1:], zero_plane], axis=0)
        beside = beside + jnp.concatenate([zero_plane, here[:-1]], axis=0)
        beside = beside + jnp.where(place == 0, 0.0, pltpu.roll(here, 1, 1))
        beside = beside + jnp.where(place == cols - 1, 0.0, pltpu.roll(here, cols - 1, 1))
        beside = beside + (edge if far == 0 else now[far - 1])
        if far + 1 < HALO:
            beside = beside + now[far + 1]
        elif beyond is not None:
            beside = beside + beyond
        after.append(
            (1.0 - relaxation) * here + relaxation * (scaled[far] + inverse[far] * beside)
        )
    return after


def spread_side(place, low, values, depth, col_groups):
    rows = iota((col_groups * HALO * depth, place.shape[1]), 0)
    hot = (rows == place).astype(F32).astype(BF16)
    added = fold(matmul(hot, masked_parts(low, values), (1, 1)), 0)
    return [
        jnp.concatenate(
            [
                added[(group * HALO + far) * depth : (group * HALO + far + 1) * depth]
                for group in range(col_groups)
            ],
            axis=1,
        )
        for far in range(HALO)
    ]


def pick_cells(table_ref, columns_ref, hot_ref, low):
    depth, area_rows, cols = table_ref.shape
    for c in range(cols // LANES):
        chunk = table_ref[:, :, c * LANES : (c + 1) * LANES]
        put_columns(chunk.reshape(depth * area_rows, LANES), c, columns_ref)
    return pick_low(matmul(columns_ref[...], hot_ref[...], (1, 0)), low)


def side_kernel_inputs(info_ref, side):
    rows = [info_ref[side, i : i + 1, :] for i in range(5)]
    whole = [x.astype(jnp.int32) for x in rows]
    return whole[0], whole[1], rows[2], whole[3], whole[4]


def row_integer(rows_ref, index):
    return rows_ref[index].astype(jnp.int32)


def row_cells(rows_ref):
    return [unstack_lanes(row_integer(rows_ref, index), 1) for index in (4, 5)]


def first_window_kernel(
    relaxation,
    grids_hbm,
    rows_ref,
    partial_ref,
    scaled_ref,
    inverse_ref,
    edges_ref,
    row_partial_ref,
    row_inverse_ref,
    chains_ref,
    matrix_ref,
    source_ref,
    storage_ref,
    hot_ref,
    columns_ref,
    sems,
):
    copies = [
        pltpu.make_async_copy(row_slice(grids_hbm, rows_ref), rows_ref, sems.at[3]),
        pltpu.make_async_copy(grids_hbm.at[2], storage_ref, sems.at[2]),
        pltpu.make_async_copy(grids_hbm.at[1], source_ref, sems.at[1]),
        pltpu.make_async_copy(grids_hbm.at[0], matrix_ref, sems.at[0]),
    ]
    for copy in copies:
        copy.start()
    for copy in copies:
        copy.wait()
    depth, area_rows, cols = matrix_ref.shape
    plane_rows = depth * area_rows
    high, low = row_cells(rows_ref)
    weight = rows_ref[0]
    fill_hot(hot_ref, high)
    added = fold(matmul(hot_ref[...], masked_parts(low, unstack_lanes(weight, 1)), (1, 1)), 0)
    for c in range(cols // LANES):
        lanes = slice(c * LANES, (c + 1) * LANES)
        extra = added[c * plane_rows : (c + 1) * plane_rows].reshape(depth, area_rows, LANES)
        inverse = 1.0 / (6.0 + storage_ref[:, :, lanes] + extra)
        scaled_ref[:, :, lanes] = source_ref[:, :, lanes] * inverse
        inverse_ref[:, :, lanes] = inverse
    row_inverse_ref[...] = weight * stack_lanes(
        pick_cells(inverse_ref, columns_ref, hot_ref, low)
    )
    partial_ref[...] = relaxed(
        matrix_ref[...], scaled_ref[...], inverse_ref[...], None, None, relaxation
    )
    row_partial_ref[...] = weight * stack_lanes(pick_cells(partial_ref, columns_ref, hot_ref, low))
    edges_ref[0] = matrix_ref[:, 0, :]
    edges_ref[1] = matrix_ref[:, area_rows - 1, :]
    chains = find_chains(rows_ref[3])
    for i, x in enumerate(chains):
        chains_ref[i] = x


def row_integer(rows_ref, index):
    return rows_ref[index].astype(jnp.int32)


def row_cells(rows_ref):
    return [unstack_lanes(row_integer(rows_ref, index), 1) for index in (4, 5)]


def both_sides(pair_ref, cross_ref, tiles):
    odd = (lax.axis_index("area") & 1) == 1
    lower = [jnp.where(odd, pair_ref[i], cross_ref[i]) for i in tiles]
    upper = [jnp.where(odd, cross_ref[i], pair_ref[i]) for i in tiles]
    return lower, upper


def beside_rows(pair_ref, cross_ref, rows_ref, area_rows):
    (lower,), (upper,) = both_sides(pair_ref, cross_ref, (0,))
    depth = lower.shape[0]
    high, low = row_cells(rows_ref)
    row = high & (area_rows - 1)
    plane = (high >> log2(area_rows)) & (depth - 1)
    place = (high >> log2(depth * area_rows)) * depth + plane
    table = jnp.concatenate([stack_lanes(lower), stack_lanes(upper)], axis=0)
    place = jnp.where(row == 0, place, place + table.shape[0] // 2)
    place = jnp.where((row == 0) | (row == area_rows - 1), place, -1)
    hot = (iota((table.shape[0], place.shape[1]), 0) == place).astype(F32).astype(BF16)
    columns = jnp.concatenate(halves(table.T), axis=0)
    return stack_lanes(pick_low(matmul(columns, hot, (1, 0)), low))


def add_rows(relaxation, values, partial_ref, inverse_ref, rows_ref, hot_ref, matrix_ref):
    depth, area_rows, cols = partial_ref.shape
    plane_rows = depth * area_rows
    high, low = row_cells(rows_ref)
    fill_hot(hot_ref, high)
    parts = masked_parts(low, unstack_lanes(values, 1))
    added = fold(matmul(hot_ref[...], parts, (1, 1)), 0)
    for c in range(cols // LANES):
        lanes = slice(c * LANES, (c + 1) * LANES)
        extra = added[c * plane_rows : (c + 1) * plane_rows].reshape(depth, area_rows, LANES)
        matrix_ref[:, :, lanes] = (
            partial_ref[:, :, lanes] + (relaxation * inverse_ref[:, :, lanes]) * extra
        )


def returned_values(returned, rows_ref):
    target, rank = row_integer(rows_ref, 1), row_integer(rows_ref, 2)
    return rows_ref[0] * pick_entries(returned, target, rank)


def first_sides(relaxation, pair_ref, cross_ref, edges_ref, scaled_ref, inverse_ref, info_ref):
    depth, cols = edges_ref.shape[1:]
    partial = []
    for side, tiles in enumerate(both_sides(pair_ref, cross_ref, range(3 * HALO + 2))):
        info_ref[side] = tiles[3 * HALO + 1]
        place, low, weight, _, _ = side_kernel_inputs(info_ref, side)
        added = spread_side(place, low, weight, depth, cols // LANES)
        scaled, inverse = [], []
        for far in range(HALO):
            storage = tiles[2 * HALO + 1 + far]
            inverse.append(jnp.where(storage > 0.0, 1.0 / (6.0 + storage + added[far]), 0.0))
            scaled.append(tiles[HALO + 1 + far] * inverse[far])
            scaled_ref[side, far] = scaled[far]
            inverse_ref[side, far] = inverse[far]
        partial.append(
            relaxed_side(
                tiles[:HALO], tiles[HALO], edges_ref[side], scaled, inverse, relaxation
            )
        )
    return partial


def window_kernel(
    relaxation,
    before,
    cap,
    first,
    last,
    arrived_ref,
    partial_before_ref,
    scaled_ref,
    inverse_ref,
    rows_ref,
    slots_ref,
    fracture_ref,
    links_ref,
    link_weights_ref,
    *refs,
):
    depth, area_rows, cols = scaled_ref.shape
    devices = arrived_ref.shape[0]
    half = devices * cap // 2
    if first:
        pair_ref, cross_ref, edges_ref, *refs = refs
        partial_ref, side_partial_ref, link_sum_ref, *refs = refs
        side_scaled_ref, side_inverse_ref, side_info_ref, *refs = refs
    else:
        side_before_ref, side_scaled_ref, side_inverse_ref, side_info_ref, *refs = refs
        partial_ref, side_partial_ref, link_sum_ref, *refs = refs
    if last:
        matrix_ref, hot_ref = refs
    else:
        row_partial_ref, matrix_ref, hot_ref, columns_ref = refs
    returned = device_values(arrived_ref, row_integer(slots_ref, 2)) if first else arrived_ref[:, 1, :]
    values = returned_values(returned, rows_ref)
    add_rows(before, values, partial_before_ref, inverse_ref, rows_ref, hot_ref, matrix_ref)
    if first:
        lower, upper = both_sides(pair_ref, cross_ref, (0,))
        for edge, tile in ((0, lower[0]), (area_rows - 1, upper[0])):
            matrix_ref[:, edge, :] = (
                matrix_ref[:, edge, :] + (before * inverse_ref[:, edge, :]) * tile
            )
        side_before = first_sides(
            before, pair_ref, cross_ref, edges_ref, side_scaled_ref, side_inverse_ref, side_info_ref
        )
    else:
        side_before = [[side_before_ref[side, far] for far in range(HALO)] for side in range(2)]
    edges = []
    for side, edge in enumerate((0, area_rows - 1)):
        place, low, weight, target, rank = side_kernel_inputs(side_info_ref, side)
        if first:
            code = jnp.concatenate(
                [side_info_ref[side, i : i + 1, :half] for i in (5, 6)], axis=1
            )
            code = from_dense(code, devices, cap).astype(jnp.int32)
            returned = device_values(arrived_ref, code)
        else:
            returned = arrived_ref[:, 2 + side, :]
        values = pick_entries(returned, stack_lanes(target), stack_lanes(rank))
        values = weight * unstack_lanes(values, 1)
        added = spread_side(place, low, values, depth, cols // LANES)
        now = [
            side_before[side][far] + before * side_inverse_ref[side, far] * added[far]
            for far in range(HALO)
        ]
        edges.append(now[0])
        after = relaxed_side(
            now,
            None,
            matrix_ref[:, edge, :],
            [side_scaled_ref[side, far] for far in range(HALO)],
            [side_inverse_ref[side, far] for far in range(HALO)],
            relaxation,
        )
        for far in range(HALO):
            side_partial_ref[side, far] = after[far]
    partial_ref[...] = relaxed(
        matrix_ref[...],
        scaled_ref[...],
        inverse_ref[...],
        edges[0],
        edges[1],
        relaxation,
    )
    if not last:
        row_partial_ref[...] = rows_ref[0] * stack_lanes(
            pick_cells(partial_ref, columns_ref, hot_ref, row_cells(rows_ref)[1])
        )
    link_sum_ref[...] = linked(fracture_ref[...], links_ref, link_weights_ref)


def returned_values(returned, rows_ref):
    target, rank = row_integer(rows_ref, 1), row_integer(rows_ref, 2)
    return rows_ref[0] * pick_entries(returned, target, rank)


def row_values(
    relaxation,
    returned,
    slots_ref,
    rows_ref,
    row_partial_ref,
    row_inverse_ref,
    chains_ref,
    beside=None,
):
    total = same_cell_sum(returned_values(returned, rows_ref), chains_ref)
    if beside is not None:
        total = total + beside
    outgoing = row_partial_ref[...] + (relaxation * row_inverse_ref[...]) * total
    return pick_entries(outgoing, row_integer(slots_ref, 0), row_integer(slots_ref, 1))


def node_sums(code, shape, *values):
    owned, blk = shape
    rows = owned * blk // LANES
    member = iota((rows, code.shape[1]), 0) == code >> log2(LANES)
    low = (iota((LANES, code.shape[1]), 0) == code & (LANES - 1)).astype(F32).astype(BF16)
    parts = []
    for value in values:
        high = value.astype(BF16).astype(F32)
        parts += [jnp.where(member, high, 0.0), jnp.where(member, value - high, 0.0)]
    sums = matmul(jnp.concatenate(parts, axis=0).astype(BF16), low, (1, 1))
    sums = [sums[i : i + rows] for i in range(0, sums.shape[0], rows)]
    return [
        unstack_lanes(sums[2 * i] + sums[2 * i + 1], owned) for i in range(len(values))
    ]


def node_values(table, code):
    found = jnp.zeros(code.shape, F32)
    low = code & (LANES - 1)
    for row in range(table.shape[0]):
        values = jnp.broadcast_to(table[row : row + 1], code.shape)
        found = jnp.where(code >> log2(LANES) == row, lane_gather(values, low), found)
    return found


def device_values(arrived_ref, code):
    found = jnp.zeros(code.shape, F32)
    low = code & (LANES - 1)
    for row in range(4 * (arrived_ref.shape[1] - 1)):
        values = lane_gather(arrived_ref[:, 1 + row // 4, row % 4, :], low)
        found = jnp.where(code >> log2(LANES) == row, values, found)
    return found


def put_requested(message_ref, values):
    zero = jnp.zeros((1, LANES), F32)
    order = group_order(values.shape[0])
    rows = {device: values[i : i + 1] for i, device in enumerate(order)}
    message_ref[:, 1, :] = values
    for place, step in ((2, -1), (3, 1)):
        message_ref[:, place, :] = jnp.concatenate(
            [rows.get(device + step, zero) for device in order], axis=0
        )


def first_step_kernel(
    relaxation,
    cap,
    area_rows,
    arrived_ref,
    pair_ref,
    cross_ref,
    slots_ref,
    rows_ref,
    row_partial_ref,
    row_inverse_ref,
    chains_ref,
    fracture_ref,
    link_sum_ref,
    fracture_source_ref,
    leak_ref,
    link_weights_ref,
    fracture_next_ref,
    fracture_inverse_ref,
    node_code_ref,
    message_hbm,
    message_ref,
    sem,
):
    message_ref[:, 0, :] = row_values(
        relaxation,
        device_values(arrived_ref, row_integer(slots_ref, 2)),
        slots_ref,
        rows_ref,
        row_partial_ref,
        row_inverse_ref,
        chains_ref,
        beside_rows(pair_ref, cross_ref, rows_ref, area_rows),
    )
    code = arrived_ref[:, 0, 0, :].astype(jnp.int32)
    node_code_ref[...] = code
    dense = to_dense(code, cap)
    weight_sum, value_sum = node_sums(
        dense,
        fracture_ref.shape,
        to_dense(arrived_ref[:, 0, 1, :], cap),
        to_dense(arrived_ref[:, 0, 2, :], cap),
    )
    diag = leak_ref[...] + jnp.sum(link_weights_ref[...], axis=0) + weight_sum
    inverse = 1.0 / diag
    fracture_inverse_ref[...] = inverse
    fracture_next = (1.0 - relaxation) * fracture_ref[...] + (relaxation * inverse) * (
        fracture_source_ref[...] + link_sum_ref[...] + value_sum
    )
    fracture_next_ref[...] = fracture_next
    put_requested(message_ref, node_values(stack_lanes(fracture_next), code))
    out = pltpu.make_async_copy(message_ref, message_hbm, sem)
    out.start()
    out.wait()


def next_fracture(
    relaxation,
    cap,
    arrived_ref,
    code,
    fracture_ref,
    link_sum_ref,
    fracture_source_ref,
    fracture_inverse_ref,
):
    (value_sum,) = node_sums(
        to_dense(code, cap), fracture_ref.shape, to_dense(arrived_ref[:, 0, :], cap)
    )
    return (1.0 - relaxation) * fracture_ref[...] + (relaxation * fracture_inverse_ref[...]) * (
        fracture_source_ref[...] + link_sum_ref[...] + value_sum
    )


def step_kernel(
    relaxation,
    cap,
    arrived_ref,
    node_code_ref,
    slots_ref,
    rows_ref,
    row_partial_ref,
    row_inverse_ref,
    chains_ref,
    fracture_ref,
    link_sum_ref,
    fracture_source_ref,
    fracture_inverse_ref,
    fracture_next_ref,
    message_hbm,
    message_ref,
    sem,
):
    message_ref[:, 0, :] = row_values(
        relaxation,
        arrived_ref[:, 1, :],
        slots_ref,
        rows_ref,
        row_partial_ref,
        row_inverse_ref,
        chains_ref,
    )
    code = node_code_ref[...]
    fracture_next = next_fracture(
        relaxation,
        cap,
        arrived_ref,
        code,
        fracture_ref,
        link_sum_ref,
        fracture_source_ref,
        fracture_inverse_ref,
    )
    fracture_next_ref[...] = fracture_next
    put_requested(message_ref, node_values(stack_lanes(fracture_next), code))
    out = pltpu.make_async_copy(message_ref, message_hbm, sem)
    out.start()
    out.wait()


def last_step_kernel(
    relaxation,
    cap,
    arrived_ref,
    node_code_ref,
    partial_ref,
    inverse_ref,
    rows_ref,
    fracture_ref,
    link_sum_ref,
    fracture_source_ref,
    fracture_inverse_ref,
    matrix_ref,
    fracture_next_ref,
    hot_ref,
):
    values = returned_values(arrived_ref[:, 1, :], rows_ref)
    add_rows(relaxation, values, partial_ref, inverse_ref, rows_ref, hot_ref, matrix_ref)
    fracture_next_ref[...] = next_fracture(
        relaxation,
        cap,
        arrived_ref,
        node_code_ref[...],
        fracture_ref,
        link_sum_ref,
        fracture_source_ref,
        fracture_inverse_ref,
    )


def call(kernel, outs, ins, name, micros, hbm_in=(), hbm_out=(), scratch=(), aliases=None, limit=VMEM_LIMIT):
    return pl.pallas_call(
        kernel,
        out_shape=[jax.ShapeDtypeStruct(shape, dtype) for shape, dtype in outs],
        in_specs=[
            pl.BlockSpec(memory_space=pltpu.HBM if i in hbm_in else pltpu.VMEM)
            for i in range(len(ins))
        ],
        out_specs=[
            pl.BlockSpec(memory_space=pltpu.HBM if i in hbm_out else pltpu.VMEM)
            for i in range(len(outs))
        ],
        scratch_shapes=list(scratch),
        input_output_aliases=aliases or {},
        compiler_params=pltpu.CompilerParams(vmem_limit_bytes=limit),
        cost_estimate=pl.CostEstimate(
            flops=0, bytes_accessed=int(micros * 3.0e6), transcendentals=0
        ),
        name=name,
    )(*ins)


def local(
    block_owner,
    transfer_cells,
    transfer_nodes,
    transfer_weights,
    row_counts,
    matrix_start,
    matrix_source,
    matrix_storage,
    fracture_start,
    fracture_source,
    fracture_leak,
    fracture_links,
    link_weights,
):
    devices = lax.axis_size("area")
    depth, area_rows, cols = matrix_start.shape
    owned, blk = fracture_start.shape
    total_rows = transfer_cells.shape[0]
    cap = 3 * total_rows // (2 * devices)
    cells = depth * area_rows * cols // LANES
    relax = relax_weights(ITERS)
    grid = (matrix_start.shape, F32)
    grids = ((GRID_SLOTS,) + matrix_start.shape, F32)
    fracture = (fracture_start.shape, F32)
    side = ((3 * HALO + 2, depth, cols), F32)
    sides = ((2, HALO, depth, cols), F32)
    hot = pltpu.VMEM((cells, total_rows), BF16)
    columns = pltpu.VMEM((2 * LANES, cells), BF16)
    padded = (devices, LANES)
    first_message = ((devices, 1 + owned * blk // LANES // 4, 4, LANES), F32)
    message_type = ((devices, 4, LANES), F32)
    pairs, crossings = [
        [(i + a, i + b) for i in range(start, devices - 1, 2) for a, b in ((0, 1), (1, 0))]
        for start in (0, 1)
    ]

    def exchange(message):
        return lax.all_to_all(
            message,
            "area",
            split_axis=0,
            concat_axis=0,
            tiled=True,
            axis_index_groups=[group_order(devices)],
        )

    staged = [
        row_counts.reshape(1, 1),
        block_owner.reshape(-1, LANES),
        transfer_cells.reshape(-1, LANES),
        transfer_nodes.reshape(-1, LANES),
        transfer_weights.reshape(-1, LANES),
        matrix_start,
        fracture_start,
        matrix_source,
        matrix_storage,
        fracture_links,
        link_weights,
    ]
    row_shape = (total_rows // LANES, LANES)
    rows = (row_shape, F32)
    info = ((6,) + row_shape, F32)
    edges = ((2, depth, cols), F32)
    slot_info, message, pair, cross, grids_start, link_sum = call(
        functools.partial(setup_kernel, devices, cap, len(staged)),
        [((3,) + padded, F32), first_message, side, side, grids, fracture],
        staged,
        "place_rows",
        5.0,
        hbm_in=range(len(staged)),
        hbm_out=(1, 2, 3, 4),
        scratch=[pltpu.VMEM(x.shape, x.dtype) for x in staged]
        + [
            pltpu.VMEM(*info),
            pltpu.VMEM(*first_message),
            pltpu.VMEM(*side),
            pltpu.VMEM(*side),
            hot,
            columns,
            pltpu.SemaphoreType.DMA((len(staged) + 7,)),
        ],
        limit=63 * 1024 * 1024,
    )
    arrived = exchange(message)
    pair = lax.ppermute(pair, "area", pairs)
    cross = lax.ppermute(cross, "area", crossings)
    row_info, partial, scaled, inverse, edge_rows, row_partial, row_inverse, chains = call(
        functools.partial(first_window_kernel, relax[0]),
        [info, grid, grid, grid, edges, rows, rows, ((3,) + row_shape, F32)],
        [grids_start],
        "stencil_first",
        4.0,
        hbm_in=(0,),
        scratch=[pltpu.VMEM(*grid)] * 3 + [hot, columns, pltpu.SemaphoreType.DMA((4,))],
    )
    fracture_now = fracture_start
    message_scratch = [pltpu.VMEM(*message_type), pltpu.SemaphoreType.DMA]
    fracture_now, fracture_inverse, node_code, message = call(
        functools.partial(first_step_kernel, relax[0], cap, area_rows),
        [fracture, fracture, (padded, jnp.int32), message_type],
        [
            arrived,
            pair,
            cross,
            slot_info,
            row_info,
            row_partial,
            row_inverse,
            chains,
            fracture_now,
            link_sum,
            fracture_source,
            fracture_leak,
            link_weights,
        ],
        "couple_first",
        2.0,
        hbm_out=(3,),
        scratch=message_scratch,
    )
    for index in range(1, ITERS):
        last = index == ITERS - 1
        old, arrived = arrived, exchange(message)
        first = index == 1
        inputs = [old, partial, scaled, inverse, row_info, slot_info, fracture_now]
        inputs += [fracture_links, link_weights]
        if first:
            inputs += [pair, cross, edge_rows]
        else:
            inputs += [side_partial, side_scaled, side_inverse, side_info]
        outs = call(
            functools.partial(window_kernel, relax[index], relax[index - 1], cap, first, last),
            [grid, sides, fracture]
            + ([sides, sides, edges] if first else [])
            + ([] if last else [rows]),
            inputs,
            "stencil",
            3.0,
            aliases={1: 0} if first else {1: 0, 9: 1},
            scratch=[pltpu.VMEM(*grid), hot] + ([] if last else [columns]),
        )
        partial, side_partial, link_sum = outs[:3]
        if first:
            side_scaled, side_inverse, side_info = outs[3:6]
        fractures = [fracture_now, link_sum, fracture_source, fracture_inverse]
        if last:
            return call(
                functools.partial(last_step_kernel, relax[index], cap),
                [grid, fracture],
                [arrived, node_code, partial, inverse, row_info] + fractures,
                "couple_last",
                2.0,
                scratch=[hot],
            )
        row_partial = outs[-1]
        fracture_now, message = call(
            functools.partial(step_kernel, relax[index], cap),
            [fracture, message_type],
            [arrived, node_code, slot_info, row_info, row_partial, row_inverse, chains]
            + fractures,
            "couple",
            2.0,
            hbm_out=(1,),
            scratch=message_scratch,
        )


def solution(mesh):
    in_specs = (
        P(),
        P("area"),
        P("area"),
        P("area"),
        P("area"),
        P("real", "area", None),
        P("real", "area", None),
        P("real", "area", None),
        P("area", "real"),
        P("area", "real"),
        P("area", "real"),
        P(None, "area", None),
        P("real", "area", None),
    )
    out_specs = (P("real", "area", None), P("area", "real"))
    return jax.shard_map(local, mesh=mesh, in_specs=in_specs, out_specs=out_specs, check_vma=False)
```

```python
import functools
import math

import jax
import jax.numpy as jnp
from jax import lax
from jax.experimental import pallas as pl
from jax.experimental.pallas import tpu as pltpu
from jax.sharding import PartitionSpec as P

ITERS = 4
HALO = ITERS - 1
GRID_SLOTS = 72
LANES = 128
F32 = jnp.float32
BF16 = jnp.bfloat16
VMEM_LIMIT = 32 * 1024 * 1024


def relax_weights(steps_total):
    return [
        1.0 / (1.0 + 0.75 * math.cos(math.pi * (2 * index + 1) / (2 * steps_total)))
        for index in range(steps_total)
    ]


def log2(value):
    assert value & (value - 1) == 0
    return value.bit_length() - 1


def group_order(devices):
    part = devices // 4
    return [part * z + i for i in reversed(range(part)) for z in (2, 0, 1, 3)]


def iota(shape, dim):
    return lax.broadcasted_iota(jnp.int32, shape, dim)


def halves(x):
    high = x.astype(BF16)
    low = (x - high.astype(F32)).astype(BF16)
    return high, low


def matmul(a, b, contract):
    return lax.dot_general(a, b, ((contract[:1], contract[1:]), ((), ())), preferred_element_type=F32)


def to_dense(x, cap):
    return jnp.concatenate([x[i : i + 1, :cap] for i in range(x.shape[0])], axis=1)


def from_dense(x, devices, cap):
    rows = jnp.concatenate([x[:, i * cap : (i + 1) * cap] for i in range(devices)], axis=0)
    return jnp.concatenate([rows, jnp.zeros((devices, LANES - cap), x.dtype)], axis=1)


def lane_gather(table, index):
    return jnp.take_along_axis(table, index, axis=1, mode="promise_in_bounds")


def masked_parts(low, *values):
    mask = iota((LANES, low.shape[1]), 0) == low
    zero = jnp.zeros((), F32)
    parts = []
    for value in values:
        high = value.astype(BF16).astype(F32)
        parts.append(jnp.where(mask, high, zero).astype(BF16))
        parts.append(jnp.where(mask, value - high, zero).astype(BF16))
    return jnp.concatenate(parts, axis=0)


def fold(wide, index):
    start = 2 * index * LANES
    return wide[:, start : start + LANES] + wide[:, start + LANES : start + 2 * LANES]


def pick_low(tall, low):
    both = tall[:LANES] + tall[LANES:]
    return jnp.sum(
        jnp.where(iota(both.shape, 0) == low, both, 0.0), axis=0, keepdims=True
    )


def stack_lanes(x):
    return jnp.concatenate(
        [x[:, i * LANES : (i + 1) * LANES] for i in range(x.shape[1] // LANES)], axis=0
    )


def unstack_lanes(x, rows):
    return jnp.concatenate([x[i : i + rows] for i in range(0, x.shape[0], rows)], axis=1)


def put_columns(chunk, index, columns_ref):
    high, low = halves(chunk.T)
    columns_ref[:LANES, index * LANES : (index + 1) * LANES] = high
    columns_ref[LANES:, index * LANES : (index + 1) * LANES] = low


def fill_hot(hot_ref, high):
    for start in range(0, hot_ref.shape[0], LANES):
        rows = iota((LANES, high.shape[1]), 0) + start
        hot_ref[start : start + LANES, :] = (rows == high).astype(F32).astype(BF16)


def pick_entries(table, row, lane):
    found = jnp.zeros(row.shape, table.dtype)
    for i in range(table.shape[0]):
        values = jnp.broadcast_to(table[i : i + 1], row.shape)
        found = jnp.where(row == i, lane_gather(values, lane), found)
    return found


def row_slice(grids_hbm, rows_ref):
    count, groups, lanes = rows_ref.shape
    return grids_hbm.at[3, :count, :groups, :lanes]


def setup_kernel(devices, cap, staged, *refs):
    sources, refs = refs[:staged], refs[staged:]
    slots_ref, message_hbm, pair_hbm, cross_hbm, grids_hbm, link_sum_ref = refs[:6]
    targets, refs = refs[6 : 6 + staged], refs[6 + staged :]
    rows_ref, message_ref, pair_ref, cross_ref, hot_ref, columns_ref, sems = refs
    copies = [
        pltpu.make_async_copy(sources[i], targets[i], sems.at[i]) for i in range(staged)
    ]
    kept = [
        pltpu.make_async_copy(targets[i], grids_hbm.at[j], sems.at[staged + 3 + j])
        for j, i in enumerate((5, 7, 8))
    ]
    kept.append(pltpu.make_async_copy(rows_ref, row_slice(grids_hbm, rows_ref), sems.at[staged + 6]))
    for copy in copies:
        copy.start()
    for copy in copies[:5]:
        copy.wait()
    counts_ref, owner_ref, cells_ref, nodes_ref, weights_ref = targets[:5]
    matrix_ref, fracture_ref, source_ref, storage_ref, links_ref, link_weights_ref = targets[5:]
    owned, blk = fracture_ref.shape
    depth, area_rows, cols = matrix_ref.shape
    groups = cells_ref.shape[0]
    plane_rows = depth * area_rows
    shape = (groups, LANES)
    nodes, cells = nodes_ref[...], cells_ref[...]
    live = iota(shape, 0) * LANES + iota(shape, 1) < counts_ref[...]
    weight = jnp.where(live, weights_ref[...], 0.0)
    block = nodes >> log2(blk)
    slot = jnp.zeros(shape, jnp.int32)
    for part in range(owner_ref.shape[0]):
        table = jnp.broadcast_to(owner_ref[part : part + 1, :], shape)
        found = lane_gather(table, block & (LANES - 1))
        slot = jnp.where(block >> log2(LANES) == part, found, slot)
    device = slot >> log2(owned)
    target = jnp.zeros(shape, jnp.int32)
    for position, place in enumerate(group_order(devices)):
        target = jnp.where(device == place, position, target)
    target = jnp.where(live, target, -1)
    node_high = ((nodes & (blk - 1)) >> log2(LANES)) * owned + (slot & (owned - 1))
    node_low = nodes & (LANES - 1)
    plane_row = cells >> log2(cols)
    cell_group = (cells & (cols - 1)) >> log2(LANES)
    cell_high = cell_group * plane_rows + plane_row
    cell_low = cells & (LANES - 1)
    high, low = unstack_lanes(cell_high, 1), unstack_lanes(cell_low, 1)
    row_weight = unstack_lanes(weight, 1)
    fill_hot(hot_ref, high)

    device_rows = iota((devices, LANES), 0)
    member = [(device_rows == target[q : q + 1]).astype(F32) for q in range(groups)]
    earlier = (iota((LANES, LANES), 0) < iota((LANES, LANES), 1)).astype(F32).astype(BF16)
    counted = matmul(jnp.concatenate(member, axis=0).astype(BF16), earlier, (1, 0))
    before = jnp.zeros((devices, 1), F32)
    rank = []
    for q in range(groups):
        inside = counted[q * devices : (q + 1) * devices] + before
        rank.append(jnp.sum(member[q] * inside, axis=0, keepdims=True).astype(jnp.int32))
        before = before + jnp.sum(member[q], axis=1, keepdims=True)
    rank_row = jnp.concatenate(rank, axis=1)
    rank = jnp.concatenate(rank, axis=0)
    member = jnp.concatenate(member, axis=1)

    first = weight.astype(BF16).astype(F32)
    second = (weight - first).astype(BF16).astype(F32)
    features = [
        jnp.ones(shape, F32),
        node_high.astype(F32),
        node_low.astype(F32),
        first,
        second,
        weight - first - second,
        iota(shape, 0).astype(F32),
        iota(shape, 1).astype(F32),
    ]
    features = [member * unstack_lanes(x, 1) for x in features]
    ranked = (iota((LANES, groups * LANES), 0) == rank_row).astype(F32).astype(BF16)
    packed = matmul(jnp.concatenate(features, axis=0).astype(BF16), ranked, (1, 1))
    packed = [packed[i * devices : (i + 1) * devices] for i in range(len(features))]
    code = jnp.where(packed[0] > 0.5, packed[1] * LANES + packed[2], -1.0)
    slot_row, slot_lane = packed[6].astype(jnp.int32), packed[7].astype(jnp.int32)
    slots_ref[0], slots_ref[1], slots_ref[2] = packed[6], packed[7], code
    alone = -1 - iota(shape, 0) * LANES - iota(shape, 1)
    cell = jnp.where(live, cells, alone)
    for i, x in enumerate((weight, target, rank, cell, cell_high, cell_low)):
        rows_ref[i] = x.astype(F32)
    kept[3].start()
    message_ref[:, 0, 0, :] = code
    message_ref[:, 0, 1, :] = packed[3] + packed[4] + packed[5]
    message_ref[:, 0, 3, :] = jnp.zeros((devices, LANES), F32)

    odd = (lax.axis_index("area") & 1) == 1
    plane = plane_row >> log2(area_rows)
    row = plane_row & (area_rows - 1)
    places = []
    for far in (area_rows - 1 - row, row):
        place = (cell_group * HALO + far) * depth + plane
        places.append(jnp.where(live & (far < HALO), place, -1).astype(F32))
    info = [low, row_weight, unstack_lanes(target, 1), unstack_lanes(rank, 1)]
    info = [x.astype(F32) for x in info]
    dense = to_dense(code, cap)
    half = dense.shape[1] // 2
    for ref, place in (
        (pair_ref, jnp.where(odd, places[1], places[0])),
        (cross_ref, jnp.where(odd, places[0], places[1])),
    ):
        tile = ref.at[3 * HALO]
        for i, x in enumerate([unstack_lanes(place, 1)] + info):
            tile[i : i + 1, :] = x
        tile[5:6, :half] = dense[:, :half]
        tile[6:7, :half] = dense[:, half:]

    for copy in copies[5:]:
        copy.wait()
    for copy in kept[:3]:
        copy.start()
    link_sum_ref[...] = linked(fracture_ref[...], links_ref, link_weights_ref)
    node_table = stack_lanes(fracture_ref[...])
    for i in range(node_table.shape[0]):
        message_ref[:, 1 + i // 4, i % 4, :] = jnp.broadcast_to(
            node_table[i : i + 1], (devices, LANES)
        )
    for part, ref in enumerate((matrix_ref, source_ref, storage_ref)):
        for far in range(HALO):
            up = ref[:, area_rows - 1 - far, :]
            down = ref[:, far, :]
            if part == 1 and far == HALO - 1:
                up = up + matrix_ref[:, area_rows - 1 - HALO, :]
                down = down + matrix_ref[:, HALO, :]
            pair_ref[part * HALO + far] = jnp.where(odd, down, up)
            cross_ref[part * HALO + far] = jnp.where(odd, up, down)
    outs = [
        pltpu.make_async_copy(pair_ref, pair_hbm, sems.at[staged]),
        pltpu.make_async_copy(cross_ref, cross_hbm, sems.at[staged + 1]),
        pltpu.make_async_copy(message_ref, message_hbm, sems.at[staged + 2]),
    ]
    outs[0].start()
    outs[1].start()
    picked = stack_lanes(pick_cells(matrix_ref, columns_ref, hot_ref, low))
    message_ref[:, 0, 2, :] = pick_entries(weight * picked, slot_row, slot_lane)
    outs[2].start()
    for out in outs + kept:
        out.wait()


def turned(rows):
    count = rows.shape[0]
    extra = -count % 8
    if extra:
        rows = jnp.concatenate([rows, jnp.zeros((extra, LANES), rows.dtype)], axis=0)
    return rows.T


def find_chains(cells):
    blocks = cells.shape[0]
    columns = turned(cells)
    none = float(blocks * LANES)
    sublane, lane = iota((LANES, LANES), 0), iota((LANES, LANES), 1)
    after = [jnp.full((8, LANES), none, F32) for _ in range(blocks)]
    before = [jnp.full((8, LANES), -1.0, F32) for _ in range(blocks)]
    count = [jnp.zeros((8, LANES), F32) for _ in range(blocks)]
    for j in range(blocks):
        cell = jnp.broadcast_to(columns[:, j : j + 1], (LANES, LANES))
        place = (sublane + j * LANES).astype(F32)
        for i in range(blocks):
            same = cell == cells[i : i + 1]
            parts = (LANES // 8, 8, LANES)
            ones = jnp.where(same, 1.0, 0.0).reshape(parts)
            count[i] = count[i] + jnp.sum(ones, axis=0)
            if j >= i:
                later = same & (sublane > lane) if j == i else same
                found = jnp.where(later, place, none).reshape(parts)
                after[i] = jnp.minimum(after[i], jnp.min(found, axis=0))
            if j <= i:
                sooner = same & (sublane < lane) if j == i else same
                found = jnp.where(sooner, place, -1.0).reshape(parts)
                before[i] = jnp.maximum(before[i], jnp.max(found, axis=0))
    after = jnp.concatenate([jnp.min(x, axis=0, keepdims=True) for x in after], axis=0)
    before = jnp.concatenate([jnp.max(x, axis=0, keepdims=True) for x in before], axis=0)
    count = jnp.concatenate([jnp.sum(x, axis=0, keepdims=True) for x in count], axis=0)
    return jnp.where(after < none, after, -1.0), before, count


def same_cell_sum(values, chains_ref):
    most = jnp.max(chains_ref[2]).astype(jnp.int32)
    rounds = log2(values.size)
    steps = sum((most > (1 << i)).astype(jnp.int32) for i in range(rounds))

    def step(_, state):
        after = []
        for total, link in (state[:2], state[2:]):
            row, lane = (link - 1) >> log2(LANES), (link - 1) & (LANES - 1)
            after += [total + pick_entries(total, row, lane), pick_entries(link, row, lane)]
        return tuple(after)

    ahead, behind = [row_integer(chains_ref, i) + 1 for i in range(2)]
    ahead, _, behind, _ = lax.fori_loop(0, steps, step, (values, ahead, values, behind))
    return ahead + behind - values


def relaxed(now, source, inverse, low_side, high_side, relaxation):
    depth, rows, cols = now.shape
    zero_plane = jnp.zeros((1, rows, cols), F32)
    beside = jnp.concatenate([now[1:], zero_plane], axis=0)
    beside = beside + jnp.concatenate([zero_plane, now[:-1]], axis=0)
    zero_row = jnp.zeros((depth, 1, cols), F32)
    above = zero_row if high_side is None else high_side[:, None]
    below = zero_row if low_side is None else low_side[:, None]
    beside = beside + jnp.concatenate([now[:, 1:], above], axis=1)
    beside = beside + jnp.concatenate([below, now[:, :-1]], axis=1)
    flat = now.reshape(depth * rows, cols)
    place = iota(flat.shape, 1)
    left = jnp.where(place == 0, 0.0, pltpu.roll(flat, 1, 1))
    right = jnp.where(place == cols - 1, 0.0, pltpu.roll(flat, cols - 1, 1))
    beside = beside + (left + right).reshape(now.shape)
    return (1.0 - relaxation) * now + relaxation * (source + inverse * beside)


def linked(fracture, links_ref, link_weights_ref):
    total = jnp.zeros(fracture.shape, F32)
    width = fracture.shape[1]
    tables = [fracture[:, i : i + LANES] for i in range(0, width, LANES)]
    sums = []
    for start in range(0, width, LANES):
        total = jnp.zeros(tables[0].shape, F32)
        for j in range(links_ref.shape[0]):
            link = links_ref[j, :, start : start + LANES]
            found = jnp.zeros(tables[0].shape, F32)
            for i, table in enumerate(tables):
                found = jnp.where(
                    link >> log2(LANES) == i, lane_gather(table, link & (LANES - 1)), found
                )
            total = total + link_weights_ref[j, :, start : start + LANES] * found
        sums.append(total)
    return jnp.concatenate(sums, axis=1)


def relaxed_side(now, edge, scaled, inverse, relaxation):
    depth, cols = edge.shape
    place = iota(edge.shape, 1)
    zero_plane = jnp.zeros((1, cols), F32)
    after = []
    for far in range(HALO):
        here = now[far]
        beside = jnp.concatenate([here[1:], zero_plane], axis=0)
        beside = beside + jnp.concatenate([zero_plane, here[:-1]], axis=0)
        beside = beside + jnp.where(place == 0, 0.0, pltpu.roll(here, 1, 1))
        beside = beside + jnp.where(place == cols - 1, 0.0, pltpu.roll(here, cols - 1, 1))
        beside = beside + (edge if far == 0 else now[far - 1])
        if far + 1 < HALO:
            beside = beside + now[far + 1]
        after.append(
            (1.0 - relaxation) * here + relaxation * (scaled[far] + inverse[far] * beside)
        )
    return after


def spread_side(place, low, values, depth, col_groups):
    rows = iota((col_groups * HALO * depth, place.shape[1]), 0)
    hot = (rows == place).astype(F32).astype(BF16)
    added = fold(matmul(hot, masked_parts(low, values), (1, 1)), 0)
    return [
        jnp.concatenate(
            [
                added[(group * HALO + far) * depth : (group * HALO + far + 1) * depth]
                for group in range(col_groups)
            ],
            axis=1,
        )
        for far in range(HALO)
    ]


def pick_cells(table_ref, columns_ref, hot_ref, low):
    depth, area_rows, cols = table_ref.shape
    for c in range(cols // LANES):
        chunk = table_ref[:, :, c * LANES : (c + 1) * LANES]
        put_columns(chunk.reshape(depth * area_rows, LANES), c, columns_ref)
    return pick_low(matmul(columns_ref[...], hot_ref[...], (1, 0)), low)


def side_kernel_inputs(info_ref, side):
    rows = [info_ref[side, i : i + 1, :] for i in range(5)]
    whole = [x.astype(jnp.int32) for x in rows]
    return whole[0], whole[1], rows[2], whole[3], whole[4]


def row_integer(rows_ref, index):
    return rows_ref[index].astype(jnp.int32)


def row_cells(rows_ref):
    return [unstack_lanes(row_integer(rows_ref, index), 1) for index in (4, 5)]


def first_window_kernel(
    relaxation,
    grids_hbm,
    rows_ref,
    partial_ref,
    scaled_ref,
    inverse_ref,
    edges_ref,
    row_partial_ref,
    row_inverse_ref,
    chains_ref,
    matrix_ref,
    source_ref,
    storage_ref,
    hot_ref,
    columns_ref,
    sems,
):
    copies = [
        pltpu.make_async_copy(row_slice(grids_hbm, rows_ref), rows_ref, sems.at[3]),
        pltpu.make_async_copy(grids_hbm.at[2], storage_ref, sems.at[2]),
        pltpu.make_async_copy(grids_hbm.at[1], source_ref, sems.at[1]),
        pltpu.make_async_copy(grids_hbm.at[0], matrix_ref, sems.at[0]),
    ]
    for copy in copies:
        copy.start()
    for copy in copies:
        copy.wait()
    depth, area_rows, cols = matrix_ref.shape
    plane_rows = depth * area_rows
    high, low = row_cells(rows_ref)
    weight = rows_ref[0]
    fill_hot(hot_ref, high)
    added = fold(matmul(hot_ref[...], masked_parts(low, unstack_lanes(weight, 1)), (1, 1)), 0)
    for c in range(cols // LANES):
        lanes = slice(c * LANES, (c + 1) * LANES)
        extra = added[c * plane_rows : (c + 1) * plane_rows].reshape(depth, area_rows, LANES)
        inverse = 1.0 / (6.0 + storage_ref[:, :, lanes] + extra)
        scaled_ref[:, :, lanes] = source_ref[:, :, lanes] * inverse
        inverse_ref[:, :, lanes] = inverse
    row_inverse_ref[...] = weight * stack_lanes(
        pick_cells(inverse_ref, columns_ref, hot_ref, low)
    )
    partial_ref[...] = relaxed(
        matrix_ref[...], scaled_ref[...], inverse_ref[...], None, None, relaxation
    )
    row_partial_ref[...] = weight * stack_lanes(pick_cells(partial_ref, columns_ref, hot_ref, low))
    edges_ref[0] = matrix_ref[:, 0, :]
    edges_ref[1] = matrix_ref[:, area_rows - 1, :]
    chains = find_chains(rows_ref[3])
    for i, x in enumerate(chains):
        chains_ref[i] = x


def row_integer(rows_ref, index):
    return rows_ref[index].astype(jnp.int32)


def row_cells(rows_ref):
    return [unstack_lanes(row_integer(rows_ref, index), 1) for index in (4, 5)]


def both_sides(pair_ref, cross_ref, tiles):
    odd = (lax.axis_index("area") & 1) == 1
    lower = [jnp.where(odd, pair_ref[i], cross_ref[i]) for i in tiles]
    upper = [jnp.where(odd, cross_ref[i], pair_ref[i]) for i in tiles]
    return lower, upper


def beside_rows(pair_ref, cross_ref, rows_ref, area_rows):
    (lower,), (upper,) = both_sides(pair_ref, cross_ref, (0,))
    depth = lower.shape[0]
    high, low = row_cells(rows_ref)
    row = high & (area_rows - 1)
    plane = (high >> log2(area_rows)) & (depth - 1)
    place = (high >> log2(depth * area_rows)) * depth + plane
    table = jnp.concatenate([stack_lanes(lower), stack_lanes(upper)], axis=0)
    place = jnp.where(row == 0, place, place + table.shape[0] // 2)
    place = jnp.where((row == 0) | (row == area_rows - 1), place, -1)
    hot = (iota((table.shape[0], place.shape[1]), 0) == place).astype(F32).astype(BF16)
    columns = jnp.concatenate(halves(table.T), axis=0)
    return stack_lanes(pick_low(matmul(columns, hot, (1, 0)), low))


def add_rows(relaxation, values, partial_ref, inverse_ref, rows_ref, hot_ref, matrix_ref):
    depth, area_rows, cols = partial_ref.shape
    plane_rows = depth * area_rows
    high, low = row_cells(rows_ref)
    fill_hot(hot_ref, high)
    parts = masked_parts(low, unstack_lanes(values, 1))
    added = fold(matmul(hot_ref[...], parts, (1, 1)), 0)
    for c in range(cols // LANES):
        lanes = slice(c * LANES, (c + 1) * LANES)
        extra = added[c * plane_rows : (c + 1) * plane_rows].reshape(depth, area_rows, LANES)
        matrix_ref[:, :, lanes] = (
            partial_ref[:, :, lanes] + (relaxation * inverse_ref[:, :, lanes]) * extra
        )


def returned_values(returned, rows_ref):
    target, rank = row_integer(rows_ref, 1), row_integer(rows_ref, 2)
    return rows_ref[0] * pick_entries(returned, target, rank)


def first_sides(relaxation, pair_ref, cross_ref, edges_ref, scaled_ref, inverse_ref, info_ref):
    depth, cols = edges_ref.shape[1:]
    partial = []
    for side, tiles in enumerate(both_sides(pair_ref, cross_ref, range(3 * HALO + 1))):
        info_ref[side] = tiles[3 * HALO]
        place, low, weight, _, _ = side_kernel_inputs(info_ref, side)
        added = spread_side(place, low, weight, depth, cols // LANES)
        scaled, inverse = [], []
        for far in range(HALO):
            storage = tiles[2 * HALO + far]
            inverse.append(jnp.where(storage > 0.0, 1.0 / (6.0 + storage + added[far]), 0.0))
            scaled.append(tiles[HALO + far] * inverse[far])
            scaled_ref[side, far] = scaled[far]
            inverse_ref[side, far] = inverse[far]
        partial.append(
            relaxed_side(tiles[:HALO], edges_ref[side], scaled, inverse, relaxation)
        )
    return partial


def window_kernel(
    relaxation,
    before,
    cap,
    first,
    last,
    arrived_ref,
    partial_before_ref,
    scaled_ref,
    inverse_ref,
    rows_ref,
    slots_ref,
    fracture_ref,
    links_ref,
    link_weights_ref,
    *refs,
):
    depth, area_rows, cols = scaled_ref.shape
    devices = arrived_ref.shape[0]
    half = devices * cap // 2
    if first:
        pair_ref, cross_ref, edges_ref, *refs = refs
        partial_ref, side_partial_ref, link_sum_ref, *refs = refs
        side_scaled_ref, side_inverse_ref, side_info_ref, *refs = refs
    else:
        side_before_ref, side_scaled_ref, side_inverse_ref, side_info_ref, *refs = refs
        partial_ref, side_partial_ref, link_sum_ref, *refs = refs
    if last:
        matrix_ref, hot_ref = refs
    else:
        row_partial_ref, matrix_ref, hot_ref, columns_ref = refs
    returned = device_values(arrived_ref, row_integer(slots_ref, 2)) if first else arrived_ref[:, 1, :]
    values = returned_values(returned, rows_ref)
    add_rows(before, values, partial_before_ref, inverse_ref, rows_ref, hot_ref, matrix_ref)
    if first:
        lower, upper = both_sides(pair_ref, cross_ref, (0,))
        for edge, tile in ((0, lower[0]), (area_rows - 1, upper[0])):
            matrix_ref[:, edge, :] = (
                matrix_ref[:, edge, :] + (before * inverse_ref[:, edge, :]) * tile
            )
        side_before = first_sides(
            before, pair_ref, cross_ref, edges_ref, side_scaled_ref, side_inverse_ref, side_info_ref
        )
    else:
        side_before = [[side_before_ref[side, far] for far in range(HALO)] for side in range(2)]
    edges = []
    for side, edge in enumerate((0, area_rows - 1)):
        place, low, weight, target, rank = side_kernel_inputs(side_info_ref, side)
        if first:
            code = jnp.concatenate(
                [side_info_ref[side, i : i + 1, :half] for i in (5, 6)], axis=1
            )
            code = from_dense(code, devices, cap).astype(jnp.int32)
            returned = device_values(arrived_ref, code)
        else:
            returned = arrived_ref[:, 2 + side, :]
        values = pick_entries(returned, stack_lanes(target), stack_lanes(rank))
        values = weight * unstack_lanes(values, 1)
        added = spread_side(place, low, values, depth, cols // LANES)
        now = [
            side_before[side][far] + before * side_inverse_ref[side, far] * added[far]
            for far in range(HALO)
        ]
        edges.append(now[0])
        after = relaxed_side(
            now,
            matrix_ref[:, edge, :],
            [side_scaled_ref[side, far] for far in range(HALO)],
            [side_inverse_ref[side, far] for far in range(HALO)],
            relaxation,
        )
        for far in range(HALO):
            side_partial_ref[side, far] = after[far]
    partial_ref[...] = relaxed(
        matrix_ref[...],
        scaled_ref[...],
        inverse_ref[...],
        edges[0],
        edges[1],
        relaxation,
    )
    if not last:
        row_partial_ref[...] = rows_ref[0] * stack_lanes(
            pick_cells(partial_ref, columns_ref, hot_ref, row_cells(rows_ref)[1])
        )
    link_sum_ref[...] = linked(fracture_ref[...], links_ref, link_weights_ref)


def returned_values(returned, rows_ref):
    target, rank = row_integer(rows_ref, 1), row_integer(rows_ref, 2)
    return rows_ref[0] * pick_entries(returned, target, rank)


def row_values(
    relaxation,
    returned,
    slots_ref,
    rows_ref,
    row_partial_ref,
    row_inverse_ref,
    chains_ref,
    beside=None,
):
    total = same_cell_sum(returned_values(returned, rows_ref), chains_ref)
    if beside is not None:
        total = total + beside
    outgoing = row_partial_ref[...] + (relaxation * row_inverse_ref[...]) * total
    return pick_entries(outgoing, row_integer(slots_ref, 0), row_integer(slots_ref, 1))


def node_sums(code, shape, *values):
    owned, blk = shape
    rows = owned * blk // LANES
    member = iota((rows, code.shape[1]), 0) == code >> log2(LANES)
    low = (iota((LANES, code.shape[1]), 0) == code & (LANES - 1)).astype(F32).astype(BF16)
    parts = []
    for value in values:
        high = value.astype(BF16).astype(F32)
        parts += [jnp.where(member, high, 0.0), jnp.where(member, value - high, 0.0)]
    sums = matmul(jnp.concatenate(parts, axis=0).astype(BF16), low, (1, 1))
    sums = [sums[i : i + rows] for i in range(0, sums.shape[0], rows)]
    return [
        unstack_lanes(sums[2 * i] + sums[2 * i + 1], owned) for i in range(len(values))
    ]


def node_values(table, code):
    found = jnp.zeros(code.shape, F32)
    low = code & (LANES - 1)
    for row in range(table.shape[0]):
        values = jnp.broadcast_to(table[row : row + 1], code.shape)
        found = jnp.where(code >> log2(LANES) == row, lane_gather(values, low), found)
    return found


def device_values(arrived_ref, code):
    found = jnp.zeros(code.shape, F32)
    low = code & (LANES - 1)
    for row in range(4 * (arrived_ref.shape[1] - 1)):
        values = lane_gather(arrived_ref[:, 1 + row // 4, row % 4, :], low)
        found = jnp.where(code >> log2(LANES) == row, values, found)
    return found


def put_requested(message_ref, values):
    zero = jnp.zeros((1, LANES), F32)
    order = group_order(values.shape[0])
    rows = {device: values[i : i + 1] for i, device in enumerate(order)}
    message_ref[:, 1, :] = values
    for place, step in ((2, -1), (3, 1)):
        message_ref[:, place, :] = jnp.concatenate(
            [rows.get(device + step, zero) for device in order], axis=0
        )


def first_step_kernel(
    relaxation,
    cap,
    area_rows,
    arrived_ref,
    pair_ref,
    cross_ref,
    slots_ref,
    rows_ref,
    row_partial_ref,
    row_inverse_ref,
    chains_ref,
    fracture_ref,
    link_sum_ref,
    fracture_source_ref,
    leak_ref,
    link_weights_ref,
    fracture_next_ref,
    fracture_inverse_ref,
    node_code_ref,
    message_hbm,
    message_ref,
    sem,
):
    message_ref[:, 0, :] = row_values(
        relaxation,
        device_values(arrived_ref, row_integer(slots_ref, 2)),
        slots_ref,
        rows_ref,
        row_partial_ref,
        row_inverse_ref,
        chains_ref,
        beside_rows(pair_ref, cross_ref, rows_ref, area_rows),
    )
    code = arrived_ref[:, 0, 0, :].astype(jnp.int32)
    node_code_ref[...] = code
    dense = to_dense(code, cap)
    weight_sum, value_sum = node_sums(
        dense,
        fracture_ref.shape,
        to_dense(arrived_ref[:, 0, 1, :], cap),
        to_dense(arrived_ref[:, 0, 2, :], cap),
    )
    diag = leak_ref[...] + jnp.sum(link_weights_ref[...], axis=0) + weight_sum
    inverse = 1.0 / diag
    fracture_inverse_ref[...] = inverse
    fracture_next = (1.0 - relaxation) * fracture_ref[...] + (relaxation * inverse) * (
        fracture_source_ref[...] + link_sum_ref[...] + value_sum
    )
    fracture_next_ref[...] = fracture_next
    put_requested(message_ref, node_values(stack_lanes(fracture_next), code))
    out = pltpu.make_async_copy(message_ref, message_hbm, sem)
    out.start()
    out.wait()


def next_fracture(
    relaxation,
    cap,
    arrived_ref,
    code,
    fracture_ref,
    link_sum_ref,
    fracture_source_ref,
    fracture_inverse_ref,
):
    (value_sum,) = node_sums(
        to_dense(code, cap), fracture_ref.shape, to_dense(arrived_ref[:, 0, :], cap)
    )
    return (1.0 - relaxation) * fracture_ref[...] + (relaxation * fracture_inverse_ref[...]) * (
        fracture_source_ref[...] + link_sum_ref[...] + value_sum
    )


def step_kernel(
    relaxation,
    cap,
    arrived_ref,
    node_code_ref,
    slots_ref,
    rows_ref,
    row_partial_ref,
    row_inverse_ref,
    chains_ref,
    fracture_ref,
    link_sum_ref,
    fracture_source_ref,
    fracture_inverse_ref,
    fracture_next_ref,
    message_hbm,
    message_ref,
    sem,
):
    message_ref[:, 0, :] = row_values(
        relaxation,
        arrived_ref[:, 1, :],
        slots_ref,
        rows_ref,
        row_partial_ref,
        row_inverse_ref,
        chains_ref,
    )
    code = node_code_ref[...]
    fracture_next = next_fracture(
        relaxation,
        cap,
        arrived_ref,
        code,
        fracture_ref,
        link_sum_ref,
        fracture_source_ref,
        fracture_inverse_ref,
    )
    fracture_next_ref[...] = fracture_next
    put_requested(message_ref, node_values(stack_lanes(fracture_next), code))
    out = pltpu.make_async_copy(message_ref, message_hbm, sem)
    out.start()
    out.wait()


def last_step_kernel(
    relaxation,
    cap,
    arrived_ref,
    node_code_ref,
    partial_ref,
    inverse_ref,
    rows_ref,
    fracture_ref,
    link_sum_ref,
    fracture_source_ref,
    fracture_inverse_ref,
    matrix_ref,
    fracture_next_ref,
    hot_ref,
):
    values = returned_values(arrived_ref[:, 1, :], rows_ref)
    add_rows(relaxation, values, partial_ref, inverse_ref, rows_ref, hot_ref, matrix_ref)
    fracture_next_ref[...] = next_fracture(
        relaxation,
        cap,
        arrived_ref,
        node_code_ref[...],
        fracture_ref,
        link_sum_ref,
        fracture_source_ref,
        fracture_inverse_ref,
    )


def call(kernel, outs, ins, name, micros, hbm_in=(), hbm_out=(), scratch=(), aliases=None, limit=VMEM_LIMIT):
    return pl.pallas_call(
        kernel,
        out_shape=[jax.ShapeDtypeStruct(shape, dtype) for shape, dtype in outs],
        in_specs=[
            pl.BlockSpec(memory_space=pltpu.HBM if i in hbm_in else pltpu.VMEM)
            for i in range(len(ins))
        ],
        out_specs=[
            pl.BlockSpec(memory_space=pltpu.HBM if i in hbm_out else pltpu.VMEM)
            for i in range(len(outs))
        ],
        scratch_shapes=list(scratch),
        input_output_aliases=aliases or {},
        compiler_params=pltpu.CompilerParams(vmem_limit_bytes=limit),
        cost_estimate=pl.CostEstimate(
            flops=0, bytes_accessed=int(micros * 3.0e6), transcendentals=0
        ),
        name=name,
    )(*ins)


def local(
    block_owner,
    transfer_cells,
    transfer_nodes,
    transfer_weights,
    row_counts,
    matrix_start,
    matrix_source,
    matrix_storage,
    fracture_start,
    fracture_source,
    fracture_leak,
    fracture_links,
    link_weights,
):
    devices = lax.axis_size("area")
    depth, area_rows, cols = matrix_start.shape
    owned, blk = fracture_start.shape
    total_rows = transfer_cells.shape[0]
    cap = 3 * total_rows // (2 * devices)
    cells = depth * area_rows * cols // LANES
    relax = relax_weights(ITERS)
    grid = (matrix_start.shape, F32)
    grids = ((GRID_SLOTS,) + matrix_start.shape, F32)
    fracture = (fracture_start.shape, F32)
    side = ((3 * HALO + 1, depth, cols), F32)
    sides = ((2, HALO, depth, cols), F32)
    hot = pltpu.VMEM((cells, total_rows), BF16)
    columns = pltpu.VMEM((2 * LANES, cells), BF16)
    padded = (devices, LANES)
    first_message = ((devices, 1 + owned * blk // LANES // 4, 4, LANES), F32)
    message_type = ((devices, 4, LANES), F32)
    pairs, crossings = [
        [(i + a, i + b) for i in range(start, devices - 1, 2) for a, b in ((0, 1), (1, 0))]
        for start in (0, 1)
    ]

    def exchange(message):
        return lax.all_to_all(
            message,
            "area",
            split_axis=0,
            concat_axis=0,
            tiled=True,
            axis_index_groups=[group_order(devices)],
        )

    staged = [
        row_counts.reshape(1, 1),
        block_owner.reshape(-1, LANES),
        transfer_cells.reshape(-1, LANES),
        transfer_nodes.reshape(-1, LANES),
        transfer_weights.reshape(-1, LANES),
        matrix_start,
        fracture_start,
        matrix_source,
        matrix_storage,
        fracture_links,
        link_weights,
    ]
    row_shape = (total_rows // LANES, LANES)
    rows = (row_shape, F32)
    info = ((6,) + row_shape, F32)
    edges = ((2, depth, cols), F32)
    slot_info, message, pair, cross, grids_start, link_sum = call(
        functools.partial(setup_kernel, devices, cap, len(staged)),
        [((3,) + padded, F32), first_message, side, side, grids, fracture],
        staged,
        "place_rows",
        5.0,
        hbm_in=range(len(staged)),
        hbm_out=(1, 2, 3, 4),
        scratch=[pltpu.VMEM(x.shape, x.dtype) for x in staged]
        + [
            pltpu.VMEM(*info),
            pltpu.VMEM(*first_message),
            pltpu.VMEM(*side),
            pltpu.VMEM(*side),
            hot,
            columns,
            pltpu.SemaphoreType.DMA((len(staged) + 7,)),
        ],
        limit=63 * 1024 * 1024,
    )
    arrived = exchange(message)
    pair = lax.ppermute(pair, "area", pairs)
    cross = lax.ppermute(cross, "area", crossings)
    row_info, partial, scaled, inverse, edge_rows, row_partial, row_inverse, chains = call(
        functools.partial(first_window_kernel, relax[0]),
        [info, grid, grid, grid, edges, rows, rows, ((3,) + row_shape, F32)],
        [grids_start],
        "stencil_first",
        4.0,
        hbm_in=(0,),
        scratch=[pltpu.VMEM(*grid)] * 3 + [hot, columns, pltpu.SemaphoreType.DMA((4,))],
    )
    fracture_now = fracture_start
    message_scratch = [pltpu.VMEM(*message_type), pltpu.SemaphoreType.DMA]
    fracture_now, fracture_inverse, node_code, message = call(
        functools.partial(first_step_kernel, relax[0], cap, area_rows),
        [fracture, fracture, (padded, jnp.int32), message_type],
        [
            arrived,
            pair,
            cross,
            slot_info,
            row_info,
            row_partial,
            row_inverse,
            chains,
            fracture_now,
            link_sum,
            fracture_source,
            fracture_leak,
            link_weights,
        ],
        "couple_first",
        2.0,
        hbm_out=(3,),
        scratch=message_scratch,
    )
    for index in range(1, ITERS):
        last = index == ITERS - 1
        old, arrived = arrived, exchange(message)
        first = index == 1
        inputs = [old, partial, scaled, inverse, row_info, slot_info, fracture_now]
        inputs += [fracture_links, link_weights]
        if first:
            inputs += [pair, cross, edge_rows]
        else:
            inputs += [side_partial, side_scaled, side_inverse, side_info]
        outs = call(
            functools.partial(window_kernel, relax[index], relax[index - 1], cap, first, last),
            [grid, sides, fracture]
            + ([sides, sides, edges] if first else [])
            + ([] if last else [rows]),
            inputs,
            "stencil",
            3.0,
            aliases={1: 0} if first else {1: 0, 9: 1},
            scratch=[pltpu.VMEM(*grid), hot] + ([] if last else [columns]),
        )
        partial, side_partial, link_sum = outs[:3]
        if first:
            side_scaled, side_inverse, side_info = outs[3:6]
        fractures = [fracture_now, link_sum, fracture_source, fracture_inverse]
        if last:
            return call(
                functools.partial(last_step_kernel, relax[index], cap),
                [grid, fracture],
                [arrived, node_code, partial, inverse, row_info] + fractures,
                "couple_last",
                2.0,
                scratch=[hot],
            )
        row_partial = outs[-1]
        fracture_now, message = call(
            functools.partial(step_kernel, relax[index], cap),
            [fracture, message_type],
            [arrived, node_code, slot_info, row_info, row_partial, row_inverse, chains]
            + fractures,
            "couple",
            2.0,
            hbm_out=(1,),
            scratch=message_scratch,
        )


def solution(mesh):
    in_specs = (
        P(),
        P("area"),
        P("area"),
        P("area"),
        P("area"),
        P("real", "area", None),
        P("real", "area", None),
        P("real", "area", None),
        P("area", "real"),
        P("area", "real"),
        P("area", "real"),
        P(None, "area", None),
        P("real", "area", None),
    )
    out_specs = (P("real", "area", None), P("area", "real"))
    return jax.shard_map(local, mesh=mesh, in_specs=in_specs, out_specs=out_specs, check_vma=False)
```

```python
import functools
import math

import jax
import jax.numpy as jnp
from jax import lax
from jax.experimental import pallas as pl
from jax.experimental.pallas import tpu as pltpu
from jax.sharding import PartitionSpec as P

ITERS = 4
HALO = ITERS - 1
GRID_SLOTS = 72
LANES = 128
F32 = jnp.float32
BF16 = jnp.bfloat16
VMEM_LIMIT = 32 * 1024 * 1024


def relax_weights(steps_total):
    return [
        1.0 / (1.0 + 0.75 * math.cos(math.pi * (2 * index + 1) / (2 * steps_total)))
        for index in range(steps_total)
    ]


def log2(value):
    assert value & (value - 1) == 0
    return value.bit_length() - 1


def group_order(devices):
    part = devices // 4
    return [part * z + i for i in reversed(range(part)) for z in (2, 0, 1, 3)]


def iota(shape, dim):
    return lax.broadcasted_iota(jnp.int32, shape, dim)


def halves(x):
    high = x.astype(BF16)
    low = (x - high.astype(F32)).astype(BF16)
    return high, low


def matmul(a, b, contract):
    return lax.dot_general(a, b, ((contract[:1], contract[1:]), ((), ())), preferred_element_type=F32)


def to_dense(x, cap):
    return jnp.concatenate([x[i : i + 1, :cap] for i in range(x.shape[0])], axis=1)


def from_dense(x, devices, cap):
    rows = jnp.concatenate([x[:, i * cap : (i + 1) * cap] for i in range(devices)], axis=0)
    return jnp.concatenate([rows, jnp.zeros((devices, LANES - cap), x.dtype)], axis=1)


def lane_gather(table, index):
    return jnp.take_along_axis(table, index, axis=1, mode="promise_in_bounds")


def masked_parts(low, *values):
    mask = iota((LANES, low.shape[1]), 0) == low
    zero = jnp.zeros((), F32)
    parts = []
    for value in values:
        high = value.astype(BF16).astype(F32)
        parts.append(jnp.where(mask, high, zero).astype(BF16))
        parts.append(jnp.where(mask, value - high, zero).astype(BF16))
    return jnp.concatenate(parts, axis=0)


def fold(wide, index):
    start = 2 * index * LANES
    return wide[:, start : start + LANES] + wide[:, start + LANES : start + 2 * LANES]


def pick_low(tall, low):
    both = tall[:LANES] + tall[LANES:]
    return jnp.sum(
        jnp.where(iota(both.shape, 0) == low, both, 0.0), axis=0, keepdims=True
    )


def stack_lanes(x):
    return jnp.concatenate(
        [x[:, i * LANES : (i + 1) * LANES] for i in range(x.shape[1] // LANES)], axis=0
    )


def unstack_lanes(x, rows):
    return jnp.concatenate([x[i : i + rows] for i in range(0, x.shape[0], rows)], axis=1)


def put_columns(chunk, index, columns_ref):
    high, low = halves(chunk.T)
    columns_ref[:LANES, index * LANES : (index + 1) * LANES] = high
    columns_ref[LANES:, index * LANES : (index + 1) * LANES] = low


def fill_hot(hot_ref, high):
    for start in range(0, hot_ref.shape[0], LANES):
        rows = iota((LANES, high.shape[1]), 0) + start
        hot_ref[start : start + LANES, :] = (rows == high).astype(F32).astype(BF16)


def pick_entries(table, row, lane):
    found = jnp.zeros(row.shape, table.dtype)
    for i in range(table.shape[0]):
        values = jnp.broadcast_to(table[i : i + 1], row.shape)
        found = jnp.where(row == i, lane_gather(values, lane), found)
    return found


def row_slice(grids_hbm, rows_ref):
    count, groups, lanes = rows_ref.shape
    return grids_hbm.at[3, :count, :groups, :lanes]


def setup_kernel(devices, cap, staged, *refs):
    sources, refs = refs[:staged], refs[staged:]
    slots_ref, message_hbm, pair_hbm, cross_hbm, grids_hbm, link_sum_ref = refs[:6]
    targets, refs = refs[6 : 6 + staged], refs[6 + staged :]
    rows_ref, message_ref, pair_ref, cross_ref, hot_ref, columns_ref, sems = refs
    copies = [
        pltpu.make_async_copy(sources[i], targets[i], sems.at[i]) for i in range(staged)
    ]
    kept = [
        pltpu.make_async_copy(targets[i], grids_hbm.at[j], sems.at[staged + 3 + j])
        for j, i in enumerate((5, 7, 8))
    ]
    kept.append(pltpu.make_async_copy(rows_ref, row_slice(grids_hbm, rows_ref), sems.at[staged + 6]))
    for copy in copies:
        copy.start()
    for copy in copies[:5]:
        copy.wait()
    counts_ref, owner_ref, cells_ref, nodes_ref, weights_ref = targets[:5]
    matrix_ref, fracture_ref, source_ref, storage_ref, links_ref, link_weights_ref = targets[5:]
    owned, blk = fracture_ref.shape
    depth, area_rows, cols = matrix_ref.shape
    groups = cells_ref.shape[0]
    plane_rows = depth * area_rows
    shape = (groups, LANES)
    nodes, cells = nodes_ref[...], cells_ref[...]
    live = iota(shape, 0) * LANES + iota(shape, 1) < counts_ref[...]
    weight = jnp.where(live, weights_ref[...], 0.0)
    block = nodes >> log2(blk)
    slot = jnp.zeros(shape, jnp.int32)
    for part in range(owner_ref.shape[0]):
        table = jnp.broadcast_to(owner_ref[part : part + 1, :], shape)
        found = lane_gather(table, block & (LANES - 1))
        slot = jnp.where(block >> log2(LANES) == part, found, slot)
    device = slot >> log2(owned)
    target = jnp.zeros(shape, jnp.int32)
    for position, place in enumerate(group_order(devices)):
        target = jnp.where(device == place, position, target)
    target = jnp.where(live, target, -1)
    node_high = ((nodes & (blk - 1)) >> log2(LANES)) * owned + (slot & (owned - 1))
    node_low = nodes & (LANES - 1)
    plane_row = cells >> log2(cols)
    cell_group = (cells & (cols - 1)) >> log2(LANES)
    cell_high = cell_group * plane_rows + plane_row
    cell_low = cells & (LANES - 1)
    high, low = unstack_lanes(cell_high, 1), unstack_lanes(cell_low, 1)
    row_weight = unstack_lanes(weight, 1)
    fill_hot(hot_ref, high)

    device_rows = iota((devices, LANES), 0)
    member = [(device_rows == target[q : q + 1]).astype(F32) for q in range(groups)]
    earlier = (iota((LANES, LANES), 0) < iota((LANES, LANES), 1)).astype(F32).astype(BF16)
    counted = matmul(jnp.concatenate(member, axis=0).astype(BF16), earlier, (1, 0))
    before = jnp.zeros((devices, 1), F32)
    rank = []
    for q in range(groups):
        inside = counted[q * devices : (q + 1) * devices] + before
        rank.append(jnp.sum(member[q] * inside, axis=0, keepdims=True).astype(jnp.int32))
        before = before + jnp.sum(member[q], axis=1, keepdims=True)
    rank_row = jnp.concatenate(rank, axis=1)
    rank = jnp.concatenate(rank, axis=0)
    member = jnp.concatenate(member, axis=1)

    first = weight.astype(BF16).astype(F32)
    second = (weight - first).astype(BF16).astype(F32)
    features = [
        jnp.ones(shape, F32),
        node_high.astype(F32),
        node_low.astype(F32),
        first,
        second,
        weight - first - second,
        iota(shape, 0).astype(F32),
        iota(shape, 1).astype(F32),
    ]
    features = [member * unstack_lanes(x, 1) for x in features]
    ranked = (iota((LANES, groups * LANES), 0) == rank_row).astype(F32).astype(BF16)
    packed = matmul(jnp.concatenate(features, axis=0).astype(BF16), ranked, (1, 1))
    packed = [packed[i * devices : (i + 1) * devices] for i in range(len(features))]
    code = jnp.where(packed[0] > 0.5, packed[1] * LANES + packed[2], -1.0)
    slot_row, slot_lane = packed[6].astype(jnp.int32), packed[7].astype(jnp.int32)
    slots_ref[0], slots_ref[1], slots_ref[2] = packed[6], packed[7], code
    alone = -1 - iota(shape, 0) * LANES - iota(shape, 1)
    cell = jnp.where(live, cells, alone)
    for i, x in enumerate((weight, target, rank, cell, cell_high, cell_low)):
        rows_ref[i] = x.astype(F32)
    kept[3].start()
    message_ref[:, 0, 0, :] = code
    message_ref[:, 0, 1, :] = packed[3] + packed[4] + packed[5]
    message_ref[:, 0, 3, :] = jnp.zeros((devices, LANES), F32)

    odd = (lax.axis_index("area") & 1) == 1
    plane = plane_row >> log2(area_rows)
    row = plane_row & (area_rows - 1)
    places = []
    for far in (area_rows - 1 - row, row):
        place = (cell_group * HALO + far) * depth + plane
        places.append(jnp.where(live & (far < HALO), place, -1).astype(F32))
    info = [low, row_weight, unstack_lanes(target, 1), unstack_lanes(rank, 1)]
    info = [x.astype(F32) for x in info]
    dense = to_dense(code, cap)
    half = dense.shape[1] // 2
    for ref, place in (
        (pair_ref, jnp.where(odd, places[1], places[0])),
        (cross_ref, jnp.where(odd, places[0], places[1])),
    ):
        tile = ref.at[3 * HALO]
        for i, x in enumerate([unstack_lanes(place, 1)] + info):
            tile[i : i + 1, :] = x
        tile[5:6, :half] = dense[:, :half]
        tile[6:7, :half] = dense[:, half:]

    for copy in copies[5:]:
        copy.wait()
    for copy in kept[:3]:
        copy.start()
    link_sum_ref[...] = linked(fracture_ref[...], links_ref, link_weights_ref)
    node_table = stack_lanes(fracture_ref[...])
    for i in range(node_table.shape[0]):
        message_ref[:, 1 + i // 4, i % 4, :] = jnp.broadcast_to(
            node_table[i : i + 1], (devices, LANES)
        )
    for part, ref in enumerate((matrix_ref, source_ref, storage_ref)):
        for far in range(HALO):
            up = ref[:, area_rows - 1 - far, :]
            down = ref[:, far, :]
            if part == 1 and far == HALO - 1:
                up = up + matrix_ref[:, area_rows - 1 - HALO, :]
                down = down + matrix_ref[:, HALO, :]
            pair_ref[part * HALO + far] = jnp.where(odd, down, up)
            cross_ref[part * HALO + far] = jnp.where(odd, up, down)
    outs = [
        pltpu.make_async_copy(pair_ref, pair_hbm, sems.at[staged]),
        pltpu.make_async_copy(cross_ref, cross_hbm, sems.at[staged + 1]),
        pltpu.make_async_copy(message_ref, message_hbm, sems.at[staged + 2]),
    ]
    outs[0].start()
    outs[1].start()
    picked = stack_lanes(pick_cells(matrix_ref, columns_ref, hot_ref, low))
    message_ref[:, 0, 2, :] = pick_entries(weight * picked, slot_row, slot_lane)
    outs[2].start()
    for out in outs + kept:
        out.wait()


def turned(rows):
    count = rows.shape[0]
    extra = -count % 8
    if extra:
        rows = jnp.concatenate([rows, jnp.zeros((extra, LANES), rows.dtype)], axis=0)
    return rows.T


def find_chains(cells):
    blocks = cells.shape[0]
    columns = turned(cells)
    none = float(blocks * LANES)
    sublane, lane = iota((LANES, LANES), 0), iota((LANES, LANES), 1)
    after = [jnp.full((8, LANES), none, F32) for _ in range(blocks)]
    before = [jnp.full((8, LANES), -1.0, F32) for _ in range(blocks)]
    count = [jnp.zeros((8, LANES), F32) for _ in range(blocks)]
    for j in range(blocks):
        cell = jnp.broadcast_to(columns[:, j : j + 1], (LANES, LANES))
        place = (sublane + j * LANES).astype(F32)
        for i in range(blocks):
            same = cell == cells[i : i + 1]
            parts = (LANES // 8, 8, LANES)
            ones = jnp.where(same, 1.0, 0.0).reshape(parts)
            count[i] = count[i] + jnp.sum(ones, axis=0)
            if j >= i:
                later = same & (sublane > lane) if j == i else same
                found = jnp.where(later, place, none).reshape(parts)
                after[i] = jnp.minimum(after[i], jnp.min(found, axis=0))
            if j <= i:
                sooner = same & (sublane < lane) if j == i else same
                found = jnp.where(sooner, place, -1.0).reshape(parts)
                before[i] = jnp.maximum(before[i], jnp.max(found, axis=0))
    after = jnp.concatenate([jnp.min(x, axis=0, keepdims=True) for x in after], axis=0)
    before = jnp.concatenate([jnp.max(x, axis=0, keepdims=True) for x in before], axis=0)
    count = jnp.concatenate([jnp.sum(x, axis=0, keepdims=True) for x in count], axis=0)
    return jnp.where(after < none, after, -1.0), before, count


def same_cell_sum(values, chains_ref):
    most = jnp.max(chains_ref[2]).astype(jnp.int32)
    rounds = log2(values.size)
    steps = sum((most > (1 << i)).astype(jnp.int32) for i in range(rounds))

    def step(_, state):
        after = []
        for total, link in (state[:2], state[2:]):
            row, lane = (link - 1) >> log2(LANES), (link - 1) & (LANES - 1)
            after += [total + pick_entries(total, row, lane), pick_entries(link, row, lane)]
        return tuple(after)

    ahead, behind = [row_integer(chains_ref, i) + 1 for i in range(2)]
    ahead, _, behind, _ = lax.fori_loop(0, steps, step, (values, ahead, values, behind))
    return ahead + behind - values


def relaxed(now, source, inverse, low_side, high_side, relaxation):
    depth, rows, cols = now.shape
    zero_plane = jnp.zeros((1, rows, cols), F32)
    beside = jnp.concatenate([now[1:], zero_plane], axis=0)
    beside = beside + jnp.concatenate([zero_plane, now[:-1]], axis=0)
    zero_row = jnp.zeros((depth, 1, cols), F32)
    above = zero_row if high_side is None else high_side[:, None]
    below = zero_row if low_side is None else low_side[:, None]
    beside = beside + jnp.concatenate([now[:, 1:], above], axis=1)
    beside = beside + jnp.concatenate([below, now[:, :-1]], axis=1)
    flat = now.reshape(depth * rows, cols)
    place = iota(flat.shape, 1)
    left = jnp.where(place == 0, 0.0, pltpu.roll(flat, 1, 1))
    right = jnp.where(place == cols - 1, 0.0, pltpu.roll(flat, cols - 1, 1))
    beside = beside + (left + right).reshape(now.shape)
    return (1.0 - relaxation) * now + relaxation * (source + inverse * beside)


def linked(fracture, links_ref, link_weights_ref):
    total = jnp.zeros(fracture.shape, F32)
    width = fracture.shape[1]
    tables = [fracture[:, i : i + LANES] for i in range(0, width, LANES)]
    sums = []
    for start in range(0, width, LANES):
        total = jnp.zeros(tables[0].shape, F32)
        for j in range(links_ref.shape[0]):
            link = links_ref[j, :, start : start + LANES]
            found = jnp.zeros(tables[0].shape, F32)
            for i, table in enumerate(tables):
                found = jnp.where(
                    link >> log2(LANES) == i, lane_gather(table, link & (LANES - 1)), found
                )
            total = total + link_weights_ref[j, :, start : start + LANES] * found
        sums.append(total)
    return jnp.concatenate(sums, axis=1)


def relaxed_side(now, edge, scaled, inverse, relaxation):
    depth, cols = edge.shape
    place = iota(edge.shape, 1)
    zero_plane = jnp.zeros((1, cols), F32)
    after = []
    for far in range(HALO):
        here = now[far]
        beside = jnp.concatenate([here[1:], zero_plane], axis=0)
        beside = beside + jnp.concatenate([zero_plane, here[:-1]], axis=0)
        beside = beside + jnp.where(place == 0, 0.0, pltpu.roll(here, 1, 1))
        beside = beside + jnp.where(place == cols - 1, 0.0, pltpu.roll(here, cols - 1, 1))
        beside = beside + (edge if far == 0 else now[far - 1])
        if far + 1 < HALO:
            beside = beside + now[far + 1]
        after.append(
            (1.0 - relaxation) * here + relaxation * (scaled[far] + inverse[far] * beside)
        )
    return after


def spread_side(place, low, values, depth, col_groups):
    rows = iota((col_groups * HALO * depth, place.shape[1]), 0)
    hot = (rows == place).astype(F32).astype(BF16)
    added = fold(matmul(hot, masked_parts(low, values), (1, 1)), 0)
    return [
        jnp.concatenate(
            [
                added[(group * HALO + far) * depth : (group * HALO + far + 1) * depth]
                for group in range(col_groups)
            ],
            axis=1,
        )
        for far in range(HALO)
    ]


def pick_cells(table_ref, columns_ref, hot_ref, low):
    depth, area_rows, cols = table_ref.shape
    for c in range(cols // LANES):
        chunk = table_ref[:, :, c * LANES : (c + 1) * LANES]
        put_columns(chunk.reshape(depth * area_rows, LANES), c, columns_ref)
    return pick_low(matmul(columns_ref[...], hot_ref[...], (1, 0)), low)


def side_kernel_inputs(info_ref, side):
    rows = [info_ref[side, i : i + 1, :] for i in range(5)]
    whole = [x.astype(jnp.int32) for x in rows]
    return whole[0], whole[1], rows[2], whole[3], whole[4]


def row_integer(rows_ref, index):
    return rows_ref[index].astype(jnp.int32)


def row_cells(rows_ref):
    return [unstack_lanes(row_integer(rows_ref, index), 1) for index in (4, 5)]


def first_window_kernel(
    relaxation,
    grids_hbm,
    rows_ref,
    partial_ref,
    scaled_ref,
    inverse_ref,
    edges_ref,
    row_partial_ref,
    row_inverse_ref,
    chains_ref,
    matrix_ref,
    source_ref,
    storage_ref,
    hot_ref,
    columns_ref,
    sems,
):
    copies = [
        pltpu.make_async_copy(row_slice(grids_hbm, rows_ref), rows_ref, sems.at[3]),
        pltpu.make_async_copy(grids_hbm.at[2], storage_ref, sems.at[2]),
        pltpu.make_async_copy(grids_hbm.at[1], source_ref, sems.at[1]),
        pltpu.make_async_copy(grids_hbm.at[0], matrix_ref, sems.at[0]),
    ]
    for copy in copies:
        copy.start()
    copies[0].wait()
    depth, area_rows, cols = matrix_ref.shape
    plane_rows = depth * area_rows
    high, low = row_cells(rows_ref)
    weight = rows_ref[0]
    fill_hot(hot_ref, high)
    added = fold(matmul(hot_ref[...], masked_parts(low, unstack_lanes(weight, 1)), (1, 1)), 0)
    for copy in copies[1:]:
        copy.wait()
    for c in range(cols // LANES):
        lanes = slice(c * LANES, (c + 1) * LANES)
        extra = added[c * plane_rows : (c + 1) * plane_rows].reshape(depth, area_rows, LANES)
        inverse = 1.0 / (6.0 + storage_ref[:, :, lanes] + extra)
        scaled_ref[:, :, lanes] = source_ref[:, :, lanes] * inverse
        inverse_ref[:, :, lanes] = inverse
    row_inverse_ref[...] = weight * stack_lanes(
        pick_cells(inverse_ref, columns_ref, hot_ref, low)
    )
    partial_ref[...] = relaxed(
        matrix_ref[...], scaled_ref[...], inverse_ref[...], None, None, relaxation
    )
    row_partial_ref[...] = weight * stack_lanes(pick_cells(partial_ref, columns_ref, hot_ref, low))
    edges_ref[0] = matrix_ref[:, 0, :]
    edges_ref[1] = matrix_ref[:, area_rows - 1, :]
    chains = find_chains(rows_ref[3])
    for i, x in enumerate(chains):
        chains_ref[i] = x


def both_sides(pair_ref, cross_ref, tiles):
    odd = (lax.axis_index("area") & 1) == 1
    lower = [jnp.where(odd, pair_ref[i], cross_ref[i]) for i in tiles]
    upper = [jnp.where(odd, cross_ref[i], pair_ref[i]) for i in tiles]
    return lower, upper


def beside_rows(pair_ref, cross_ref, rows_ref, area_rows):
    (lower,), (upper,) = both_sides(pair_ref, cross_ref, (0,))
    depth = lower.shape[0]
    high, low = row_cells(rows_ref)
    row = high & (area_rows - 1)
    plane = (high >> log2(area_rows)) & (depth - 1)
    place = (high >> log2(depth * area_rows)) * depth + plane
    table = jnp.concatenate([stack_lanes(lower), stack_lanes(upper)], axis=0)
    place = jnp.where(row == 0, place, place + table.shape[0] // 2)
    place = jnp.where((row == 0) | (row == area_rows - 1), place, -1)
    hot = (iota((table.shape[0], place.shape[1]), 0) == place).astype(F32).astype(BF16)
    columns = jnp.concatenate(halves(table.T), axis=0)
    return stack_lanes(pick_low(matmul(columns, hot, (1, 0)), low))


def add_rows(relaxation, values, partial_ref, inverse_ref, rows_ref, hot_ref, matrix_ref):
    depth, area_rows, cols = partial_ref.shape
    plane_rows = depth * area_rows
    high, low = row_cells(rows_ref)
    fill_hot(hot_ref, high)
    parts = masked_parts(low, unstack_lanes(values, 1))
    added = fold(matmul(hot_ref[...], parts, (1, 1)), 0)
    for c in range(cols // LANES):
        lanes = slice(c * LANES, (c + 1) * LANES)
        extra = added[c * plane_rows : (c + 1) * plane_rows].reshape(depth, area_rows, LANES)
        matrix_ref[:, :, lanes] = (
            partial_ref[:, :, lanes] + (relaxation * inverse_ref[:, :, lanes]) * extra
        )


def returned_values(returned, rows_ref):
    target, rank = row_integer(rows_ref, 1), row_integer(rows_ref, 2)
    return rows_ref[0] * pick_entries(returned, target, rank)


def first_sides(relaxation, pair_ref, cross_ref, edges_ref, scaled_ref, inverse_ref, info_ref):
    depth, cols = edges_ref.shape[1:]
    partial = []
    for side, tiles in enumerate(both_sides(pair_ref, cross_ref, range(3 * HALO + 1))):
        info_ref[side] = tiles[3 * HALO]
        place, low, weight, _, _ = side_kernel_inputs(info_ref, side)
        added = spread_side(place, low, weight, depth, cols // LANES)
        scaled, inverse = [], []
        for far in range(HALO):
            storage = tiles[2 * HALO + far]
            inverse.append(jnp.where(storage > 0.0, 1.0 / (6.0 + storage + added[far]), 0.0))
            scaled.append(tiles[HALO + far] * inverse[far])
            scaled_ref[side, far] = scaled[far]
            inverse_ref[side, far] = inverse[far]
        partial.append(
            relaxed_side(tiles[:HALO], edges_ref[side], scaled, inverse, relaxation)
        )
    return partial


def window_kernel(
    relaxation,
    before,
    cap,
    first,
    last,
    arrived_ref,
    partial_before_ref,
    scaled_ref,
    inverse_ref,
    rows_ref,
    slots_ref,
    fracture_ref,
    links_ref,
    link_weights_ref,
    *refs,
):
    depth, area_rows, cols = scaled_ref.shape
    devices = arrived_ref.shape[0]
    half = devices * cap // 2
    if first:
        pair_ref, cross_ref, edges_ref, *refs = refs
        partial_ref, side_partial_ref, link_sum_ref, *refs = refs
        side_scaled_ref, side_inverse_ref, side_info_ref, *refs = refs
    else:
        side_before_ref, side_scaled_ref, side_inverse_ref, side_info_ref, *refs = refs
        partial_ref, side_partial_ref, link_sum_ref, *refs = refs
    if last:
        matrix_ref, hot_ref = refs
    else:
        row_partial_ref, matrix_ref, hot_ref, columns_ref = refs
    returned = device_values(arrived_ref, row_integer(slots_ref, 2)) if first else arrived_ref[:, 1, :]
    values = returned_values(returned, rows_ref)
    add_rows(before, values, partial_before_ref, inverse_ref, rows_ref, hot_ref, matrix_ref)
    if first:
        lower, upper = both_sides(pair_ref, cross_ref, (0,))
        for edge, tile in ((0, lower[0]), (area_rows - 1, upper[0])):
            matrix_ref[:, edge, :] = (
                matrix_ref[:, edge, :] + (before * inverse_ref[:, edge, :]) * tile
            )
        side_before = first_sides(
            before, pair_ref, cross_ref, edges_ref, side_scaled_ref, side_inverse_ref, side_info_ref
        )
    else:
        side_before = [[side_before_ref[side, far] for far in range(HALO)] for side in range(2)]
    edges = []
    for side, edge in enumerate((0, area_rows - 1)):
        place, low, weight, target, rank = side_kernel_inputs(side_info_ref, side)
        if first:
            code = jnp.concatenate(
                [side_info_ref[side, i : i + 1, :half] for i in (5, 6)], axis=1
            )
            code = from_dense(code, devices, cap).astype(jnp.int32)
            returned = device_values(arrived_ref, code)
        else:
            returned = arrived_ref[:, 2 + side, :]
        values = pick_entries(returned, stack_lanes(target), stack_lanes(rank))
        values = weight * unstack_lanes(values, 1)
        added = spread_side(place, low, values, depth, cols // LANES)
        now = [
            side_before[side][far] + before * side_inverse_ref[side, far] * added[far]
            for far in range(HALO)
        ]
        edges.append(now[0])
        after = relaxed_side(
            now,
            matrix_ref[:, edge, :],
            [side_scaled_ref[side, far] for far in range(HALO)],
            [side_inverse_ref[side, far] for far in range(HALO)],
            relaxation,
        )
        for far in range(HALO):
            side_partial_ref[side, far] = after[far]
    partial_ref[...] = relaxed(
        matrix_ref[...],
        scaled_ref[...],
        inverse_ref[...],
        edges[0],
        edges[1],
        relaxation,
    )
    if not last:
        row_partial_ref[...] = rows_ref[0] * stack_lanes(
            pick_cells(partial_ref, columns_ref, hot_ref, row_cells(rows_ref)[1])
        )
    link_sum_ref[...] = linked(fracture_ref[...], links_ref, link_weights_ref)


def row_values(
    relaxation,
    returned,
    slots_ref,
    rows_ref,
    row_partial_ref,
    row_inverse_ref,
    chains_ref,
    beside=None,
):
    total = same_cell_sum(returned_values(returned, rows_ref), chains_ref)
    if beside is not None:
        total = total + beside
    outgoing = row_partial_ref[...] + (relaxation * row_inverse_ref[...]) * total
    return pick_entries(outgoing, row_integer(slots_ref, 0), row_integer(slots_ref, 1))


def node_sums(code, shape, *values):
    owned, blk = shape
    rows = owned * blk // LANES
    member = iota((rows, code.shape[1]), 0) == code >> log2(LANES)
    low = (iota((LANES, code.shape[1]), 0) == code & (LANES - 1)).astype(F32).astype(BF16)
    parts = []
    for value in values:
        high = value.astype(BF16).astype(F32)
        parts += [jnp.where(member, high, 0.0), jnp.where(member, value - high, 0.0)]
    sums = matmul(jnp.concatenate(parts, axis=0).astype(BF16), low, (1, 1))
    sums = [sums[i : i + rows] for i in range(0, sums.shape[0], rows)]
    return [
        unstack_lanes(sums[2 * i] + sums[2 * i + 1], owned) for i in range(len(values))
    ]


def node_values(table, code):
    found = jnp.zeros(code.shape, F32)
    low = code & (LANES - 1)
    for row in range(table.shape[0]):
        values = jnp.broadcast_to(table[row : row + 1], code.shape)
        found = jnp.where(code >> log2(LANES) == row, lane_gather(values, low), found)
    return found


def device_values(arrived_ref, code):
    found = jnp.zeros(code.shape, F32)
    low = code & (LANES - 1)
    for row in range(4 * (arrived_ref.shape[1] - 1)):
        values = lane_gather(arrived_ref[:, 1 + row // 4, row % 4, :], low)
        found = jnp.where(code >> log2(LANES) == row, values, found)
    return found


def put_requested(message_ref, values):
    zero = jnp.zeros((1, LANES), F32)
    order = group_order(values.shape[0])
    rows = {device: values[i : i + 1] for i, device in enumerate(order)}
    message_ref[:, 1, :] = values
    for place, step in ((2, -1), (3, 1)):
        message_ref[:, place, :] = jnp.concatenate(
            [rows.get(device + step, zero) for device in order], axis=0
        )


def first_step_kernel(
    relaxation,
    cap,
    area_rows,
    arrived_ref,
    pair_ref,
    cross_ref,
    slots_ref,
    rows_ref,
    row_partial_ref,
    row_inverse_ref,
    chains_ref,
    fracture_ref,
    link_sum_ref,
    fracture_source_ref,
    leak_ref,
    link_weights_ref,
    fracture_next_ref,
    fracture_inverse_ref,
    node_code_ref,
    message_hbm,
    message_ref,
    sem,
):
    message_ref[:, 0, :] = row_values(
        relaxation,
        device_values(arrived_ref, row_integer(slots_ref, 2)),
        slots_ref,
        rows_ref,
        row_partial_ref,
        row_inverse_ref,
        chains_ref,
        beside_rows(pair_ref, cross_ref, rows_ref, area_rows),
    )
    code = arrived_ref[:, 0, 0, :].astype(jnp.int32)
    node_code_ref[...] = code
    dense = to_dense(code, cap)
    weight_sum, value_sum = node_sums(
        dense,
        fracture_ref.shape,
        to_dense(arrived_ref[:, 0, 1, :], cap),
        to_dense(arrived_ref[:, 0, 2, :], cap),
    )
    diag = leak_ref[...] + jnp.sum(link_weights_ref[...], axis=0) + weight_sum
    inverse = 1.0 / diag
    fracture_inverse_ref[...] = inverse
    fracture_next = (1.0 - relaxation) * fracture_ref[...] + (relaxation * inverse) * (
        fracture_source_ref[...] + link_sum_ref[...] + value_sum
    )
    fracture_next_ref[...] = fracture_next
    put_requested(message_ref, node_values(stack_lanes(fracture_next), code))
    out = pltpu.make_async_copy(message_ref, message_hbm, sem)
    out.start()
    out.wait()


def next_fracture(
    relaxation,
    cap,
    arrived_ref,
    code,
    fracture_ref,
    link_sum_ref,
    fracture_source_ref,
    fracture_inverse_ref,
):
    (value_sum,) = node_sums(
        to_dense(code, cap), fracture_ref.shape, to_dense(arrived_ref[:, 0, :], cap)
    )
    return (1.0 - relaxation) * fracture_ref[...] + (relaxation * fracture_inverse_ref[...]) * (
        fracture_source_ref[...] + link_sum_ref[...] + value_sum
    )


def step_kernel(
    relaxation,
    cap,
    arrived_ref,
    node_code_ref,
    slots_ref,
    rows_ref,
    row_partial_ref,
    row_inverse_ref,
    chains_ref,
    fracture_ref,
    link_sum_ref,
    fracture_source_ref,
    fracture_inverse_ref,
    fracture_next_ref,
    message_hbm,
    message_ref,
    sem,
):
    message_ref[:, 0, :] = row_values(
        relaxation,
        arrived_ref[:, 1, :],
        slots_ref,
        rows_ref,
        row_partial_ref,
        row_inverse_ref,
        chains_ref,
    )
    code = node_code_ref[...]
    fracture_next = next_fracture(
        relaxation,
        cap,
        arrived_ref,
        code,
        fracture_ref,
        link_sum_ref,
        fracture_source_ref,
        fracture_inverse_ref,
    )
    fracture_next_ref[...] = fracture_next
    put_requested(message_ref, node_values(stack_lanes(fracture_next), code))
    out = pltpu.make_async_copy(message_ref, message_hbm, sem)
    out.start()
    out.wait()


def last_step_kernel(
    relaxation,
    cap,
    arrived_ref,
    node_code_ref,
    partial_ref,
    inverse_ref,
    rows_ref,
    fracture_ref,
    link_sum_ref,
    fracture_source_ref,
    fracture_inverse_ref,
    matrix_ref,
    fracture_next_ref,
    hot_ref,
):
    values = returned_values(arrived_ref[:, 1, :], rows_ref)
    add_rows(relaxation, values, partial_ref, inverse_ref, rows_ref, hot_ref, matrix_ref)
    fracture_next_ref[...] = next_fracture(
        relaxation,
        cap,
        arrived_ref,
        node_code_ref[...],
        fracture_ref,
        link_sum_ref,
        fracture_source_ref,
        fracture_inverse_ref,
    )


def call(kernel, outs, ins, name, micros, hbm_in=(), hbm_out=(), scratch=(), aliases=None, limit=VMEM_LIMIT):
    return pl.pallas_call(
        kernel,
        out_shape=[jax.ShapeDtypeStruct(shape, dtype) for shape, dtype in outs],
        in_specs=[
            pl.BlockSpec(memory_space=pltpu.HBM if i in hbm_in else pltpu.VMEM)
            for i in range(len(ins))
        ],
        out_specs=[
            pl.BlockSpec(memory_space=pltpu.HBM if i in hbm_out else pltpu.VMEM)
            for i in range(len(outs))
        ],
        scratch_shapes=list(scratch),
        input_output_aliases=aliases or {},
        compiler_params=pltpu.CompilerParams(vmem_limit_bytes=limit),
        cost_estimate=pl.CostEstimate(
            flops=0, bytes_accessed=int(micros * 3.0e6), transcendentals=0
        ),
        name=name,
    )(*ins)


def local(
    block_owner,
    transfer_cells,
    transfer_nodes,
    transfer_weights,
    row_counts,
    matrix_start,
    matrix_source,
    matrix_storage,
    fracture_start,
    fracture_source,
    fracture_leak,
    fracture_links,
    link_weights,
):
    devices = lax.axis_size("area")
    depth, area_rows, cols = matrix_start.shape
    owned, blk = fracture_start.shape
    total_rows = transfer_cells.shape[0]
    cap = 3 * total_rows // (2 * devices)
    cells = depth * area_rows * cols // LANES
    relax = relax_weights(ITERS)
    grid = (matrix_start.shape, F32)
    grids = ((GRID_SLOTS,) + matrix_start.shape, F32)
    fracture = (fracture_start.shape, F32)
    side = ((3 * HALO + 1, depth, cols), F32)
    sides = ((2, HALO, depth, cols), F32)
    hot = pltpu.VMEM((cells, total_rows), BF16)
    columns = pltpu.VMEM((2 * LANES, cells), BF16)
    padded = (devices, LANES)
    first_message = ((devices, 1 + owned * blk // LANES // 4, 4, LANES), F32)
    message_type = ((devices, 4, LANES), F32)
    pairs, crossings = [
        [(i + a, i + b) for i in range(start, devices - 1, 2) for a, b in ((0, 1), (1, 0))]
        for start in (0, 1)
    ]

    def exchange(message):
        return lax.all_to_all(
            message,
            "area",
            split_axis=0,
            concat_axis=0,
            tiled=True,
            axis_index_groups=[group_order(devices)],
        )

    staged = [
        row_counts.reshape(1, 1),
        block_owner.reshape(-1, LANES),
        transfer_cells.reshape(-1, LANES),
        transfer_nodes.reshape(-1, LANES),
        transfer_weights.reshape(-1, LANES),
        matrix_start,
        fracture_start,
        matrix_source,
        matrix_storage,
        fracture_links,
        link_weights,
    ]
    row_shape = (total_rows // LANES, LANES)
    rows = (row_shape, F32)
    info = ((6,) + row_shape, F32)
    edges = ((2, depth, cols), F32)
    slot_info, message, pair, cross, grids_start, link_sum = call(
        functools.partial(setup_kernel, devices, cap, len(staged)),
        [((3,) + padded, F32), first_message, side, side, grids, fracture],
        staged,
        "place_rows",
        5.0,
        hbm_in=range(len(staged)),
        hbm_out=(1, 2, 3, 4),
        scratch=[pltpu.VMEM(x.shape, x.dtype) for x in staged]
        + [
            pltpu.VMEM(*info),
            pltpu.VMEM(*first_message),
            pltpu.VMEM(*side),
            pltpu.VMEM(*side),
            hot,
            columns,
            pltpu.SemaphoreType.DMA((len(staged) + 7,)),
        ],
        limit=63 * 1024 * 1024,
    )
    arrived = exchange(message)
    pair = lax.ppermute(pair, "area", pairs)
    cross = lax.ppermute(cross, "area", crossings)
    row_info, partial, scaled, inverse, edge_rows, row_partial, row_inverse, chains = call(
        functools.partial(first_window_kernel, relax[0]),
        [info, grid, grid, grid, edges, rows, rows, ((3,) + row_shape, F32)],
        [grids_start],
        "stencil_first",
        4.0,
        hbm_in=(0,),
        scratch=[pltpu.VMEM(*grid)] * 3 + [hot, columns, pltpu.SemaphoreType.DMA((4,))],
    )
    fracture_now = fracture_start
    message_scratch = [pltpu.VMEM(*message_type), pltpu.SemaphoreType.DMA]
    fracture_now, fracture_inverse, node_code, message = call(
        functools.partial(first_step_kernel, relax[0], cap, area_rows),
        [fracture, fracture, (padded, jnp.int32), message_type],
        [
            arrived,
            pair,
            cross,
            slot_info,
            row_info,
            row_partial,
            row_inverse,
            chains,
            fracture_now,
            link_sum,
            fracture_source,
            fracture_leak,
            link_weights,
        ],
        "couple_first",
        2.0,
        hbm_out=(3,),
        scratch=message_scratch,
    )
    for index in range(1, ITERS):
        last = index == ITERS - 1
        old, arrived = arrived, exchange(message)
        first = index == 1
        inputs = [old, partial, scaled, inverse, row_info, slot_info, fracture_now]
        inputs += [fracture_links, link_weights]
        if first:
            inputs += [pair, cross, edge_rows]
        else:
            inputs += [side_partial, side_scaled, side_inverse, side_info]
        outs = call(
            functools.partial(window_kernel, relax[index], relax[index - 1], cap, first, last),
            [grid, sides, fracture]
            + ([sides, sides, edges] if first else [])
            + ([] if last else [rows]),
            inputs,
            "stencil",
            3.0,
            aliases={1: 0} if first else {1: 0, 9: 1},
            scratch=[pltpu.VMEM(*grid), hot] + ([] if last else [columns]),
        )
        partial, side_partial, link_sum = outs[:3]
        if first:
            side_scaled, side_inverse, side_info = outs[3:6]
        fractures = [fracture_now, link_sum, fracture_source, fracture_inverse]
        if last:
            return call(
                functools.partial(last_step_kernel, relax[index], cap),
                [grid, fracture],
                [arrived, node_code, partial, inverse, row_info] + fractures,
                "couple_last",
                2.0,
                scratch=[hot],
            )
        row_partial = outs[-1]
        fracture_now, message = call(
            functools.partial(step_kernel, relax[index], cap),
            [fracture, message_type],
            [arrived, node_code, slot_info, row_info, row_partial, row_inverse, chains]
            + fractures,
            "couple",
            2.0,
            hbm_out=(1,),
            scratch=message_scratch,
        )


def solution(mesh):
    in_specs = (
        P(),
        P("area"),
        P("area"),
        P("area"),
        P("area"),
        P("real", "area", None),
        P("real", "area", None),
        P("real", "area", None),
        P("area", "real"),
        P("area", "real"),
        P("area", "real"),
        P(None, "area", None),
        P("real", "area", None),
    )
    out_specs = (P("real", "area", None), P("area", "real"))
    return jax.shard_map(local, mesh=mesh, in_specs=in_specs, out_specs=out_specs, check_vma=False)
```

```python
import functools
import math

import jax
import jax.numpy as jnp
from jax import lax
from jax.experimental import pallas as pl
from jax.experimental.pallas import tpu as pltpu
from jax.sharding import PartitionSpec as P

ITERS = 4
HALO = ITERS - 1
GRID_SLOTS = 72
LANES = 128
F32 = jnp.float32
BF16 = jnp.bfloat16
VMEM_LIMIT = 32 * 1024 * 1024


def relax_weights(steps_total):
    return [
        1.0 / (1.0 + 0.75 * math.cos(math.pi * (2 * index + 1) / (2 * steps_total)))
        for index in range(steps_total)
    ]


def log2(value):
    assert value & (value - 1) == 0
    return value.bit_length() - 1


def group_order(devices):
    part = devices // 4
    return [part * z + i for i in reversed(range(part)) for z in (2, 0, 1, 3)]


def iota(shape, dim):
    return lax.broadcasted_iota(jnp.int32, shape, dim)


def halves(x):
    high = x.astype(BF16)
    low = (x - high.astype(F32)).astype(BF16)
    return high, low


def matmul(a, b, contract):
    return lax.dot_general(a, b, ((contract[:1], contract[1:]), ((), ())), preferred_element_type=F32)


def to_dense(x, cap):
    return jnp.concatenate([x[i : i + 1, :cap] for i in range(x.shape[0])], axis=1)


def from_dense(x, devices, cap):
    rows = jnp.concatenate([x[:, i * cap : (i + 1) * cap] for i in range(devices)], axis=0)
    return jnp.concatenate([rows, jnp.zeros((devices, LANES - cap), x.dtype)], axis=1)


def lane_gather(table, index):
    return jnp.take_along_axis(table, index, axis=1, mode="promise_in_bounds")


def masked_parts(low, *values):
    mask = iota((LANES, low.shape[1]), 0) == low
    zero = jnp.zeros((), F32)
    parts = []
    for value in values:
        high = value.astype(BF16).astype(F32)
        parts.append(jnp.where(mask, high, zero).astype(BF16))
        parts.append(jnp.where(mask, value - high, zero).astype(BF16))
    return jnp.concatenate(parts, axis=0)


def fold(wide, index):
    start = 2 * index * LANES
    return wide[:, start : start + LANES] + wide[:, start + LANES : start + 2 * LANES]


def pick_low(tall, low):
    both = tall[:LANES] + tall[LANES:]
    return jnp.sum(
        jnp.where(iota(both.shape, 0) == low, both, 0.0), axis=0, keepdims=True
    )


def stack_lanes(x):
    return jnp.concatenate(
        [x[:, i * LANES : (i + 1) * LANES] for i in range(x.shape[1] // LANES)], axis=0
    )


def unstack_lanes(x, rows):
    return jnp.concatenate([x[i : i + rows] for i in range(0, x.shape[0], rows)], axis=1)


def put_columns(chunk, index, columns_ref):
    high, low = halves(chunk.T)
    columns_ref[:LANES, index * LANES : (index + 1) * LANES] = high
    columns_ref[LANES:, index * LANES : (index + 1) * LANES] = low


def fill_hot(hot_ref, high):
    for start in range(0, hot_ref.shape[0], LANES):
        rows = iota((LANES, high.shape[1]), 0) + start
        hot_ref[start : start + LANES, :] = (rows == high).astype(F32).astype(BF16)


def pick_entries(table, row, lane):
    found = jnp.zeros(row.shape, table.dtype)
    for i in range(table.shape[0]):
        values = jnp.broadcast_to(table[i : i + 1], row.shape)
        found = jnp.where(row == i, lane_gather(values, lane), found)
    return found


def row_slice(grids_hbm, rows_ref):
    count, groups, lanes = rows_ref.shape
    return grids_hbm.at[3, :count, :groups, :lanes]


def setup_kernel(devices, cap, staged, *refs):
    sources, refs = refs[:staged], refs[staged:]
    slots_ref, message_hbm, pair_hbm, cross_hbm, grids_hbm, link_sum_ref = refs[:6]
    targets, refs = refs[6 : 6 + staged], refs[6 + staged :]
    rows_ref, message_ref, pair_ref, cross_ref, hot_ref, columns_ref, sems = refs
    copies = [
        pltpu.make_async_copy(sources[i], targets[i], sems.at[i]) for i in range(staged)
    ]
    kept = [
        pltpu.make_async_copy(targets[i], grids_hbm.at[j], sems.at[staged + 3 + j])
        for j, i in enumerate((5, 7, 8))
    ]
    kept.append(pltpu.make_async_copy(rows_ref, row_slice(grids_hbm, rows_ref), sems.at[staged + 6]))
    for copy in copies:
        copy.start()
    for copy in copies[:5]:
        copy.wait()
    counts_ref, owner_ref, cells_ref, nodes_ref, weights_ref = targets[:5]
    matrix_ref, fracture_ref, source_ref, storage_ref, links_ref, link_weights_ref = targets[5:]
    owned, blk = fracture_ref.shape
    depth, area_rows, cols = matrix_ref.shape
    groups = cells_ref.shape[0]
    plane_rows = depth * area_rows
    shape = (groups, LANES)
    nodes, cells = nodes_ref[...], cells_ref[...]
    live = iota(shape, 0) * LANES + iota(shape, 1) < counts_ref[...]
    weight = jnp.where(live, weights_ref[...], 0.0)
    block = nodes >> log2(blk)
    slot = jnp.zeros(shape, jnp.int32)
    for part in range(owner_ref.shape[0]):
        table = jnp.broadcast_to(owner_ref[part : part + 1, :], shape)
        found = lane_gather(table, block & (LANES - 1))
        slot = jnp.where(block >> log2(LANES) == part, found, slot)
    device = slot >> log2(owned)
    target = jnp.zeros(shape, jnp.int32)
    for position, place in enumerate(group_order(devices)):
        target = jnp.where(device == place, position, target)
    target = jnp.where(live, target, -1)
    node_high = ((nodes & (blk - 1)) >> log2(LANES)) * owned + (slot & (owned - 1))
    node_low = nodes & (LANES - 1)
    plane_row = cells >> log2(cols)
    cell_group = (cells & (cols - 1)) >> log2(LANES)
    cell_high = cell_group * plane_rows + plane_row
    cell_low = cells & (LANES - 1)
    high, low = unstack_lanes(cell_high, 1), unstack_lanes(cell_low, 1)
    row_weight = unstack_lanes(weight, 1)
    fill_hot(hot_ref, high)

    device_rows = iota((devices, LANES), 0)
    member = [(device_rows == target[q : q + 1]).astype(F32) for q in range(groups)]
    earlier = (iota((LANES, LANES), 0) < iota((LANES, LANES), 1)).astype(F32).astype(BF16)
    counted = matmul(jnp.concatenate(member, axis=0).astype(BF16), earlier, (1, 0))
    before = jnp.zeros((devices, 1), F32)
    rank = []
    for q in range(groups):
        inside = counted[q * devices : (q + 1) * devices] + before
        rank.append(jnp.sum(member[q] * inside, axis=0, keepdims=True).astype(jnp.int32))
        before = before + jnp.sum(member[q], axis=1, keepdims=True)
    rank_row = jnp.concatenate(rank, axis=1)
    rank = jnp.concatenate(rank, axis=0)
    member = jnp.concatenate(member, axis=1)

    first = weight.astype(BF16).astype(F32)
    second = (weight - first).astype(BF16).astype(F32)
    features = [
        jnp.ones(shape, F32),
        node_high.astype(F32),
        node_low.astype(F32),
        first,
        second,
        weight - first - second,
        iota(shape, 0).astype(F32),
        iota(shape, 1).astype(F32),
    ]
    features = [member * unstack_lanes(x, 1) for x in features]
    ranked = (iota((LANES, groups * LANES), 0) == rank_row).astype(F32).astype(BF16)
    packed = matmul(jnp.concatenate(features, axis=0).astype(BF16), ranked, (1, 1))
    packed = [packed[i * devices : (i + 1) * devices] for i in range(len(features))]
    code = jnp.where(packed[0] > 0.5, packed[1] * LANES + packed[2], -1.0)
    slot_row, slot_lane = packed[6].astype(jnp.int32), packed[7].astype(jnp.int32)
    slots_ref[0], slots_ref[1], slots_ref[2] = packed[6], packed[7], code
    alone = -1 - iota(shape, 0) * LANES - iota(shape, 1)
    cell = jnp.where(live, cells, alone)
    for i, x in enumerate((weight, target, rank, cell, cell_high, cell_low)):
        rows_ref[i] = x.astype(F32)
    kept[3].start()
    message_ref[:, 0, 0, :] = code
    message_ref[:, 0, 1, :] = packed[3] + packed[4] + packed[5]
    message_ref[:, 0, 3, :] = jnp.zeros((devices, LANES), F32)

    odd = (lax.axis_index("area") & 1) == 1
    plane = plane_row >> log2(area_rows)
    row = plane_row & (area_rows - 1)
    places = []
    for far in (area_rows - 1 - row, row):
        place = (cell_group * HALO + far) * depth + plane
        places.append(jnp.where(live & (far < HALO), place, -1).astype(F32))
    info = [low, row_weight, unstack_lanes(target, 1), unstack_lanes(rank, 1)]
    info = [x.astype(F32) for x in info]
    dense = to_dense(code, cap)
    half = dense.shape[1] // 2
    for ref, place in (
        (pair_ref, jnp.where(odd, places[1], places[0])),
        (cross_ref, jnp.where(odd, places[0], places[1])),
    ):
        tile = ref.at[3 * HALO]
        for i, x in enumerate([unstack_lanes(place, 1)] + info):
            tile[i : i + 1, :] = x
        tile[5:6, :half] = dense[:, :half]
        tile[6:7, :half] = dense[:, half:]

    for copy in copies[5:]:
        copy.wait()
    for copy in kept[:3]:
        copy.start()
    node_table = stack_lanes(fracture_ref[...])
    for i in range(node_table.shape[0]):
        message_ref[:, 1 + i // 4, i % 4, :] = jnp.broadcast_to(
            node_table[i : i + 1], (devices, LANES)
        )
    picked = stack_lanes(pick_cells(matrix_ref, columns_ref, hot_ref, low))
    message_ref[:, 0, 2, :] = pick_entries(weight * picked, slot_row, slot_lane)
    message_copy = pltpu.make_async_copy(message_ref, message_hbm, sems.at[staged + 2])
    message_copy.start()
    for part, ref in enumerate((matrix_ref, source_ref, storage_ref)):
        for far in range(HALO):
            up = ref[:, area_rows - 1 - far, :]
            down = ref[:, far, :]
            if part == 1 and far == HALO - 1:
                up = up + matrix_ref[:, area_rows - 1 - HALO, :]
                down = down + matrix_ref[:, HALO, :]
            pair_ref[part * HALO + far] = jnp.where(odd, down, up)
            cross_ref[part * HALO + far] = jnp.where(odd, up, down)
    outs = [
        pltpu.make_async_copy(pair_ref, pair_hbm, sems.at[staged]),
        pltpu.make_async_copy(cross_ref, cross_hbm, sems.at[staged + 1]),
        message_copy,
    ]
    outs[0].start()
    outs[1].start()
    link_sum_ref[...] = linked(fracture_ref[...], links_ref, link_weights_ref)
    for out in outs + kept:
        out.wait()


def turned(rows):
    count = rows.shape[0]
    extra = -count % 8
    if extra:
        rows = jnp.concatenate([rows, jnp.zeros((extra, LANES), rows.dtype)], axis=0)
    return rows.T


def find_chains(cells):
    blocks = cells.shape[0]
    columns = turned(cells)
    none = float(blocks * LANES)
    sublane, lane = iota((LANES, LANES), 0), iota((LANES, LANES), 1)
    after = [jnp.full((8, LANES), none, F32) for _ in range(blocks)]
    before = [jnp.full((8, LANES), -1.0, F32) for _ in range(blocks)]
    count = [jnp.zeros((8, LANES), F32) for _ in range(blocks)]
    for j in range(blocks):
        cell = jnp.broadcast_to(columns[:, j : j + 1], (LANES, LANES))
        place = (sublane + j * LANES).astype(F32)
        for i in range(blocks):
            same = cell == cells[i : i + 1]
            parts = (LANES // 8, 8, LANES)
            ones = jnp.where(same, 1.0, 0.0).reshape(parts)
            count[i] = count[i] + jnp.sum(ones, axis=0)
            if j >= i:
                later = same & (sublane > lane) if j == i else same
                found = jnp.where(later, place, none).reshape(parts)
                after[i] = jnp.minimum(after[i], jnp.min(found, axis=0))
            if j <= i:
                sooner = same & (sublane < lane) if j == i else same
                found = jnp.where(sooner, place, -1.0).reshape(parts)
                before[i] = jnp.maximum(before[i], jnp.max(found, axis=0))
    after = jnp.concatenate([jnp.min(x, axis=0, keepdims=True) for x in after], axis=0)
    before = jnp.concatenate([jnp.max(x, axis=0, keepdims=True) for x in before], axis=0)
    count = jnp.concatenate([jnp.sum(x, axis=0, keepdims=True) for x in count], axis=0)
    return jnp.where(after < none, after, -1.0), before, count


def same_cell_sum(values, chains_ref):
    most = jnp.max(chains_ref[2]).astype(jnp.int32)
    rounds = log2(values.size)
    steps = sum((most > (1 << i)).astype(jnp.int32) for i in range(rounds))

    def step(_, state):
        after = []
        for total, link in (state[:2], state[2:]):
            row, lane = (link - 1) >> log2(LANES), (link - 1) & (LANES - 1)
            after += [total + pick_entries(total, row, lane), pick_entries(link, row, lane)]
        return tuple(after)

    ahead, behind = [row_integer(chains_ref, i) + 1 for i in range(2)]
    ahead, _, behind, _ = lax.fori_loop(0, steps, step, (values, ahead, values, behind))
    return ahead + behind - values


def relaxed(now, source, inverse, low_side, high_side, relaxation):
    depth, rows, cols = now.shape
    zero_plane = jnp.zeros((1, rows, cols), F32)
    beside = jnp.concatenate([now[1:], zero_plane], axis=0)
    beside = beside + jnp.concatenate([zero_plane, now[:-1]], axis=0)
    zero_row = jnp.zeros((depth, 1, cols), F32)
    above = zero_row if high_side is None else high_side[:, None]
    below = zero_row if low_side is None else low_side[:, None]
    beside = beside + jnp.concatenate([now[:, 1:], above], axis=1)
    beside = beside + jnp.concatenate([below, now[:, :-1]], axis=1)
    flat = now.reshape(depth * rows, cols)
    place = iota(flat.shape, 1)
    left = jnp.where(place == 0, 0.0, pltpu.roll(flat, 1, 1))
    right = jnp.where(place == cols - 1, 0.0, pltpu.roll(flat, cols - 1, 1))
    beside = beside + (left + right).reshape(now.shape)
    return (1.0 - relaxation) * now + relaxation * (source + inverse * beside)


def linked(fracture, links_ref, link_weights_ref):
    total = jnp.zeros(fracture.shape, F32)
    width = fracture.shape[1]
    tables = [fracture[:, i : i + LANES] for i in range(0, width, LANES)]
    sums = []
    for start in range(0, width, LANES):
        total = jnp.zeros(tables[0].shape, F32)
        for j in range(links_ref.shape[0]):
            link = links_ref[j, :, start : start + LANES]
            found = jnp.zeros(tables[0].shape, F32)
            for i, table in enumerate(tables):
                found = jnp.where(
                    link >> log2(LANES) == i, lane_gather(table, link & (LANES - 1)), found
                )
            total = total + link_weights_ref[j, :, start : start + LANES] * found
        sums.append(total)
    return jnp.concatenate(sums, axis=1)


def relaxed_side(now, edge, scaled, inverse, relaxation):
    depth, cols = edge.shape
    place = iota(edge.shape, 1)
    zero_plane = jnp.zeros((1, cols), F32)
    after = []
    for far in range(HALO):
        here = now[far]
        beside = jnp.concatenate([here[1:], zero_plane], axis=0)
        beside = beside + jnp.concatenate([zero_plane, here[:-1]], axis=0)
        beside = beside + jnp.where(place == 0, 0.0, pltpu.roll(here, 1, 1))
        beside = beside + jnp.where(place == cols - 1, 0.0, pltpu.roll(here, cols - 1, 1))
        beside = beside + (edge if far == 0 else now[far - 1])
        if far + 1 < HALO:
            beside = beside + now[far + 1]
        after.append(
            (1.0 - relaxation) * here + relaxation * (scaled[far] + inverse[far] * beside)
        )
    return after


def spread_side(place, low, values, depth, col_groups):
    rows = iota((col_groups * HALO * depth, place.shape[1]), 0)
    hot = (rows == place).astype(F32).astype(BF16)
    added = fold(matmul(hot, masked_parts(low, values), (1, 1)), 0)
    return [
        jnp.concatenate(
            [
                added[(group * HALO + far) * depth : (group * HALO + far + 1) * depth]
                for group in range(col_groups)
            ],
            axis=1,
        )
        for far in range(HALO)
    ]


def pick_cells(table_ref, columns_ref, hot_ref, low):
    depth, area_rows, cols = table_ref.shape
    for c in range(cols // LANES):
        chunk = table_ref[:, :, c * LANES : (c + 1) * LANES]
        put_columns(chunk.reshape(depth * area_rows, LANES), c, columns_ref)
    return pick_low(matmul(columns_ref[...], hot_ref[...], (1, 0)), low)


def side_kernel_inputs(info_ref, side):
    rows = [info_ref[side, i : i + 1, :] for i in range(5)]
    whole = [x.astype(jnp.int32) for x in rows]
    return whole[0], whole[1], rows[2], whole[3], whole[4]


def row_integer(rows_ref, index):
    return rows_ref[index].astype(jnp.int32)


def row_cells(rows_ref):
    return [unstack_lanes(row_integer(rows_ref, index), 1) for index in (4, 5)]


def first_window_kernel(
    relaxation,
    grids_hbm,
    rows_ref,
    partial_ref,
    scaled_ref,
    inverse_ref,
    edges_ref,
    row_partial_ref,
    row_inverse_ref,
    chains_ref,
    matrix_ref,
    source_ref,
    storage_ref,
    hot_ref,
    columns_ref,
    sems,
):
    copies = [
        pltpu.make_async_copy(row_slice(grids_hbm, rows_ref), rows_ref, sems.at[3]),
        pltpu.make_async_copy(grids_hbm.at[2], storage_ref, sems.at[2]),
        pltpu.make_async_copy(grids_hbm.at[1], source_ref, sems.at[1]),
        pltpu.make_async_copy(grids_hbm.at[0], matrix_ref, sems.at[0]),
    ]
    for copy in copies:
        copy.start()
    copies[0].wait()
    depth, area_rows, cols = matrix_ref.shape
    plane_rows = depth * area_rows
    high, low = row_cells(rows_ref)
    weight = rows_ref[0]
    fill_hot(hot_ref, high)
    added = fold(matmul(hot_ref[...], masked_parts(low, unstack_lanes(weight, 1)), (1, 1)), 0)
    for copy in copies[1:]:
        copy.wait()
    for c in range(cols // LANES):
        lanes = slice(c * LANES, (c + 1) * LANES)
        extra = added[c * plane_rows : (c + 1) * plane_rows].reshape(depth, area_rows, LANES)
        inverse = 1.0 / (6.0 + storage_ref[:, :, lanes] + extra)
        scaled_ref[:, :, lanes] = source_ref[:, :, lanes] * inverse
        inverse_ref[:, :, lanes] = inverse
    row_inverse_ref[...] = weight * stack_lanes(
        pick_cells(inverse_ref, columns_ref, hot_ref, low)
    )
    partial_ref[...] = relaxed(
        matrix_ref[...], scaled_ref[...], inverse_ref[...], None, None, relaxation
    )
    row_partial_ref[...] = weight * stack_lanes(pick_cells(partial_ref, columns_ref, hot_ref, low))
    edges_ref[0] = matrix_ref[:, 0, :]
    edges_ref[1] = matrix_ref[:, area_rows - 1, :]
    chains = find_chains(rows_ref[3])
    for i, x in enumerate(chains):
        chains_ref[i] = x


def both_sides(pair_ref, cross_ref, tiles):
    odd = (lax.axis_index("area") & 1) == 1
    lower = [jnp.where(odd, pair_ref[i], cross_ref[i]) for i in tiles]
    upper = [jnp.where(odd, cross_ref[i], pair_ref[i]) for i in tiles]
    return lower, upper


def beside_rows(pair_ref, cross_ref, rows_ref, area_rows):
    (lower,), (upper,) = both_sides(pair_ref, cross_ref, (0,))
    depth = lower.shape[0]
    high, low = row_cells(rows_ref)
    row = high & (area_rows - 1)
    plane = (high >> log2(area_rows)) & (depth - 1)
    place = (high >> log2(depth * area_rows)) * depth + plane
    table = jnp.concatenate([stack_lanes(lower), stack_lanes(upper)], axis=0)
    place = jnp.where(row == 0, place, place + table.shape[0] // 2)
    place = jnp.where((row == 0) | (row == area_rows - 1), place, -1)
    hot = (iota((table.shape[0], place.shape[1]), 0) == place).astype(F32).astype(BF16)
    columns = jnp.concatenate(halves(table.T), axis=0)
    return stack_lanes(pick_low(matmul(columns, hot, (1, 0)), low))


def add_rows(relaxation, values, partial_ref, inverse_ref, rows_ref, hot_ref, matrix_ref):
    depth, area_rows, cols = partial_ref.shape
    plane_rows = depth * area_rows
    high, low = row_cells(rows_ref)
    fill_hot(hot_ref, high)
    parts = masked_parts(low, unstack_lanes(values, 1))
    added = fold(matmul(hot_ref[...], parts, (1, 1)), 0)
    for c in range(cols // LANES):
        lanes = slice(c * LANES, (c + 1) * LANES)
        extra = added[c * plane_rows : (c + 1) * plane_rows].reshape(depth, area_rows, LANES)
        matrix_ref[:, :, lanes] = (
            partial_ref[:, :, lanes] + (relaxation * inverse_ref[:, :, lanes]) * extra
        )


def returned_values(returned, rows_ref):
    target, rank = row_integer(rows_ref, 1), row_integer(rows_ref, 2)
    return rows_ref[0] * pick_entries(returned, target, rank)


def first_sides(relaxation, pair_ref, cross_ref, edges_ref, scaled_ref, inverse_ref, info_ref):
    depth, cols = edges_ref.shape[1:]
    partial = []
    for side, tiles in enumerate(both_sides(pair_ref, cross_ref, range(3 * HALO + 1))):
        info_ref[side] = tiles[3 * HALO]
        place, low, weight, _, _ = side_kernel_inputs(info_ref, side)
        added = spread_side(place, low, weight, depth, cols // LANES)
        scaled, inverse = [], []
        for far in range(HALO):
            storage = tiles[2 * HALO + far]
            inverse.append(jnp.where(storage > 0.0, 1.0 / (6.0 + storage + added[far]), 0.0))
            scaled.append(tiles[HALO + far] * inverse[far])
            scaled_ref[side, far] = scaled[far]
            inverse_ref[side, far] = inverse[far]
        partial.append(
            relaxed_side(tiles[:HALO], edges_ref[side], scaled, inverse, relaxation)
        )
    return partial


def window_kernel(
    relaxation,
    before,
    cap,
    first,
    last,
    arrived_ref,
    partial_before_ref,
    scaled_ref,
    inverse_ref,
    rows_ref,
    slots_ref,
    fracture_ref,
    links_ref,
    link_weights_ref,
    *refs,
):
    depth, area_rows, cols = scaled_ref.shape
    devices = arrived_ref.shape[0]
    half = devices * cap // 2
    if first:
        pair_ref, cross_ref, edges_ref, *refs = refs
        partial_ref, side_partial_ref, link_sum_ref, *refs = refs
        side_scaled_ref, side_inverse_ref, side_info_ref, *refs = refs
    else:
        side_before_ref, side_scaled_ref, side_inverse_ref, side_info_ref, *refs = refs
        partial_ref, side_partial_ref, link_sum_ref, *refs = refs
    if last:
        matrix_ref, hot_ref = refs
    else:
        row_partial_ref, matrix_ref, hot_ref, columns_ref = refs
    returned = device_values(arrived_ref, row_integer(slots_ref, 2)) if first else arrived_ref[:, 1, :]
    values = returned_values(returned, rows_ref)
    add_rows(before, values, partial_before_ref, inverse_ref, rows_ref, hot_ref, matrix_ref)
    if first:
        lower, upper = both_sides(pair_ref, cross_ref, (0,))
        for edge, tile in ((0, lower[0]), (area_rows - 1, upper[0])):
            matrix_ref[:, edge, :] = (
                matrix_ref[:, edge, :] + (before * inverse_ref[:, edge, :]) * tile
            )
        side_before = first_sides(
            before, pair_ref, cross_ref, edges_ref, side_scaled_ref, side_inverse_ref, side_info_ref
        )
    else:
        side_before = [[side_before_ref[side, far] for far in range(HALO)] for side in range(2)]
    edges = []
    for side, edge in enumerate((0, area_rows - 1)):
        place, low, weight, target, rank = side_kernel_inputs(side_info_ref, side)
        if first:
            code = jnp.concatenate(
                [side_info_ref[side, i : i + 1, :half] for i in (5, 6)], axis=1
            )
            code = from_dense(code, devices, cap).astype(jnp.int32)
            returned = device_values(arrived_ref, code)
        else:
            returned = arrived_ref[:, 2 + side, :]
        values = pick_entries(returned, stack_lanes(target), stack_lanes(rank))
        values = weight * unstack_lanes(values, 1)
        added = spread_side(place, low, values, depth, cols // LANES)
        now = [
            side_before[side][far] + before * side_inverse_ref[side, far] * added[far]
            for far in range(HALO)
        ]
        edges.append(now[0])
        after = relaxed_side(
            now,
            matrix_ref[:, edge, :],
            [side_scaled_ref[side, far] for far in range(HALO)],
            [side_inverse_ref[side, far] for far in range(HALO)],
            relaxation,
        )
        for far in range(HALO):
            side_partial_ref[side, far] = after[far]
    partial_ref[...] = relaxed(
        matrix_ref[...],
        scaled_ref[...],
        inverse_ref[...],
        edges[0],
        edges[1],
        relaxation,
    )
    if not last:
        row_partial_ref[...] = rows_ref[0] * stack_lanes(
            pick_cells(partial_ref, columns_ref, hot_ref, row_cells(rows_ref)[1])
        )
    link_sum_ref[...] = linked(fracture_ref[...], links_ref, link_weights_ref)


def row_values(
    relaxation,
    returned,
    slots_ref,
    rows_ref,
    row_partial_ref,
    row_inverse_ref,
    chains_ref,
    beside=None,
):
    total = same_cell_sum(returned_values(returned, rows_ref), chains_ref)
    if beside is not None:
        total = total + beside
    outgoing = row_partial_ref[...] + (relaxation * row_inverse_ref[...]) * total
    return pick_entries(outgoing, row_integer(slots_ref, 0), row_integer(slots_ref, 1))


def node_sums(code, shape, *values):
    owned, blk = shape
    rows = owned * blk // LANES
    member = iota((rows, code.shape[1]), 0) == code >> log2(LANES)
    low = (iota((LANES, code.shape[1]), 0) == code & (LANES - 1)).astype(F32).astype(BF16)
    parts = []
    for value in values:
        high = value.astype(BF16).astype(F32)
        parts += [jnp.where(member, high, 0.0), jnp.where(member, value - high, 0.0)]
    sums = matmul(jnp.concatenate(parts, axis=0).astype(BF16), low, (1, 1))
    sums = [sums[i : i + rows] for i in range(0, sums.shape[0], rows)]
    return [
        unstack_lanes(sums[2 * i] + sums[2 * i + 1], owned) for i in range(len(values))
    ]


def node_values(table, code):
    found = jnp.zeros(code.shape, F32)
    low = code & (LANES - 1)
    for row in range(table.shape[0]):
        values = jnp.broadcast_to(table[row : row + 1], code.shape)
        found = jnp.where(code >> log2(LANES) == row, lane_gather(values, low), found)
    return found


def device_values(arrived_ref, code):
    found = jnp.zeros(code.shape, F32)
    low = code & (LANES - 1)
    for row in range(4 * (arrived_ref.shape[1] - 1)):
        values = lane_gather(arrived_ref[:, 1 + row // 4, row % 4, :], low)
        found = jnp.where(code >> log2(LANES) == row, values, found)
    return found


def put_requested(message_ref, values):
    zero = jnp.zeros((1, LANES), F32)
    order = group_order(values.shape[0])
    rows = {device: values[i : i + 1] for i, device in enumerate(order)}
    message_ref[:, 1, :] = values
    for place, step in ((2, -1), (3, 1)):
        message_ref[:, place, :] = jnp.concatenate(
            [rows.get(device + step, zero) for device in order], axis=0
        )


def first_step_kernel(
    relaxation,
    cap,
    area_rows,
    arrived_ref,
    pair_ref,
    cross_ref,
    slots_ref,
    rows_ref,
    row_partial_ref,
    row_inverse_ref,
    chains_ref,
    fracture_ref,
    link_sum_ref,
    fracture_source_ref,
    leak_ref,
    link_weights_ref,
    fracture_next_ref,
    fracture_inverse_ref,
    node_code_ref,
    message_hbm,
    message_ref,
    sem,
):
    message_ref[:, 0, :] = row_values(
        relaxation,
        device_values(arrived_ref, row_integer(slots_ref, 2)),
        slots_ref,
        rows_ref,
        row_partial_ref,
        row_inverse_ref,
        chains_ref,
        beside_rows(pair_ref, cross_ref, rows_ref, area_rows),
    )
    code = arrived_ref[:, 0, 0, :].astype(jnp.int32)
    node_code_ref[...] = code
    dense = to_dense(code, cap)
    weight_sum, value_sum = node_sums(
        dense,
        fracture_ref.shape,
        to_dense(arrived_ref[:, 0, 1, :], cap),
        to_dense(arrived_ref[:, 0, 2, :], cap),
    )
    diag = leak_ref[...] + jnp.sum(link_weights_ref[...], axis=0) + weight_sum
    inverse = 1.0 / diag
    fracture_inverse_ref[...] = inverse
    fracture_next = (1.0 - relaxation) * fracture_ref[...] + (relaxation * inverse) * (
        fracture_source_ref[...] + link_sum_ref[...] + value_sum
    )
    fracture_next_ref[...] = fracture_next
    put_requested(message_ref, node_values(stack_lanes(fracture_next), code))
    out = pltpu.make_async_copy(message_ref, message_hbm, sem)
    out.start()
    out.wait()


def next_fracture(
    relaxation,
    cap,
    arrived_ref,
    code,
    fracture_ref,
    link_sum_ref,
    fracture_source_ref,
    fracture_inverse_ref,
):
    (value_sum,) = node_sums(
        to_dense(code, cap), fracture_ref.shape, to_dense(arrived_ref[:, 0, :], cap)
    )
    return (1.0 - relaxation) * fracture_ref[...] + (relaxation * fracture_inverse_ref[...]) * (
        fracture_source_ref[...] + link_sum_ref[...] + value_sum
    )


def step_kernel(
    relaxation,
    cap,
    arrived_ref,
    node_code_ref,
    slots_ref,
    rows_ref,
    row_partial_ref,
    row_inverse_ref,
    chains_ref,
    fracture_ref,
    link_sum_ref,
    fracture_source_ref,
    fracture_inverse_ref,
    fracture_next_ref,
    message_hbm,
    message_ref,
    sem,
):
    message_ref[:, 0, :] = row_values(
        relaxation,
        arrived_ref[:, 1, :],
        slots_ref,
        rows_ref,
        row_partial_ref,
        row_inverse_ref,
        chains_ref,
    )
    code = node_code_ref[...]
    fracture_next = next_fracture(
        relaxation,
        cap,
        arrived_ref,
        code,
        fracture_ref,
        link_sum_ref,
        fracture_source_ref,
        fracture_inverse_ref,
    )
    fracture_next_ref[...] = fracture_next
    put_requested(message_ref, node_values(stack_lanes(fracture_next), code))
    out = pltpu.make_async_copy(message_ref, message_hbm, sem)
    out.start()
    out.wait()


def last_step_kernel(
    relaxation,
    cap,
    arrived_ref,
    node_code_ref,
    partial_ref,
    inverse_ref,
    rows_ref,
    fracture_ref,
    link_sum_ref,
    fracture_source_ref,
    fracture_inverse_ref,
    matrix_ref,
    fracture_next_ref,
    hot_ref,
):
    values = returned_values(arrived_ref[:, 1, :], rows_ref)
    add_rows(relaxation, values, partial_ref, inverse_ref, rows_ref, hot_ref, matrix_ref)
    fracture_next_ref[...] = next_fracture(
        relaxation,
        cap,
        arrived_ref,
        node_code_ref[...],
        fracture_ref,
        link_sum_ref,
        fracture_source_ref,
        fracture_inverse_ref,
    )


def call(kernel, outs, ins, name, micros, hbm_in=(), hbm_out=(), scratch=(), aliases=None, limit=VMEM_LIMIT):
    return pl.pallas_call(
        kernel,
        out_shape=[jax.ShapeDtypeStruct(shape, dtype) for shape, dtype in outs],
        in_specs=[
            pl.BlockSpec(memory_space=pltpu.HBM if i in hbm_in else pltpu.VMEM)
            for i in range(len(ins))
        ],
        out_specs=[
            pl.BlockSpec(memory_space=pltpu.HBM if i in hbm_out else pltpu.VMEM)
            for i in range(len(outs))
        ],
        scratch_shapes=list(scratch),
        input_output_aliases=aliases or {},
        compiler_params=pltpu.CompilerParams(vmem_limit_bytes=limit),
        cost_estimate=pl.CostEstimate(
            flops=0, bytes_accessed=int(micros * 3.0e6), transcendentals=0
        ),
        name=name,
    )(*ins)


def local(
    block_owner,
    transfer_cells,
    transfer_nodes,
    transfer_weights,
    row_counts,
    matrix_start,
    matrix_source,
    matrix_storage,
    fracture_start,
    fracture_source,
    fracture_leak,
    fracture_links,
    link_weights,
):
    devices = lax.axis_size("area")
    depth, area_rows, cols = matrix_start.shape
    owned, blk = fracture_start.shape
    total_rows = transfer_cells.shape[0]
    cap = 3 * total_rows // (2 * devices)
    cells = depth * area_rows * cols // LANES
    relax = relax_weights(ITERS)
    grid = (matrix_start.shape, F32)
    grids = ((GRID_SLOTS,) + matrix_start.shape, F32)
    fracture = (fracture_start.shape, F32)
    side = ((3 * HALO + 1, depth, cols), F32)
    sides = ((2, HALO, depth, cols), F32)
    hot = pltpu.VMEM((cells, total_rows), BF16)
    columns = pltpu.VMEM((2 * LANES, cells), BF16)
    padded = (devices, LANES)
    first_message = ((devices, 1 + owned * blk // LANES // 4, 4, LANES), F32)
    message_type = ((devices, 4, LANES), F32)
    pairs, crossings = [
        [(i + a, i + b) for i in range(start, devices - 1, 2) for a, b in ((0, 1), (1, 0))]
        for start in (0, 1)
    ]

    def exchange(message):
        return lax.all_to_all(
            message,
            "area",
            split_axis=0,
            concat_axis=0,
            tiled=True,
            axis_index_groups=[group_order(devices)],
        )

    staged = [
        row_counts.reshape(1, 1),
        block_owner.reshape(-1, LANES),
        transfer_cells.reshape(-1, LANES),
        transfer_nodes.reshape(-1, LANES),
        transfer_weights.reshape(-1, LANES),
        matrix_start,
        fracture_start,
        matrix_source,
        matrix_storage,
        fracture_links,
        link_weights,
    ]
    row_shape = (total_rows // LANES, LANES)
    rows = (row_shape, F32)
    info = ((6,) + row_shape, F32)
    edges = ((2, depth, cols), F32)
    slot_info, message, pair, cross, grids_start, link_sum = call(
        functools.partial(setup_kernel, devices, cap, len(staged)),
        [((3,) + padded, F32), first_message, side, side, grids, fracture],
        staged,
        "place_rows",
        5.0,
        hbm_in=range(len(staged)),
        hbm_out=(1, 2, 3, 4),
        scratch=[pltpu.VMEM(x.shape, x.dtype) for x in staged]
        + [
            pltpu.VMEM(*info),
            pltpu.VMEM(*first_message),
            pltpu.VMEM(*side),
            pltpu.VMEM(*side),
            hot,
            columns,
            pltpu.SemaphoreType.DMA((len(staged) + 7,)),
        ],
        limit=63 * 1024 * 1024,
    )
    arrived = exchange(message)
    pair = lax.ppermute(pair, "area", pairs)
    cross = lax.ppermute(cross, "area", crossings)
    row_info, partial, scaled, inverse, edge_rows, row_partial, row_inverse, chains = call(
        functools.partial(first_window_kernel, relax[0]),
        [info, grid, grid, grid, edges, rows, rows, ((3,) + row_shape, F32)],
        [grids_start],
        "stencil_first",
        4.0,
        hbm_in=(0,),
        scratch=[pltpu.VMEM(*grid)] * 3 + [hot, columns, pltpu.SemaphoreType.DMA((4,))],
    )
    fracture_now = fracture_start
    message_scratch = [pltpu.VMEM(*message_type), pltpu.SemaphoreType.DMA]
    fracture_now, fracture_inverse, node_code, message = call(
        functools.partial(first_step_kernel, relax[0], cap, area_rows),
        [fracture, fracture, (padded, jnp.int32), message_type],
        [
            arrived,
            pair,
            cross,
            slot_info,
            row_info,
            row_partial,
            row_inverse,
            chains,
            fracture_now,
            link_sum,
            fracture_source,
            fracture_leak,
            link_weights,
        ],
        "couple_first",
        2.0,
        hbm_out=(3,),
        scratch=message_scratch,
    )
    for index in range(1, ITERS):
        last = index == ITERS - 1
        old, arrived = arrived, exchange(message)
        first = index == 1
        inputs = [old, partial, scaled, inverse, row_info, slot_info, fracture_now]
        inputs += [fracture_links, link_weights]
        if first:
            inputs += [pair, cross, edge_rows]
        else:
            inputs += [side_partial, side_scaled, side_inverse, side_info]
        outs = call(
            functools.partial(window_kernel, relax[index], relax[index - 1], cap, first, last),
            [grid, sides, fracture]
            + ([sides, sides, edges] if first else [])
            + ([] if last else [rows]),
            inputs,
            "stencil",
            3.0,
            aliases={1: 0} if first else {1: 0, 9: 1},
            scratch=[pltpu.VMEM(*grid), hot] + ([] if last else [columns]),
        )
        partial, side_partial, link_sum = outs[:3]
        if first:
            side_scaled, side_inverse, side_info = outs[3:6]
        fractures = [fracture_now, link_sum, fracture_source, fracture_inverse]
        if last:
            return call(
                functools.partial(last_step_kernel, relax[index], cap),
                [grid, fracture],
                [arrived, node_code, partial, inverse, row_info] + fractures,
                "couple_last",
                2.0,
                scratch=[hot],
            )
        row_partial = outs[-1]
        fracture_now, message = call(
            functools.partial(step_kernel, relax[index], cap),
            [fracture, message_type],
            [arrived, node_code, slot_info, row_info, row_partial, row_inverse, chains]
            + fractures,
            "couple",
            2.0,
            hbm_out=(1,),
            scratch=message_scratch,
        )


def solution(mesh):
    in_specs = (
        P(),
        P("area"),
        P("area"),
        P("area"),
        P("area"),
        P("real", "area", None),
        P("real", "area", None),
        P("real", "area", None),
        P("area", "real"),
        P("area", "real"),
        P("area", "real"),
        P(None, "area", None),
        P("real", "area", None),
    )
    out_specs = (P("real", "area", None), P("area", "real"))
    return jax.shard_map(local, mesh=mesh, in_specs=in_specs, out_specs=out_specs, check_vma=False)
```
